512 devices in a mesh: rep: 8 (over y), day: 64 (over x, z, core).
Axes of the slice: x: 4, y: 8, z: 8, core: 2. Of those that a mesh axis runs over, the one named last changes fastest.
Arguments:
- events: bfloat16 [524288, 512], P(('rep', 'day')), may hold values from -6 to 6
- event_user: int32 [524288], P(('rep', 'day')), may hold values from 0 to 63, as said below
- event_day: int32 [524288], P(('rep', 'day')), may hold values from 0 to 3
- score_weight: bfloat16 [512, 8], replicated, may hold values from -0.25 to 0.25
- value_weight: bfloat16 [512, 512], replicated, may hold values from -0.25 to 0.25
- qkv_weight: bfloat16 [512, 1536], replicated, may hold values from -0.25 to 0.25
- cotangent: bfloat16 [512, 256, 512], P(('rep', 'day')), may hold values from -6 to 6
Outputs:
- grad_qkv_weight: float32 [512, 1536], P('day')
- grad_score_weight: float32 [512, 8], P('day')
The draws below stay inside these ranges and needn't reach their ends.
Inputs may be any that keep to these rules, and one draw needn't show every extreme that they name: `event_user`: in every block of 1024 events each of the 64 users has at least one event on each of the 4 days.
All inputs are finite; a program needn't handle non-finite values.
Results may differ from the reference program's by a relative error of at most 0.015.
Values may be sent and summed in bfloat16 or wider, within the bound.
No kernel may reach another device: no remote copies, remote signals or barrier semaphores. Data moves between devices by JAX's collectives and lax.ppermute only.
A program may use at most 128 MiB of HBM per device.

```python
import math
import jax
import jax.numpy as jnp
from jax import lax

D = 512
H = 8
DH = 64
DAY_DEV = 4
USER_DEV = 1
EV_DEV = 1024
BUCKETS = 64
GROUPS = 8
USER_GRP = 64
USERS = 512
DAYS = 256
UD_DEV = 256
EV_ALL = 524288


def shared_segments(key):
    block_count = EV_ALL // EV_DEV
    slot_count = USER_GRP * DAY_DEV
    extra_count = EV_DEV - slot_count
    split_keys = jax.random.split(key, 4)
    first_pick = jax.random.randint(split_keys[0], (block_count, extra_count), 0, slot_count)
    skewed_pick = jax.random.randint(split_keys[1], (block_count, extra_count), 0, first_pick + 1)
    relabel = jax.vmap(lambda sub_key: jax.random.permutation(sub_key, slot_count))(jax.random.split(split_keys[2], block_count))
    picked = jnp.take_along_axis(relabel, skewed_pick, axis=1).astype(jnp.int32)
    base_slots = jnp.broadcast_to(jnp.arange(slot_count, dtype=jnp.int32), (block_count, slot_count))
    joined = jnp.concatenate([base_slots, picked], axis=1)
    shuffle = jax.vmap(lambda sub_key: jax.random.permutation(sub_key, EV_DEV))(jax.random.split(split_keys[3], block_count))
    return jnp.take_along_axis(joined, shuffle, axis=1).reshape(EV_ALL).astype(jnp.int32)


def draw_event_user(key, part):
    segments = shared_segments(key)
    return (segments // DAY_DEV).astype(jnp.int32)


def draw_event_day(key, part):
    segments = shared_segments(key)
    return (segments % DAY_DEV).astype(jnp.int32)


def block_scale(key, dims, cuts, least, top_value):
    gain = 1.0
    for dim, blocks in cuts:
        steps = jax.random.uniform(jax.random.fold_in(jax.random.fold_in(key, 6), dim), (blocks,), jnp.float32, least / len(cuts), top_value / len(cuts))
        gain = gain * jnp.repeat(jnp.exp(steps), dims[dim] // blocks).reshape((-1,) + (1,) * (len(dims) - 1 - dim))
    return gain


def scatter_about(rng, extent, deviation, bound, pieces=(), held_as=jnp.bfloat16):
    level = block_scale(rng, extent, pieces, -0.22, 0.18) if pieces else 1.0
    result = jax.random.normal(rng, extent, jnp.float32) * deviation * level
    return jnp.minimum(jnp.maximum(result, -bound), bound).astype(held_as)


def setup_inputs(seed: int = 0) -> dict:
    splits = jax.random.split(jax.random.key(seed), 8)
    events = scatter_about(splits[0], (EV_ALL, D), 1.0, 6.0, ((0, 512),))
    event_user = draw_event_user(jax.random.fold_in(splits[7], 71), 0)
    event_day = draw_event_day(jax.random.fold_in(splits[7], 71), 0)
    score_weight = scatter_about(splits[3], (D, H), D ** -0.5, 0.25)
    value_weight = scatter_about(splits[4], (D, D), D ** -0.5, 0.25)
    qkv_weight = scatter_about(splits[5], (D, 3 * D), D ** -0.5, 0.25)
    cotangent = scatter_about(splits[6], (USERS, DAYS, D), 1.0, 6.0, ((0, 512),))
    return {"events": events, "event_user": event_user, "event_day": event_day, "score_weight": score_weight, "value_weight": value_weight, "qkv_weight": qkv_weight, "cotangent": cotangent}


def attention_pass(summary_rows, cotangent_rows, qkv_weight, loss_scale):
    user_batch = summary_rows.shape[0]
    wide_summary = summary_rows.astype(jnp.float32)
    inverse_rms = lax.rsqrt(lax.optimization_barrier(jnp.mean(wide_summary * wide_summary, axis=-1, keepdims=True)) + 1e-06)
    normed = (wide_summary * inverse_rms).astype(jnp.bfloat16)
    flat_normed = normed.reshape(user_batch * DAYS, D)
    projected = jnp.dot(flat_normed, qkv_weight, preferred_element_type=jnp.float32).astype(jnp.bfloat16)
    projected = projected.reshape(user_batch, DAYS, 3, H, DH)
    queries = projected[:, :, 0].astype(jnp.float32)
    key_rows = projected[:, :, 1].astype(jnp.float32)
    value_rows = projected[:, :, 2].astype(jnp.float32)
    cotangent_heads = cotangent_rows.astype(jnp.float32).reshape(user_batch, DAYS, H, DH)
    root_size = math.sqrt(DH)
    logits = jnp.einsum('bqhd,bkhd->bhqk', queries, key_rows) / root_size
    causal = jnp.arange(DAYS)[:, None] >= jnp.arange(DAYS)[None, :]
    exponent = jnp.where(causal, jnp.exp(logits), jnp.float32(0.0))
    attention = exponent / lax.optimization_barrier(jnp.sum(exponent, axis=-1, keepdims=True))
    rounded = lax.optimization_barrier(attention.astype(jnp.bfloat16)).astype(jnp.float32)
    grad_probs = jnp.einsum('bqhd,bkhd->bhqk', cotangent_heads, value_rows) * loss_scale
    grad_logits = attention * (grad_probs - lax.optimization_barrier(jnp.sum(grad_probs * attention, axis=-1, keepdims=True))) / root_size
    grad_logits = lax.optimization_barrier(grad_logits.astype(jnp.bfloat16)).astype(jnp.float32)
    grad_query = jnp.einsum('bhqk,bkhd->bqhd', grad_logits, key_rows)
    grad_key = jnp.einsum('bhqk,bqhd->bkhd', grad_logits, queries)
    grad_value = jnp.einsum('bhqk,bqhd->bkhd', rounded, cotangent_heads) * loss_scale
    grad_qkv = jnp.stack([grad_query, grad_key, grad_value], axis=2).astype(jnp.bfloat16)
    grad_qkv = grad_qkv.reshape(user_batch * DAYS, 3 * D)
    grad_weight = jnp.dot(flat_normed.T, grad_qkv, preferred_element_type=jnp.float32)
    grad_normed = jnp.dot(grad_qkv, qkv_weight.T, preferred_element_type=jnp.float32).reshape(user_batch, DAYS, D)
    cubed = inverse_rms * inverse_rms * inverse_rms
    grad_summary = cotangent_rows.astype(jnp.float32) * loss_scale + inverse_rms * grad_normed - wide_summary * cubed * lax.optimization_barrier(jnp.mean(grad_normed * wide_summary, axis=-1, keepdims=True))
    return (grad_weight, grad_summary.astype(jnp.bfloat16))

def pool_block(block_events, block_user, block_day, score_weight):
    segment = block_user * DAY_DEV + block_day
    logits = jnp.dot(block_events, score_weight, preferred_element_type=jnp.float32)
    exponent = jnp.exp(logits)
    denominator = jax.ops.segment_sum(exponent, segment, num_segments=UD_DEV)
    return (segment, exponent / denominator[segment])

def reference(events, event_user, event_day, score_weight, value_weight, qkv_weight, cotangent):
    block_count = GROUPS * BUCKETS
    event_blocks = events.reshape(block_count, EV_DEV, D)
    user_blocks = event_user.reshape(block_count, EV_DEV)
    day_blocks = event_day.reshape(block_count, EV_DEV)
    value_heads = value_weight.astype(jnp.float32).reshape(D, H, DH)

    def forward_block(inputs):
        block_events, block_user, block_day = inputs
        segment, weight = pool_block(block_events, block_user, block_day, score_weight)
        wide_events = block_events.astype(jnp.float32)
        pooled = jnp.stack([jax.ops.segment_sum(weight[:, head_index, None] * wide_events, segment, num_segments=UD_DEV) for head_index in range(H)], axis=1)
        exact = jnp.einsum('uhd,dhk->uhk', pooled, value_heads, precision=lax.Precision.HIGHEST)
        return exact.reshape(UD_DEV, D)
    exact_blocks = lax.map(forward_block, (event_blocks, user_blocks, day_blocks))
    summaries = exact_blocks.astype(jnp.bfloat16).reshape(GROUPS, BUCKETS, USER_GRP, DAY_DEV, D)
    summaries = summaries.transpose(0, 2, 1, 3, 4).reshape(block_count, USER_DEV, DAYS, D)
    cotangent_blocks = cotangent.reshape(block_count, USER_DEV, DAYS, D)
    loss_scale = 1.0 / math.sqrt(USERS * DAYS)

    def user_step(carry, inputs):
        grad_weight, grad_summary = attention_pass(inputs[0], inputs[1], qkv_weight, loss_scale)
        return (carry + grad_weight, grad_summary)
    grad_qkv_weight, grad_summaries = lax.scan(user_step, jnp.zeros((D, 3 * D), jnp.float32), (summaries, cotangent_blocks))
    grad_days = grad_summaries.reshape(GROUPS, USER_GRP, BUCKETS, DAY_DEV, D)
    grad_days = grad_days.transpose(0, 2, 1, 3, 4).reshape(block_count, UD_DEV, D)

    def backward_block(carry, inputs):
        block_events, block_user, block_day, exact, grad_rows = inputs
        segment, weight = pool_block(block_events, block_user, block_day, score_weight)
        grad_wide = grad_rows.astype(jnp.float32)
        spread = jnp.einsum('uhk,dhk->uhd', grad_wide.reshape(UD_DEV, H, DH), value_heads, precision=lax.Precision.HIGHEST)
        grad_pool = lax.optimization_barrier(jnp.sum(block_events.astype(jnp.float32)[:, None, :] * spread[segment], axis=-1))
        inner_terms = lax.optimization_barrier(jnp.sum((grad_wide * exact).reshape(UD_DEV, H, DH), axis=-1))
        grad_scores = (weight * (grad_pool - inner_terms[segment])).astype(jnp.bfloat16)
        return (carry + jnp.dot(block_events.T, grad_scores, preferred_element_type=jnp.float32), None)
    grad_score_weight, unused = lax.scan(backward_block, jnp.zeros((D, H), jnp.float32), (event_blocks, user_blocks, day_blocks, exact_blocks, grad_days))
    return (grad_qkv_weight, grad_score_weight)
```

```python
import functools
import math

import jax
import jax.numpy as jnp
from jax import lax
from jax.experimental import pallas as pl
from jax.experimental.pallas import tpu as pltpu
from jax.sharding import Mesh, PartitionSpec as P

DAY = ("x", "z", "core")
F32 = jnp.float32
BF16 = jnp.bfloat16
BF16_MAX = 3.3895313892515355e38


def iota(shape, dim):
    return lax.broadcasted_iota(jnp.int32, shape, dim)


def one_hot(condition):
    return jnp.where(condition, 1.0, 0.0).astype(BF16)


def dot(a, b, dims):
    return lax.dot_general(a, b, ((dims[0], dims[1]), ((), ())), preferred_element_type=F32)


def nn(a, b):
    return dot(a, b, ((1,), (0,)))


def nt(a, b):
    return dot(a, b, ((1,), (1,)))


def tn(a, b):
    return dot(a, b, ((0,), (0,)))


def split3(x):
    high = jnp.minimum(x, BF16_MAX).astype(BF16)
    rest = x - high.astype(F32)
    middle = rest.astype(BF16)
    low = (rest - middle.astype(F32)).astype(BF16)
    return jnp.concatenate([high.astype(F32), middle.astype(F32), low.astype(F32)], 0).astype(BF16)


def join3(x):
    n = x.shape[0] // 3
    return x[:n] + x[n : 2 * n] + x[2 * n :]


def slot_rows(user_ref, day_ref, users, slots):
    segment = day_ref[...] * users + user_ref[...]
    return one_hot(iota((slots, segment.shape[1]), 0) == segment)


def rows_of(x, width):
    return jnp.concatenate([x[:, i : i + width] for i in range(0, x.shape[1], width)], axis=0)


def lanes_of(x, rows):
    return jnp.concatenate([x[i : i + rows] for i in range(0, x.shape[0], rows)], axis=1)


def pool_kernel(users, slots, user_ref, day_ref, events_ref, score_ref, value_ref, summary_ref, weight_ref):
    width, heads = score_ref.shape
    events = events_ref[...]
    rows = slot_rows(user_ref, day_ref, users, slots)
    eye = one_hot(iota((heads, heads), 0) == iota((heads, heads), 1))
    score_t = nt(eye, score_ref[...]).astype(BF16)
    exponent = jnp.exp(nt(score_t, events))
    denominator = join3(nt(split3(exponent), rows))
    weight = exponent / join3(nn(split3(denominator), rows))
    weight_ref[...] = weight
    expand = one_hot(iota((3 * heads, width), 1) // (width // heads) == iota((3 * heads, width), 0) % heads)
    values = nn(events, value_ref[...])
    weighted = (values * tn(split3(weight), expand)).astype(BF16)
    pooled = nn(rows, weighted)
    summary_ref[...] = lanes_of(pooled.astype(BF16), users)


def centre_kernel(users, slots, user_ref, day_ref, events_ref, value_ref, summary_ref, out_ref):
    rows = slot_rows(user_ref, day_ref, users, slots)
    pooled = rows_of(summary_ref[...], value_ref.shape[0])
    values = nn(events_ref[...], value_ref[...])
    out_ref[...] = (values - tn(rows, pooled)).astype(BF16)


def attention_kernel(heads, loss_scale, x_ref, cot_ref, qkv_weight_ref, grad_ref, normed_ref, grad_qkv_ref):
    width = qkv_weight_ref.shape[0]
    days = cot_ref.shape[0]
    buckets = x_ref.shape[0]
    day_dev = days // buckets
    size = width // heads
    row_day = (iota((days, days), 0) % buckets) * day_dev + iota((days, days), 0) // buckets
    column_day = (iota((days, days), 1) % buckets) * day_dev + iota((days, days), 1) // buckets
    causal = column_day <= row_day
    cot = nn(one_hot(iota((days, days), 1) == row_day), cot_ref[...]).astype(BF16)
    wide = rows_of(x_ref[...], width).astype(F32)
    inverse = lax.rsqrt(jnp.mean(wide * wide, axis=-1, keepdims=True) + 1e-06)
    normed = (wide * inverse).astype(BF16)
    normed_ref[...] = normed
    qkv = nn(normed, qkv_weight_ref[...]).astype(BF16)
    pair = 2 * size
    left = iota((days, pair), 1) < size
    zero = jnp.zeros((days, pair), BF16)
    root = 1.0 / math.sqrt(size)
    parts = ([], [], [])
    for start in range(0, width, pair):
        q, k, v = (qkv[:, i * width + start : i * width + start + pair] for i in range(3))
        c = cot[:, start : start + pair]
        held = ([], [], [], [], [])
        for half in range(2):
            mine = left if half == 0 else ~left
            q1, k1, v1, c1 = (jnp.where(mine, a, zero) for a in (q, k, v, c))
            exponent = jnp.where(causal, jnp.exp(nt(q, k1) * root), 0.0)
            total = jnp.sum(exponent, axis=-1, keepdims=True)
            guard = jnp.where(total > 1.0, 2.0**-64, 1.0)
            attention = (exponent * guard) * (1.0 / (total * guard))
            grad_probs = nt(c, v1) * loss_scale
            inner = jnp.sum(grad_probs * attention, axis=-1, keepdims=True)
            grad_logits = (attention * (grad_probs - inner) * root).astype(BF16)
            for group, item in zip(held, (grad_logits, attention.astype(BF16), q1, k1, c1)):
                group.append(item)
        logits_grad, probs, q2, k2, c2 = held
        parts[0].append(nn(jnp.concatenate(logits_grad, 1), jnp.concatenate(k2, 0)))
        parts[1].append(tn(jnp.concatenate(logits_grad, 0), jnp.concatenate(q2, 0)))
        parts[2].append(tn(jnp.concatenate(probs, 0), jnp.concatenate(c2, 0)) * loss_scale)
    grad_qkv = jnp.concatenate([a.astype(BF16) for part in parts for a in part], axis=1)
    grad_qkv_ref[...] = grad_qkv
    grad_normed = nt(grad_qkv, qkv_weight_ref[...])
    cubed = inverse * inverse * inverse
    grad = (
        cot.astype(F32) * loss_scale
        + inverse * grad_normed
        - wide * cubed * jnp.mean(grad_normed * wide, axis=-1, keepdims=True)
    )
    grad_ref[...] = lanes_of(grad.astype(BF16), buckets)


def outer_kernel(rows, core_ref, normed_ref, grad_qkv_ref, mine_ref, other_ref):
    width, columns = normed_ref.shape[1], grad_qkv_ref.shape[1]
    product = tn(normed_ref[...], grad_qkv_ref[...]).reshape(width // (2 * rows), 2, rows, columns)
    even = product[:, 0].reshape(width // 2, columns).astype(BF16)
    odd = product[:, 1].reshape(width // 2, columns).astype(BF16)
    first = core_ref[0] == 0

    @pl.when(first)
    def _():
        mine_ref[...] = even
        other_ref[...] = odd

    @pl.when(jnp.logical_not(first))
    def _():
        mine_ref[...] = odd
        other_ref[...] = even


def score_kernel(users, slots, user_ref, day_ref, events_ref, centred_ref, weight_ref, grad_ref, out_ref):
    width = events_ref.shape[1]
    heads = weight_ref.shape[0]
    parts, lanes = out_ref.shape
    depth = width // parts
    rows = slot_rows(user_ref, day_ref, users, slots)
    grad = tn(rows, rows_of(grad_ref[...], width))
    terms = (grad * centred_ref[...].astype(F32)).astype(BF16)
    reduce = one_hot(iota((lanes, width), 1) // (width // heads) == iota((lanes, width), 0) % heads)
    weight = jnp.concatenate([weight_ref[...]] * (lanes // heads), axis=0)
    scores = (weight * nt(reduce, terms)).astype(BF16)
    spread = nn(scores, events_ref[...])
    keep = iota((lanes, width), 1) % depth == iota((lanes, width), 0) // heads
    spread = jnp.where(keep, spread, 0.0).astype(BF16)
    pick = one_hot(iota((parts, width), 1) // depth == iota((parts, width), 0))
    out_ref[...] = nt(pick, spread).astype(BF16)


def merge_kernel(weight_ref, score_ref, out_ref):
    copies, depth, columns = out_ref.shape
    lanes = score_ref.shape[1]
    weight = jnp.sum(weight_ref[...].astype(F32), axis=0).astype(BF16)
    score = jnp.sum(score_ref[...].astype(F32), axis=0, keepdims=True)
    keep = iota((depth, lanes), 1) // depth == iota((depth, lanes), 0)
    score = jnp.where(keep, jnp.broadcast_to(score, (depth, lanes)), 0.0).astype(BF16)
    for i in range(copies):
        out_ref[i, :, : columns - lanes] = weight
        out_ref[i, :, columns - lanes :] = score


def final_kernel(x_ref, weight_ref, score_ref):
    columns = weight_ref.shape[1]
    heads = score_ref.shape[1]
    total = jnp.sum(x_ref[...].astype(F32), axis=0)
    weight_ref[...] = total[:, :columns]
    score = total[:, columns:]
    lanes = score.shape[1]
    pick = one_hot(iota((lanes, heads), 0) % heads == iota((lanes, heads), 1))
    score_ref[...] = join3(nn(split3(score), pick))


def call(kernel, outs, args, scalars=0, flops=0):
    vmem = pl.BlockSpec(memory_space=pltpu.VMEM)
    smem = pl.BlockSpec(memory_space=pltpu.SMEM)
    moved = sum(a.size * a.dtype.itemsize for a in args) + sum(math.prod(s) * jnp.dtype(t).itemsize for s, t in outs)
    return pl.pallas_call(
        kernel,
        out_shape=[jax.ShapeDtypeStruct(s, t) for s, t in outs],
        in_specs=[smem] * scalars + [vmem] * (len(args) - scalars),
        out_specs=[vmem] * len(outs),
        compiler_params=pltpu.CompilerParams(vmem_limit_bytes=48 * 2**20),
        cost_estimate=pl.CostEstimate(flops=flops, bytes_accessed=moved, transcendentals=0),
    )(*args)


def shards(sizes, events, event_user, event_day, score_weight, value_weight, qkv_weight, cotangent):
    groups, x_size, z_size, cores = sizes
    buckets = x_size * z_size * cores
    user_dev, days, width = cotangent.shape
    heads = score_weight.shape[1]
    day_dev = days // buckets
    users = user_dev * buckets
    slots = users * day_dev
    count = events.shape[0]
    rows = width // buckets
    loss_scale = 1.0 / math.sqrt(user_dev * buckets * groups * days)
    user_row = event_user.reshape(1, count)
    day_row = event_day.reshape(1, count)

    summary, weight = call(
        functools.partial(pool_kernel, users, slots),
        [((users, day_dev * width), BF16), ((heads, count), F32)],
        (user_row, day_row, events, score_weight, value_weight),
        flops=2 * count * width * (width + slots),
    )
    by_user = lax.all_to_all(summary, DAY, split_axis=0, concat_axis=0, tiled=True)
    (centred,) = call(
        functools.partial(centre_kernel, users, slots),
        [((count, width), BF16)],
        (user_row, day_row, events, value_weight, summary),
        flops=2 * count * width * (width + slots),
    )
    grad_summary, normed, grad_qkv = call(
        functools.partial(attention_kernel, heads, loss_scale),
        [((buckets, day_dev * width), BF16), ((days, width), BF16), ((days, 3 * width), BF16)],
        (by_user, cotangent.reshape(days, width), qkv_weight),
        flops=2 * days * width * (6 * width + 14 * days),
    )
    grad_days = lax.all_to_all(grad_summary, DAY, split_axis=0, concat_axis=0, tiled=True)
    mine, other = call(
        functools.partial(outer_kernel, rows),
        [((width // 2, 3 * width), BF16)] * 2,
        (lax.axis_index("core").reshape(1), normed, grad_qkv),
        scalars=1,
        flops=2 * days * width * 3 * width,
    )
    theirs = lax.ppermute(other, "core", [(i, cores - 1 - i) for i in range(cores)])
    chip = (mine.astype(F32) + theirs.astype(F32)).astype(BF16)
    chip = chip.reshape(x_size * z_size, rows, 3 * width)
    plane = lax.all_to_all(chip, ("x", "z"), split_axis=0, concat_axis=0, tiled=True)
    (score_part,) = call(
        functools.partial(score_kernel, users, slots),
        [((buckets, 128), BF16)],
        (user_row, day_row, events, centred, weight, grad_days),
        flops=2 * count * width * (slots + 256),
    )
    score_rows = lax.all_to_all(score_part, DAY, split_axis=0, concat_axis=0, tiled=True)
    (merged,) = call(
        merge_kernel,
        [((groups, rows, 3 * width + 128), BF16)],
        (plane, score_rows),
    )
    everyone = lax.all_to_all(merged, "rep", split_axis=0, concat_axis=0, tiled=True)
    return tuple(call(final_kernel, [((rows, 3 * width), F32), ((rows, heads), F32)], (everyone,)))


def solution(mesh):
    sizes = (8, 4, 8, 2)
    split = Mesh(mesh.devices.reshape(sizes), ("rep",) + DAY)
    whole = ("rep",) + DAY
    in_specs = (P(whole, None), P(whole), P(whole), P(), P(), P(), P(whole, None, None))
    out_specs = (P(DAY, None), P(DAY, None))
    return jax.shard_map(
        functools.partial(shards, sizes), mesh=split, in_specs=in_specs, out_specs=out_specs, check_vma=False
    )
```

```python
import functools
import math

import jax
import jax.numpy as jnp
from jax import lax
from jax.experimental import pallas as pl
from jax.experimental.pallas import tpu as pltpu
from jax.sharding import Mesh, PartitionSpec as P

DAY = ("x", "z", "core")
F32 = jnp.float32
BF16 = jnp.bfloat16
BF16_MAX = 3.3895313892515355e38


def iota(shape, dim):
    return lax.broadcasted_iota(jnp.int32, shape, dim)


def one_hot(condition):
    return jnp.where(condition, 1.0, 0.0).astype(BF16)


def dot(a, b, dims):
    return lax.dot_general(a, b, ((dims[0], dims[1]), ((), ())), preferred_element_type=F32)


def nn(a, b):
    return dot(a, b, ((1,), (0,)))


def nt(a, b):
    return dot(a, b, ((1,), (1,)))


def tn(a, b):
    return dot(a, b, ((0,), (0,)))


def split3(x):
    high = jnp.minimum(x, BF16_MAX).astype(BF16)
    rest = x - high.astype(F32)
    middle = rest.astype(BF16)
    low = (rest - middle.astype(F32)).astype(BF16)
    return jnp.concatenate([high.astype(F32), middle.astype(F32), low.astype(F32)], 0).astype(BF16)


def join3(x):
    n = x.shape[0] // 3
    return x[:n] + x[n : 2 * n] + x[2 * n :]


def slot_rows(user_ref, day_ref, users, slots):
    segment = user_ref[...] * (slots // users) + day_ref[...]
    return one_hot(iota((slots, segment.shape[1]), 0) == segment)


def to_rows(x, width):
    return x.astype(F32).reshape(x.size // width, width).astype(BF16)


def to_blocks(x, blocks):
    return x.reshape(blocks, x.size // (blocks * 128), 128).astype(BF16)


def pool_kernel(
    users, slots, user_ref, day_ref, score_ref, events_ref, value_ref, summary_ref, weight_ref, events_buf, value_buf, sems
):
    width, heads = score_ref.shape
    count = events_ref.shape[0]
    copies = []
    for source, target, parts in ((events_ref, events_buf, 8), (value_ref, value_buf, 4)):
        step = source.shape[0] // parts
        for i in range(parts):
            piece = pl.ds(i * step, step)
            copies.append(pltpu.make_async_copy(source.at[piece, :], target.at[piece, :], sems.at[len(copies)]))
    for copy in copies:
        copy.start()
    rows = slot_rows(user_ref, day_ref, users, slots)
    eye = one_hot(iota((heads, heads), 0) == iota((heads, heads), 1))
    score_t = nt(eye, score_ref[...]).astype(BF16)
    expand = one_hot(iota((3 * heads, width), 1) // (width // heads) == iota((3 * heads, width), 0) % heads)
    for copy in copies[:8]:
        copy.wait()
    events = events_buf[...]
    exponent = jnp.exp(nt(score_t, events))
    denominator = join3(nt(split3(exponent), rows))
    weight = exponent / join3(nn(split3(denominator), rows))
    weight_ref[...] = weight
    for copy in copies[8:]:
        copy.wait()
    values = nn(events, value_buf[...])
    weighted = (values * tn(split3(weight), expand)).astype(BF16)
    summary_ref[...] = to_blocks(nn(rows, weighted), users)


def centre_kernel(users, slots, user_ref, day_ref, events_ref, value_ref, summary_ref, out_ref):
    rows = slot_rows(user_ref, day_ref, users, slots)
    pooled = to_rows(summary_ref[...], value_ref.shape[1])
    values = nn(events_ref[...], value_ref[...])
    out_ref[...] = (values - tn(rows, pooled)).astype(BF16)


def attention_kernel(heads, loss_scale, x_ref, cot_ref, qkv_weight_ref, grad_ref, normed_ref, grad_qkv_ref):
    width = qkv_weight_ref.shape[0]
    days = cot_ref.shape[0]
    buckets = x_ref.shape[0]
    size = width // heads
    causal = iota((days, days), 1) <= iota((days, days), 0)
    cot = cot_ref[...]
    wide = to_rows(x_ref[...], width).astype(F32)
    inverse = lax.rsqrt(jnp.mean(wide * wide, axis=-1, keepdims=True) + 1e-06)
    normed = (wide * inverse).astype(BF16)
    normed_ref[...] = normed
    qkv = nn(normed, qkv_weight_ref[...]).astype(BF16)
    pair = 2 * size
    left = iota((days, pair), 1) < size
    zero = jnp.zeros((days, pair), BF16)
    root = 1.0 / math.sqrt(size)
    parts = ([], [], [])
    for start in range(0, width, pair):
        q, k, v = (qkv[:, i * width + start : i * width + start + pair] for i in range(3))
        c = cot[:, start : start + pair]
        held = ([], [], [], [], [])
        for half in range(2):
            mine = left if half == 0 else ~left
            q1, k1, v1, c1 = (jnp.where(mine, a, zero) for a in (q, k, v, c))
            exponent = jnp.where(causal, jnp.exp(nt(q, k1) * root), 0.0)
            total = jnp.sum(exponent, axis=-1, keepdims=True)
            guard = jnp.where(total > 1.0, 2.0**-64, 1.0)
            attention = (exponent * guard) * (1.0 / (total * guard))
            grad_probs = nt(c, v1) * loss_scale
            inner = jnp.sum(grad_probs * attention, axis=-1, keepdims=True)
            grad_logits = (attention * (grad_probs - inner) * root).astype(BF16)
            for group, item in zip(held, (grad_logits, attention.astype(BF16), q1, k1, c1)):
                group.append(item)
        logits_grad, probs, q2, k2, c2 = held
        parts[0].append(nn(jnp.concatenate(logits_grad, 1), jnp.concatenate(k2, 0)))
        parts[1].append(tn(jnp.concatenate(logits_grad, 0), jnp.concatenate(q2, 0)))
        parts[2].append(tn(jnp.concatenate(probs, 0), jnp.concatenate(c2, 0)) * loss_scale)
    grad_qkv = jnp.concatenate([a.astype(BF16) for part in parts for a in part], axis=1)
    grad_qkv_ref[...] = grad_qkv
    grad_normed = nt(grad_qkv, qkv_weight_ref[...])
    cubed = inverse * inverse * inverse
    grad = (
        cot.astype(F32) * loss_scale
        + inverse * grad_normed
        - wide * cubed * jnp.mean(grad_normed * wide, axis=-1, keepdims=True)
    )
    grad_ref[...] = to_blocks(grad, buckets)


def outer_kernel(rows, core_ref, normed_ref, grad_qkv_ref, mine_ref, other_ref):
    width, columns = normed_ref.shape[1], grad_qkv_ref.shape[1]
    product = tn(normed_ref[...], grad_qkv_ref[...]).reshape(width // (2 * rows), 2, rows, columns)
    even = product[:, 0].reshape(width // 2, columns).astype(BF16)
    odd = product[:, 1].reshape(width // 2, columns).astype(BF16)
    first = core_ref[0] == 0

    @pl.when(first)
    def _():
        mine_ref[...] = even
        other_ref[...] = odd

    @pl.when(jnp.logical_not(first))
    def _():
        mine_ref[...] = odd
        other_ref[...] = even


def fold_kernel(row_ref, mine_ref, theirs_ref, keep_ref, send_ref):
    half = keep_ref.shape[1]
    total = (mine_ref[...].astype(F32) + theirs_ref[...].astype(F32)).astype(BF16)
    first = row_ref[0] == 0

    @pl.when(first)
    def _():
        keep_ref[...] = total[:, :half]
        send_ref[...] = total[:, half:]

    @pl.when(jnp.logical_not(first))
    def _():
        keep_ref[...] = total[:, half:]
        send_ref[...] = total[:, :half]


def score_kernel(
    users, slots, cores, user_ref, day_ref, events_ref, centred_ref, weight_ref, grad_ref, keep_ref, got_ref, out_ref
):
    width = events_ref.shape[1]
    heads = weight_ref.shape[0]
    chips, depth, columns = out_ref.shape
    half = keep_ref.shape[1]
    lanes = columns - half
    weight_sum = keep_ref[...].astype(F32) + got_ref[...].astype(F32)
    out_ref[:, :, :half] = weight_sum.reshape(chips, depth, half).astype(BF16)
    rows = slot_rows(user_ref, day_ref, users, slots)
    grad = tn(rows, to_rows(grad_ref[...], width))
    terms = (grad * centred_ref[...].astype(F32)).astype(BF16)
    reduce = one_hot(iota((lanes, width), 1) // (width // heads) == iota((lanes, width), 0) % heads)
    weight = jnp.concatenate([weight_ref[...]] * (lanes // heads), axis=0)
    scores = (weight * nt(reduce, terms)).astype(BF16)
    spread = nn(scores, events_ref[...])
    keep = (iota((lanes, width), 1) // depth) % cores == iota((lanes, width), 0) // heads
    turned = jnp.transpose(jnp.where(keep, spread, 0.0), (1, 0))
    out_ref[:, :, half:] = jnp.sum(turned.reshape(chips, cores, depth, lanes), axis=1).astype(BF16)


def merge_kernel(x_ref, out_ref):
    total = jnp.sum(x_ref[...].astype(F32), axis=0).astype(BF16)
    for i in range(out_ref.shape[0]):
        out_ref[i] = total


def final_kernel(cores, core_ref, x_ref, weight_ref, score_ref):
    half = weight_ref.shape[1] // 2
    heads = score_ref.shape[1]
    groups = x_ref.shape[0] // cores
    core = core_ref[0]
    mine = [x_ref[cores * r + core].astype(F32) for r in range(groups)]
    weight_ref[:, :half] = sum(m[:, :half] for m in mine[0::2])
    weight_ref[:, half:] = sum(m[:, :half] for m in mine[1::2])
    score = jnp.sum(x_ref[:, :, half:].astype(F32), axis=0)
    lanes = score.shape[1]
    pick = one_hot(iota((lanes, heads), 0) == iota((lanes, heads), 1) + core * heads)
    depth = score.shape[0]
    pieces = nn(split3(score), pick)
    score_ref[...] = pieces[:depth] + pieces[depth : 2 * depth] + pieces[2 * depth :]


def call(kernel, outs, args, scalars=0, flops=0, whole=(), scratch=(), limit=24):
    vmem = pl.BlockSpec(memory_space=pltpu.VMEM)
    smem = pl.BlockSpec(memory_space=pltpu.SMEM)
    anywhere = pl.BlockSpec(memory_space=pl.ANY)
    specs = [smem if i < scalars else anywhere if i in whole else vmem for i in range(len(args))]
    moved = sum(a.size * a.dtype.itemsize for a in args) + sum(math.prod(s) * jnp.dtype(t).itemsize for s, t in outs)
    return pl.pallas_call(
        kernel,
        out_shape=[jax.ShapeDtypeStruct(s, t) for s, t in outs],
        in_specs=specs,
        out_specs=[vmem] * len(outs),
        scratch_shapes=scratch,
        compiler_params=pltpu.CompilerParams(vmem_limit_bytes=limit * 2**20),
        cost_estimate=pl.CostEstimate(flops=flops, bytes_accessed=moved, transcendentals=0),
    )(*args)


def shards(sizes, events, event_user, event_day, score_weight, value_weight, qkv_weight, cotangent):
    groups, x_size, z_size, cores = sizes
    chips = x_size * z_size
    buckets = chips * cores
    user_dev, days, width = cotangent.shape
    heads = score_weight.shape[1]
    day_dev = days // buckets
    users = user_dev * buckets
    slots = users * day_dev
    count = events.shape[0]
    rows = width // buckets
    half = 3 * width // 2
    loss_scale = 1.0 / math.sqrt(user_dev * buckets * groups * days)
    user_row = event_user.reshape(1, count)
    day_row = event_day.reshape(1, count)
    core = lax.axis_index("core").reshape(1)
    parity = (lax.axis_index("rep") % 2).reshape(1)

    block = ((buckets, day_dev * width // 128, 128), BF16)
    summary, weight = call(
        functools.partial(pool_kernel, users, slots),
        [block, ((heads, count), F32)],
        (user_row, day_row, score_weight, events, value_weight),
        flops=2 * count * width * (width + slots),
        whole=(3, 4),
        scratch=[pltpu.VMEM((count, width), BF16), pltpu.VMEM((width, width), BF16), pltpu.SemaphoreType.DMA((12,))],
        limit=60,
    )
    by_user = lax.all_to_all(summary, DAY, split_axis=0, concat_axis=0, tiled=True)
    (centred,) = call(
        functools.partial(centre_kernel, users, slots),
        [((count, width), BF16)],
        (user_row, day_row, events, value_weight, summary),
        flops=2 * count * width * (width + slots),
    )
    grad_summary, normed, grad_qkv = call(
        functools.partial(attention_kernel, heads, loss_scale),
        [block, ((days, width), BF16), ((days, 3 * width), BF16)],
        (by_user, cotangent.reshape(days, width), qkv_weight),
        flops=2 * days * width * (6 * width + 14 * days),
    )
    grad_days = lax.all_to_all(grad_summary, DAY, split_axis=0, concat_axis=0, tiled=True)
    mine, other = call(
        functools.partial(outer_kernel, rows),
        [((width // 2, 3 * width), BF16)] * 2,
        (core, normed, grad_qkv),
        scalars=1,
        flops=2 * days * width * 3 * width,
    )
    theirs = lax.ppermute(other, "core", [(i, cores - 1 - i) for i in range(cores)])
    keep, send = call(fold_kernel, [((width // 2, half), BF16)] * 2, (parity, mine, theirs), scalars=1)
    got = lax.ppermute(send, "rep", [(i, i ^ 1) for i in range(groups)])
    (partial_sums,) = call(
        functools.partial(score_kernel, users, slots, cores),
        [((chips, rows, half + 128), BF16)],
        (user_row, day_row, events, centred, weight, grad_days, keep, got),
        flops=2 * count * width * (slots + 256),
    )
    plane = lax.all_to_all(partial_sums, ("x", "z"), split_axis=0, concat_axis=0, tiled=True)
    (merged,) = call(merge_kernel, [((groups * cores, rows, half + 128), BF16)], (plane,))
    everyone = lax.all_to_all(merged, ("rep", "core"), split_axis=0, concat_axis=0, tiled=True)
    return tuple(
        call(
            functools.partial(final_kernel, cores),
            [((rows, 3 * width), F32), ((rows, heads), F32)],
            (core, everyone),
            scalars=1,
        )
    )


def solution(mesh):
    sizes = (8, 4, 8, 2)
    split = Mesh(mesh.devices.reshape(sizes), ("rep",) + DAY)
    whole = ("rep",) + DAY
    in_specs = (P(whole, None), P(whole), P(whole), P(), P(), P(), P(whole, None, None))
    out_specs = (P(DAY, None), P(DAY, None))
    return jax.shard_map(
        functools.partial(shards, sizes), mesh=split, in_specs=in_specs, out_specs=out_specs, check_vma=False
    )
```

```python
import functools
import math

import jax
import jax.numpy as jnp
from jax import lax
from jax.experimental import pallas as pl
from jax.experimental.pallas import tpu as pltpu
from jax.sharding import Mesh, PartitionSpec as P

DAY = ("x", "z", "core")
F32 = jnp.float32
BF16 = jnp.bfloat16
BF16_MAX = 3.3895313892515355e38


def iota(shape, dim):
    return lax.broadcasted_iota(jnp.int32, shape, dim)


def one_hot(condition):
    return jnp.where(condition, 1.0, 0.0).astype(BF16)


def dot(a, b, dims):
    return lax.dot_general(a, b, ((dims[0], dims[1]), ((), ())), preferred_element_type=F32)


def nn(a, b):
    return dot(a, b, ((1,), (0,)))


def nt(a, b):
    return dot(a, b, ((1,), (1,)))


def tn(a, b):
    return dot(a, b, ((0,), (0,)))


def split3(x):
    high = jnp.minimum(x, BF16_MAX).astype(BF16)
    rest = x - high.astype(F32)
    middle = rest.astype(BF16)
    low = (rest - middle.astype(F32)).astype(BF16)
    return jnp.concatenate([high.astype(F32), middle.astype(F32), low.astype(F32)], 0).astype(BF16)


def join3(x):
    n = x.shape[0] // 3
    return x[:n] + x[n : 2 * n] + x[2 * n :]


def slot_rows(user_ref, day_ref, users, slots):
    segment = user_ref[...] * (slots // users) + day_ref[...]
    return one_hot(iota((slots, segment.shape[1]), 0) == segment)


def to_rows(x, width):
    blocks, depth, lanes = x.shape
    parts = width // lanes
    x = x.astype(F32).reshape(blocks, parts, depth // parts, lanes)
    return jnp.concatenate([x[:, i].reshape(-1, lanes) for i in range(parts)], axis=1)


def to_blocks(x, blocks):
    parts = x.shape[1] // 128
    x = x.astype(F32)
    pieces = [x[:, i * 128 : (i + 1) * 128].reshape(blocks, -1, 128) for i in range(parts)]
    return jnp.concatenate(pieces, axis=1).astype(BF16)


def pool_kernel(
    users, slots, user_ref, day_ref, score_ref, events_ref, value_ref, summary_ref, weight_ref,
    events_buf, value_buf, value_sem, event_sems,
):
    heads, width = score_ref.shape
    steps = event_sems.shape[0]
    step = events_ref.shape[0] // steps
    value_copy = pltpu.make_async_copy(value_ref, value_buf, value_sem)
    pieces = [pl.ds(i * step, step) for i in range(steps)]
    copies = [
        pltpu.make_async_copy(events_ref.at[piece, :], events_buf.at[piece, :], event_sems.at[i])
        for i, piece in enumerate(pieces)
    ]
    value_copy.start()
    for copy in copies:
        copy.start()
    rows = slot_rows(user_ref, day_ref, users, slots)
    expand = one_hot(iota((3 * heads, width), 1) // (width // heads) == iota((3 * heads, width), 0) % heads)
    score = score_ref[...]
    value_copy.wait()
    value = value_buf[...]
    logits, values = [], []
    for i in range(steps):
        copies[i].wait()
        part = events_buf[pieces[i], :]
        logits.append(nt(score, part))
        values.append(nn(part, value))
    exponent = jnp.exp(jnp.concatenate(logits, axis=1))
    denominator = join3(nt(split3(exponent), rows))
    weight = exponent / join3(nn(split3(denominator), rows))
    weight_ref[...] = weight
    weighted = (jnp.concatenate(values, axis=0) * tn(split3(weight), expand)).astype(BF16)
    summary_ref[...] = to_blocks(nn(rows, weighted), users)


def centre_kernel(users, slots, user_ref, day_ref, events_ref, value_ref, summary_ref, out_ref):
    rows = slot_rows(user_ref, day_ref, users, slots)
    pooled = to_rows(summary_ref[...], value_ref.shape[1]).astype(BF16)
    values = nn(events_ref[...], value_ref[...])
    out_ref[...] = (values - tn(rows, pooled)).astype(BF16)


def attention_kernel(heads, loss_scale, x_ref, cot_ref, qkv_weight_ref, grad_ref, pack_ref, pack_buf, sems):
    width = qkv_weight_ref.shape[0]
    days = cot_ref.shape[0]
    buckets = x_ref.shape[0]
    size = width // heads
    causal = iota((days, days), 1) <= iota((days, days), 0)
    cot = cot_ref[...]
    wide = to_rows(x_ref[...], width)
    inverse = lax.rsqrt(jnp.mean(wide * wide, axis=-1, keepdims=True) + 1e-06)
    normed = (wide * inverse).astype(BF16)
    pieces = [pl.ds(i * width, width) for i in range(4)]
    copies = [pltpu.make_async_copy(pack_buf.at[:, p], pack_ref.at[:, p], sems.at[i]) for i, p in enumerate(pieces)]
    pack_buf[:, pieces[0]] = normed
    copies[0].start()
    qkv = nn(normed, qkv_weight_ref[...]).astype(BF16)
    pair = 2 * size
    left = iota((days, pair), 1) < size
    zero = jnp.zeros((days, pair), BF16)
    root = 1.0 / math.sqrt(size)
    parts = ([], [], [])
    for start in range(0, width, pair):
        q, k, v = (qkv[:, i * width + start : i * width + start + pair] for i in range(3))
        c = cot[:, start : start + pair]
        held = ([], [], [], [], [])
        for half in range(2):
            mine = left if half == 0 else ~left
            q1, k1, v1, c1 = (jnp.where(mine, a, zero) for a in (q, k, v, c))
            exponent = jnp.where(causal, jnp.exp(nt(q, k1) * root), 0.0)
            total = jnp.sum(exponent, axis=-1, keepdims=True)
            guard = jnp.where(total > 1.0, 2.0**-64, 1.0)
            attention = (exponent * guard) * (1.0 / (total * guard))
            grad_probs = nt(c, v1) * loss_scale
            inner = jnp.sum(grad_probs * attention, axis=-1, keepdims=True)
            grad_logits = (attention * (grad_probs - inner) * root).astype(BF16)
            for group, item in zip(held, (grad_logits, attention.astype(BF16), q1, k1, c1)):
                group.append(item)
        logits_grad, probs, q2, k2, c2 = held
        parts[0].append(nn(jnp.concatenate(logits_grad, 1), jnp.concatenate(k2, 0)))
        parts[1].append(tn(jnp.concatenate(logits_grad, 0), jnp.concatenate(q2, 0)))
        parts[2].append(tn(jnp.concatenate(probs, 0), jnp.concatenate(c2, 0)) * loss_scale)
    grad_qkv = jnp.concatenate([a.astype(BF16) for part in parts for a in part], axis=1)
    pack_buf[:, width:] = grad_qkv
    for copy in copies[1:]:
        copy.start()
    grad_normed = nt(grad_qkv, qkv_weight_ref[...])
    cubed = inverse * inverse * inverse
    grad = (
        cot.astype(F32) * loss_scale
        + inverse * grad_normed
        - wide * cubed * jnp.mean(grad_normed * wide, axis=-1, keepdims=True)
    )
    grad_ref[...] = to_blocks(grad, buckets)
    for copy in copies:
        copy.wait()


def outer_kernel(depth, core_ref, row_ref, mine_ref, theirs_ref, keep_ref, up_ref, down_ref):
    quarter = up_ref.shape[1]
    width = mine_ref.shape[1] - 4 * quarter
    count = width // 2
    both = jnp.concatenate([mine_ref[...], theirs_ref[...]], axis=0)
    column = iota((width, count), 1)
    pick = one_hot(iota((width, count), 0) == (2 * (column // depth) + core_ref[0]) * depth + column % depth)
    total = tn(nn(both[:, :width], pick).astype(BF16), both[:, width:]).astype(BF16)
    first = row_ref[0] & 1 == 0
    for side, send_ref in ((0, up_ref), (1, down_ref)):
        low = total[:, 2 * side * quarter : (2 * side + 1) * quarter]
        high = total[:, (2 * side + 1) * quarter : (2 * side + 2) * quarter]
        keep_ref[:, side * quarter : (side + 1) * quarter] = jnp.where(first, low, high)
        send_ref[...] = jnp.where(first, high, low)


def score_kernel(
    users, slots, cores, user_ref, day_ref, events_ref, centred_ref, weight_ref, grad_ref, keep_ref, up_ref, down_ref, out_ref
):
    width = events_ref.shape[1]
    heads = weight_ref.shape[0]
    chips, depth, columns = out_ref.shape
    half = keep_ref.shape[1]
    lanes = columns - half
    quarter = half // 2
    for start, got_ref in ((0, up_ref), (quarter, down_ref)):
        weight_sum = keep_ref[:, start : start + quarter].astype(F32) + got_ref[...].astype(F32)
        out_ref[:, :, start : start + quarter] = weight_sum.reshape(chips, depth, quarter).astype(BF16)
    rows = slot_rows(user_ref, day_ref, users, slots)
    grad = tn(rows, to_rows(grad_ref[...], width).astype(BF16))
    terms = (grad * centred_ref[...].astype(F32)).astype(BF16)
    reduce = one_hot(iota((lanes, width), 1) // (width // heads) == iota((lanes, width), 0) % heads)
    weight = jnp.concatenate([weight_ref[...]] * (lanes // heads), axis=0)
    scores = (weight * nt(reduce, terms)).astype(BF16)
    spread = nn(scores, events_ref[...])
    keep = (iota((lanes, width), 1) // depth) % cores == iota((lanes, width), 0) // heads
    turned = jnp.transpose(jnp.where(keep, spread, 0.0), (1, 0))
    out_ref[:, :, half:] = jnp.sum(turned.reshape(chips, cores, depth, lanes), axis=1).astype(BF16)


def merge_kernel(x_ref, out_ref):
    total = jnp.sum(x_ref[...].astype(F32), axis=0).astype(BF16)
    for i in range(out_ref.shape[0]):
        out_ref[i] = total


def final_kernel(cores, core_ref, x_ref, weight_ref, score_ref):
    half = weight_ref.shape[1] // 2
    heads = score_ref.shape[1]
    groups = x_ref.shape[0] // cores
    core = core_ref[0]
    mine = [x_ref[cores * r + core].astype(F32) for r in range(groups)]
    quarter = half // 2
    for side in range(2):
        for bit in range(2):
            held = [m[:, side * quarter : (side + 1) * quarter] for r, m in enumerate(mine) if r % 2 == bit]
            weight_ref[:, (2 * side + bit) * quarter : (2 * side + bit + 1) * quarter] = sum(held)
    score = jnp.sum(x_ref[:, :, half:].astype(F32), axis=0)
    lanes = score.shape[1]
    pick = one_hot(iota((lanes, heads), 0) == iota((lanes, heads), 1) + core * heads)
    depth = score.shape[0]
    pieces = nn(split3(score), pick)
    score_ref[...] = pieces[:depth] + pieces[depth : 2 * depth] + pieces[2 * depth :]


def call(kernel, outs, args, scalars=0, flops=0, moved=None, whole=(), out_whole=(), scratch=(), limit=24):
    vmem = pl.BlockSpec(memory_space=pltpu.VMEM)
    smem = pl.BlockSpec(memory_space=pltpu.SMEM)
    anywhere = pl.BlockSpec(memory_space=pltpu.HBM)
    specs = [smem if i < scalars else anywhere if i in whole else vmem for i in range(len(args))]
    if moved is None:
        moved = sum(a.size * a.dtype.itemsize for a in args) + sum(math.prod(s) * jnp.dtype(t).itemsize for s, t in outs)
    return pl.pallas_call(
        kernel,
        out_shape=[pltpu.HBM(s, t) if i in out_whole else jax.ShapeDtypeStruct(s, t) for i, (s, t) in enumerate(outs)],
        in_specs=specs,
        out_specs=[anywhere if i in out_whole else vmem for i in range(len(outs))],
        scratch_shapes=scratch,
        compiler_params=pltpu.CompilerParams(vmem_limit_bytes=limit * 2**20),
        cost_estimate=pl.CostEstimate(flops=flops, bytes_accessed=moved, transcendentals=0),
    )(*args)


def shards(sizes, events, event_user, event_day, score_weight, value_weight, qkv_weight, cotangent):
    groups, x_size, z_size, cores = sizes
    chips = x_size * z_size
    buckets = chips * cores
    user_dev, days, width = cotangent.shape
    heads = score_weight.shape[1]
    day_dev = days // buckets
    users = user_dev * buckets
    slots = users * day_dev
    count = events.shape[0]
    rows = width // buckets
    half = 3 * width // 2
    loss_scale = 1.0 / math.sqrt(user_dev * buckets * groups * days)
    user_row = event_user.reshape(1, count)
    day_row = event_day.reshape(1, count)
    core = lax.axis_index("core").reshape(1)
    row = lax.axis_index("rep").reshape(1)

    block = ((buckets, day_dev * width // 128, 128), BF16)
    summary, weight = call(
        functools.partial(pool_kernel, users, slots),
        [block, ((heads, count), F32)],
        (user_row, day_row, score_weight.T, events, value_weight),
        flops=2 * count * width * (width + slots),
        whole=(3, 4),
        scratch=[
            pltpu.VMEM((count, width), BF16),
            pltpu.VMEM((width, width), BF16),
            pltpu.SemaphoreType.DMA,
            pltpu.SemaphoreType.DMA((4,)),
        ],
        limit=60,
    )
    by_user = lax.all_to_all(summary, DAY, split_axis=0, concat_axis=0, tiled=True)
    (centred,) = call(
        functools.partial(centre_kernel, users, slots),
        [((count, width), BF16)],
        (user_row, day_row, events, value_weight, summary),
        flops=2 * count * width * (width + slots),
    )
    grad_summary, mine = call(
        functools.partial(attention_kernel, heads, loss_scale),
        [block, ((days, 4 * width), BF16)],
        (by_user, cotangent.reshape(days, width), qkv_weight),
        flops=2 * days * width * (6 * width + 14 * days),
        out_whole=(1,),
        scratch=[pltpu.VMEM((days, 4 * width), BF16), pltpu.SemaphoreType.DMA((4,))],
    )
    grad_days = lax.all_to_all(grad_summary, DAY, split_axis=0, concat_axis=0, tiled=True)
    theirs = lax.ppermute(mine, "core", [(i, cores - 1 - i) for i in range(cores)])
    keep, send_up, send_down = call(
        functools.partial(outer_kernel, rows),
        [((width // 2, half), BF16)] + [((width // 2, half // 2), BF16)] * 2,
        (core, row, mine, theirs),
        scalars=2,
        moved=0,
    )
    up = lax.ppermute(send_up, "rep", [(i, i ^ 1) for i in range(groups)])
    down = lax.ppermute(send_down, "rep", [(i, (((i + 1) ^ 1) - 1) % groups) for i in range(groups)])
    (partial_sums,) = call(
        functools.partial(score_kernel, users, slots, cores),
        [((chips, rows, half + 128), BF16)],
        (user_row, day_row, events, centred, weight, grad_days, keep, up, down),
        flops=2 * count * width * (slots + 256),
    )
    plane = lax.all_to_all(partial_sums, ("x", "z"), split_axis=0, concat_axis=0, tiled=True)
    (merged,) = call(merge_kernel, [((groups * cores, rows, half + 128), BF16)], (plane,))
    everyone = lax.all_to_all(merged, ("rep", "core"), split_axis=0, concat_axis=0, tiled=True)
    return tuple(
        call(
            functools.partial(final_kernel, cores),
            [((rows, 3 * width), F32), ((rows, heads), F32)],
            (core, everyone),
            scalars=1,
        )
    )


def solution(mesh):
    sizes = (8, 4, 8, 2)
    split = Mesh(mesh.devices.reshape(sizes), ("rep",) + DAY)
    whole = ("rep",) + DAY
    in_specs = (P(whole, None), P(whole), P(whole), P(), P(), P(), P(whole, None, None))
    out_specs = (P(DAY, None), P(DAY, None))
    return jax.shard_map(
        functools.partial(shards, sizes), mesh=split, in_specs=in_specs, out_specs=out_specs, check_vma=False
    )
```

```python
import functools
import math

import jax
import jax.numpy as jnp
from jax import lax
from jax.experimental import pallas as pl
from jax.experimental.pallas import tpu as pltpu
from jax.sharding import Mesh, PartitionSpec as P

DAY = ("x", "z", "core")
F32 = jnp.float32
BF16 = jnp.bfloat16
BF16_MAX = 3.3895313892515355e38


def iota(shape, dim):
    return lax.broadcasted_iota(jnp.int32, shape, dim)


def one_hot(condition):
    return jnp.where(condition, 1.0, 0.0).astype(BF16)


def dot(a, b, dims):
    return lax.dot_general(a, b, ((dims[0], dims[1]), ((), ())), preferred_element_type=F32)


def nn(a, b):
    return dot(a, b, ((1,), (0,)))


def nt(a, b):
    return dot(a, b, ((1,), (1,)))


def tn(a, b):
    return dot(a, b, ((0,), (0,)))


def split3(x):
    high = jnp.minimum(x, BF16_MAX).astype(BF16)
    rest = x - high.astype(F32)
    middle = rest.astype(BF16)
    low = (rest - middle.astype(F32)).astype(BF16)
    return jnp.concatenate([high.astype(F32), middle.astype(F32), low.astype(F32)], 0).astype(BF16)


def join3(x):
    n = x.shape[0] // 3
    return x[:n] + x[n : 2 * n] + x[2 * n :]


def slot_rows(user_ref, day_ref, users, slots):
    segment = user_ref[...] * (slots // users) + day_ref[...]
    return one_hot(iota((slots, segment.shape[1]), 0) == segment)


def to_rows(x, width):
    blocks, depth, lanes = x.shape
    parts = width // lanes
    x = x.astype(F32).reshape(blocks, parts, depth // parts, lanes)
    return jnp.concatenate([x[:, i].reshape(-1, lanes) for i in range(parts)], axis=1)


def to_blocks(x, blocks):
    parts = x.shape[1] // 128
    x = x.astype(F32)
    pieces = [x[:, i * 128 : (i + 1) * 128].reshape(blocks, -1, 128) for i in range(parts)]
    return jnp.concatenate(pieces, axis=1).astype(BF16)


def pool_kernel(
    users, slots, user_ref, day_ref, score_ref, events_ref, value_ref, summary_ref, weight_ref,
    events_buf, value_buf, value_sem, event_sems,
):
    heads, width = score_ref.shape
    steps = event_sems.shape[0]
    step = events_ref.shape[0] // steps
    value_copy = pltpu.make_async_copy(value_ref, value_buf, value_sem)
    pieces = [pl.ds(i * step, step) for i in range(steps)]
    copies = [
        pltpu.make_async_copy(events_ref.at[piece, :], events_buf.at[piece, :], event_sems.at[i])
        for i, piece in enumerate(pieces)
    ]
    value_copy.start()
    for copy in copies:
        copy.start()
    rows = slot_rows(user_ref, day_ref, users, slots)
    expand = one_hot(iota((3 * heads, width), 1) // (width // heads) == iota((3 * heads, width), 0) % heads)
    score = score_ref[...]
    value_copy.wait()
    value = value_buf[...]
    logits, values = [], []
    for i in range(steps):
        copies[i].wait()
        part = events_buf[pieces[i], :]
        logits.append(nt(score, part))
        values.append(nn(part, value))
    exponent = jnp.exp(jnp.concatenate(logits, axis=1))
    denominator = join3(nt(split3(exponent), rows))
    weight = exponent / join3(nn(split3(denominator), rows))
    weight_ref[...] = weight
    weighted = (jnp.concatenate(values, axis=0) * tn(split3(weight), expand)).astype(BF16)
    summary_ref[...] = to_blocks(nn(rows, weighted), users)


def centre_kernel(users, slots, user_ref, day_ref, events_ref, value_ref, summary_ref, qkv_ref, out_ref, qkv_out, sem):
    copy = pltpu.make_async_copy(qkv_ref, qkv_out, sem)
    copy.start()
    rows = slot_rows(user_ref, day_ref, users, slots)
    pooled = to_rows(summary_ref[...], value_ref.shape[1]).astype(BF16)
    values = nn(events_ref[...], value_ref[...])
    out_ref[...] = (values - tn(rows, pooled)).astype(BF16)
    copy.wait()


def attention_kernel(heads, loss_scale, core_ref, x_ref, cot_ref, qkv_weight_ref, grad_ref, mine_ref, send_ref, cot_buf, mine_buf, send_buf, sems):
    width = qkv_weight_ref.shape[0]
    days = cot_ref.shape[0]
    cot_copy = pltpu.make_async_copy(cot_ref, cot_buf, sems.at[2])
    cot_copy.start()
    buckets = x_ref.shape[0]
    size = width // heads
    causal = iota((days, days), 1) <= iota((days, days), 0)
    wide = to_rows(x_ref[...], width)
    inverse = lax.rsqrt(jnp.mean(wide * wide, axis=-1, keepdims=True) + 1e-06)
    normed = (wide * inverse).astype(BF16)
    mine_buf[:, :width] = normed
    send_buf[:, :width] = normed
    qkv = nn(normed, qkv_weight_ref[...]).astype(BF16)
    cot_copy.wait()
    cot = cot_buf[...]
    pair = 2 * size
    left = iota((days, pair), 1) < size
    zero = jnp.zeros((days, pair), BF16)
    root = 1.0 / math.sqrt(size)
    parts = ([], [], [])
    for start in range(0, width, pair):
        q, k, v = (qkv[:, i * width + start : i * width + start + pair] for i in range(3))
        c = cot[:, start : start + pair]
        held = ([], [], [], [], [])
        for half in range(2):
            mine = left if half == 0 else ~left
            q1, k1, v1, c1 = (jnp.where(mine, a, zero) for a in (q, k, v, c))
            exponent = jnp.where(causal, jnp.exp(nt(q, k1) * root), 0.0)
            total = jnp.sum(exponent, axis=-1, keepdims=True)
            guard = jnp.where(total > 1.0, 2.0**-64, 1.0)
            attention = (exponent * guard) * (1.0 / (total * guard))
            grad_probs = nt(c, v1) * loss_scale
            inner = jnp.sum(grad_probs * attention, axis=-1, keepdims=True)
            grad_logits = (attention * (grad_probs - inner) * root).astype(BF16)
            for group, item in zip(held, (grad_logits, attention.astype(BF16), q1, k1, c1)):
                group.append(item)
        logits_grad, probs, q2, k2, c2 = held
        parts[0].append(nn(jnp.concatenate(logits_grad, 1), jnp.concatenate(k2, 0)))
        parts[1].append(tn(jnp.concatenate(logits_grad, 0), jnp.concatenate(q2, 0)))
        parts[2].append(tn(jnp.concatenate(probs, 0), jnp.concatenate(c2, 0)) * loss_scale)
    grad_qkv = jnp.concatenate([a.astype(BF16) for part in parts for a in part], axis=1)
    half = 3 * width // 2
    first = core_ref[0] == 0
    mine_buf[:, width:] = jnp.where(first, grad_qkv[:, :half], grad_qkv[:, half:])
    send_buf[:, width:] = jnp.where(first, grad_qkv[:, half:], grad_qkv[:, :half])
    copies = [
        pltpu.make_async_copy(send_buf, send_ref, sems.at[0]),
        pltpu.make_async_copy(mine_buf, mine_ref, sems.at[1]),
    ]
    for copy in copies:
        copy.start()
    grad_normed = nt(grad_qkv, qkv_weight_ref[...])
    cubed = inverse * inverse * inverse
    grad = (
        cot.astype(F32) * loss_scale
        + inverse * grad_normed
        - wide * cubed * jnp.mean(grad_normed * wide, axis=-1, keepdims=True)
    )
    grad_ref[...] = to_blocks(grad, buckets)
    for copy in copies:
        copy.wait()


def outer_kernel(width, mine_ref, theirs_ref, out_ref):
    both = jnp.concatenate([mine_ref[...], theirs_ref[...]], axis=0)
    out_ref[...] = tn(both[:, :width], both[:, width:]).reshape(out_ref.shape).astype(BF16)


def score_kernel(users, slots, user_ref, day_ref, events_ref, centred_ref, weight_ref, grad_ref, outer_ref, out_ref):
    width = events_ref.shape[1]
    heads = weight_ref.shape[0]
    parts, depth, half = outer_ref.shape
    lanes = out_ref.shape[2] - half
    out_ref[:, :, :half] = outer_ref[...]
    rows = slot_rows(user_ref, day_ref, users, slots)
    grad = tn(rows, to_rows(grad_ref[...], width).astype(BF16))
    terms = (grad * centred_ref[...].astype(F32)).astype(BF16)
    reduce = one_hot(iota((heads, width), 1) // (width // heads) == iota((heads, width), 0))
    scores = (weight_ref[...] * nt(reduce, terms)).astype(BF16)
    scores = jnp.concatenate([scores.astype(F32), jnp.zeros((lanes - heads, scores.shape[1]), F32)], axis=0).astype(BF16)
    turned = jnp.transpose(nn(scores, events_ref[...]), (1, 0))
    out_ref[:, :, half:] = turned.reshape(parts, depth, lanes).astype(BF16)


def merge_kernel(cores, x_ref, out_ref):
    parts, depth, columns = x_ref.shape
    half = columns - 128
    total = jnp.sum(x_ref[...].astype(F32).reshape(parts // cores, cores, depth, columns), axis=0)
    score = jnp.sum(total[:, :, half:], axis=0)
    pieces = [total[i, :, :half] for i in range(cores)] + [score]
    merged = jnp.concatenate(pieces, axis=1).astype(BF16)
    for i in range(out_ref.shape[0]):
        out_ref[i] = merged


def final_kernel(x_ref, weight_ref, score_ref):
    columns = weight_ref.shape[1]
    total = jnp.sum(x_ref[...].astype(F32), axis=0)
    weight_ref[...] = total[:, :columns]
    score_ref[...] = total[:, columns : columns + score_ref.shape[1]]


def call(kernel, outs, args, scalars=0, flops=0, moved=None, whole=(), held=(), out_whole=(), out_far=(), out_near=(), scratch=(), limit=24):
    vmem = pl.BlockSpec(memory_space=pltpu.VMEM)
    smem = pl.BlockSpec(memory_space=pltpu.SMEM)
    anywhere = pl.BlockSpec(memory_space=pltpu.HBM)
    specs = [smem if i < scalars else anywhere if i in whole else vmem for i in range(len(args))]
    if moved is None:
        moved = sum(a.size * a.dtype.itemsize for a in args) + sum(math.prod(s) * jnp.dtype(t).itemsize for s, t in outs)
    args = [pltpu.with_memory_space_constraint(a, pltpu.HBM) if i in whole + held else a for i, a in enumerate(args)]
    return pl.pallas_call(
        kernel,
        out_shape=[
            pltpu.HBM(s, t) if i in out_whole + out_far else pltpu.VMEM(s, t) if i in out_near else jax.ShapeDtypeStruct(s, t)
            for i, (s, t) in enumerate(outs)
        ],
        in_specs=specs,
        out_specs=[anywhere if i in out_whole else vmem for i in range(len(outs))],
        scratch_shapes=scratch,
        compiler_params=pltpu.CompilerParams(vmem_limit_bytes=limit * 2**20),
        cost_estimate=pl.CostEstimate(flops=flops, bytes_accessed=moved, transcendentals=0),
    )(*args)


def shards(sizes, events, event_user, event_day, score_weight, value_weight, qkv_weight, cotangent):
    groups, x_size, z_size, cores = sizes
    buckets = x_size * z_size * cores
    user_dev, days, width = cotangent.shape
    heads = score_weight.shape[1]
    day_dev = days // buckets
    users = user_dev * buckets
    slots = users * day_dev
    count = events.shape[0]
    rows = width // buckets
    half = 3 * width // 2
    loss_scale = 1.0 / math.sqrt(user_dev * buckets * groups * days)
    user_row = event_user.reshape(1, count)
    day_row = event_day.reshape(1, count)
    core = lax.axis_index("core").reshape(1)

    block = ((buckets, day_dev * width // 128, 128), BF16)
    summary, weight = call(
        functools.partial(pool_kernel, users, slots),
        [block, ((heads, count), F32)],
        (user_row, day_row, score_weight.T, events, value_weight),
        flops=2 * count * width * (width + slots),
        whole=(3, 4),
        scratch=[
            pltpu.VMEM((count, width), BF16),
            pltpu.VMEM((width, width), BF16),
            pltpu.SemaphoreType.DMA,
            pltpu.SemaphoreType.DMA((4,)),
        ],
        limit=60,
    )
    by_user = lax.all_to_all(summary, DAY, split_axis=0, concat_axis=0, tiled=True)
    centred, qkv_held = call(
        functools.partial(centre_kernel, users, slots),
        [((count, width), BF16), (qkv_weight.shape, BF16)],
        (user_row, day_row, events, value_weight, summary, qkv_weight),
        flops=2 * count * width * (width + slots),
        whole=(5,),
        held=(2, 3),
        out_far=(0,),
        out_near=(1,),
        scratch=[pltpu.SemaphoreType.DMA],
    )
    grad_summary, mine, send = call(
        functools.partial(attention_kernel, heads, loss_scale),
        [block, ((days, width + half), BF16), ((days, width + half), BF16)],
        (core, by_user, cotangent.reshape(days, width), qkv_held),
        scalars=1,
        whole=(2,),
        flops=2 * days * width * (6 * width + 14 * days),
        out_whole=(1, 2),
        scratch=[pltpu.VMEM((days, width), BF16)] + [pltpu.VMEM((days, width + half), BF16)] * 2 + [pltpu.SemaphoreType.DMA((3,))],
    )
    grad_days = lax.all_to_all(grad_summary, DAY, split_axis=0, concat_axis=0, tiled=True)
    theirs = lax.ppermute(send, "core", [(i, cores - 1 - i) for i in range(cores)])
    (outer,) = call(functools.partial(outer_kernel, width), [((buckets, rows, half), BF16)], (mine, theirs), moved=0, held=(0,))
    (partial_sums,) = call(
        functools.partial(score_kernel, users, slots),
        [((buckets, rows, half + 128), BF16)],
        (user_row, day_row, events, centred, weight, grad_days, outer),
        flops=2 * count * width * (slots + 256),
    )
    gathered = lax.all_to_all(partial_sums, DAY, split_axis=0, concat_axis=0, tiled=True)
    (merged,) = call(
        functools.partial(merge_kernel, cores), [((groups, rows, 3 * width + 128), BF16)], (gathered,)
    )
    everyone = lax.all_to_all(merged, "rep", split_axis=0, concat_axis=0, tiled=True)
    return tuple(call(final_kernel, [((rows, 3 * width), F32), ((rows, heads), F32)], (everyone,)))


def solution(mesh):
    sizes = (8, 4, 8, 2)
    split = Mesh(mesh.devices.reshape(sizes), ("rep",) + DAY)
    whole = ("rep",) + DAY
    in_specs = (P(whole, None), P(whole), P(whole), P(), P(), P(), P(whole, None, None))
    out_specs = (P(DAY, None), P(DAY, None))
    return jax.shard_map(
        functools.partial(shards, sizes), mesh=split, in_specs=in_specs, out_specs=out_specs, check_vma=False
    )
```

```python
import functools
import math

import jax
import jax.numpy as jnp
from jax import lax
from jax.experimental import pallas as pl
from jax.experimental.pallas import tpu as pltpu
from jax.sharding import Mesh, PartitionSpec as P

DAY = ("x", "z", "core")
F32 = jnp.float32
BF16 = jnp.bfloat16
BF16_MAX = 3.3895313892515355e38


def iota(shape, dim):
    return lax.broadcasted_iota(jnp.int32, shape, dim)


def one_hot(condition):
    return jnp.where(condition, 1.0, 0.0).astype(BF16)


def dot(a, b, dims):
    return lax.dot_general(a, b, ((dims[0], dims[1]), ((), ())), preferred_element_type=F32)


def nn(a, b):
    return dot(a, b, ((1,), (0,)))


def nt(a, b):
    return dot(a, b, ((1,), (1,)))


def tn(a, b):
    return dot(a, b, ((0,), (0,)))


def split3(x):
    high = jnp.minimum(x, BF16_MAX).astype(BF16)
    rest = x - high.astype(F32)
    middle = rest.astype(BF16)
    low = (rest - middle.astype(F32)).astype(BF16)
    return jnp.concatenate([high.astype(F32), middle.astype(F32), low.astype(F32)], 0).astype(BF16)


def join3(x):
    n = x.shape[0] // 3
    return x[:n] + x[n : 2 * n] + x[2 * n :]


def slot_rows(user_ref, day_ref, users, slots):
    segment = user_ref[...] * (slots // users) + day_ref[...]
    return one_hot(iota((slots, segment.shape[1]), 0) == segment)


def to_rows(x, width):
    blocks, depth, lanes = x.shape
    parts = width // lanes
    x = x.astype(F32).reshape(blocks, parts, depth // parts, lanes)
    return jnp.concatenate([x[:, i].reshape(-1, lanes) for i in range(parts)], axis=1)


def to_blocks(x, blocks):
    parts = x.shape[1] // 128
    x = x.astype(F32)
    pieces = [x[:, i * 128 : (i + 1) * 128].reshape(blocks, -1, 128) for i in range(parts)]
    return jnp.concatenate(pieces, axis=1).astype(BF16)


def pool_kernel(users, slots, *refs):
    sources, (summary_ref, weight_ref), held, sems = refs[:5], refs[5:7], refs[7:12], refs[12]
    copies = [pltpu.make_async_copy(source, target, sems.at[i]) for i, (source, target) in enumerate(zip(sources, held))]
    for copy in copies:
        copy.start()
    user_ref, day_ref, score_ref, events_ref, value_ref = held
    heads, width = score_ref.shape
    expand = one_hot(iota((3 * heads, width), 1) // (width // heads) == iota((3 * heads, width), 0) % heads)
    copies[0].wait()
    copies[1].wait()
    rows = slot_rows(user_ref, day_ref, users, slots)
    copies[2].wait()
    copies[3].wait()
    exponent = jnp.exp(nt(score_ref[...], events_ref[...]))
    denominator = join3(nt(split3(exponent), rows))
    weight = exponent / join3(nn(split3(denominator), rows))
    weight_ref[...] = weight
    wide = tn(split3(weight), expand)
    copies[4].wait()
    weighted = (nn(events_ref[...], value_ref[...]) * wide).astype(BF16)
    summary_ref[...] = to_blocks(nn(rows, weighted), users)


def centre_kernel(users, slots, user_ref, day_ref, events_ref, value_ref, summary_ref, qkv_ref, out_ref, qkv_out, sem):
    copy = pltpu.make_async_copy(qkv_ref, qkv_out, sem)
    copy.start()
    rows = slot_rows(user_ref, day_ref, users, slots)
    pooled = to_rows(summary_ref[...], value_ref.shape[1]).astype(BF16)
    values = nn(events_ref[...], value_ref[...])
    out_ref[...] = (values - tn(rows, pooled)).astype(BF16)
    copy.wait()


def attention_kernel(heads, loss_scale, core_ref, x_ref, cot_ref, qkv_weight_ref, grad_ref, mine_ref, send_ref, cot_buf, mine_buf, sems):
    width = qkv_weight_ref.shape[0]
    days = cot_ref.shape[0]
    cot_copy = pltpu.make_async_copy(cot_ref, cot_buf, sems.at[1])
    cot_copy.start()
    buckets = x_ref.shape[0]
    size = width // heads
    causal = iota((days, days), 1) <= iota((days, days), 0)
    wide = to_rows(x_ref[...], width)
    inverse = lax.rsqrt(jnp.mean(wide * wide, axis=-1, keepdims=True) + 1e-06)
    normed = (wide * inverse).astype(BF16)
    mine_buf[:, :width] = normed
    send_ref[:, :width] = normed
    qkv = nn(normed, qkv_weight_ref[...]).astype(BF16)
    cot_copy.wait()
    cot = cot_buf[...]
    pair = 2 * size
    left = iota((days, pair), 1) < size
    zero = jnp.zeros((days, pair), BF16)
    root = 1.0 / math.sqrt(size)
    parts = ([], [], [])
    for start in range(0, width, pair):
        q, k, v = (qkv[:, i * width + start : i * width + start + pair] for i in range(3))
        c = cot[:, start : start + pair]
        held = ([], [], [], [], [])
        for half in range(2):
            mine = left if half == 0 else ~left
            q1, k1, v1, c1 = (jnp.where(mine, a, zero) for a in (q, k, v, c))
            exponent = jnp.where(causal, jnp.exp(nt(q, k1) * root), 0.0)
            total = jnp.sum(exponent, axis=-1, keepdims=True)
            guard = jnp.where(total > 1.0, 2.0**-64, 1.0)
            attention = (exponent * guard) * (1.0 / (total * guard))
            grad_probs = nt(c, v1) * loss_scale
            inner = jnp.sum(grad_probs * attention, axis=-1, keepdims=True)
            grad_logits = (attention * (grad_probs - inner) * root).astype(BF16)
            for group, item in zip(held, (grad_logits, attention.astype(BF16), q1, k1, c1)):
                group.append(item)
        logits_grad, probs, q2, k2, c2 = held
        parts[0].append(nn(jnp.concatenate(logits_grad, 1), jnp.concatenate(k2, 0)))
        parts[1].append(tn(jnp.concatenate(logits_grad, 0), jnp.concatenate(q2, 0)))
        parts[2].append(tn(jnp.concatenate(probs, 0), jnp.concatenate(c2, 0)) * loss_scale)
    grad_qkv = jnp.concatenate([a.astype(BF16) for part in parts for a in part], axis=1)
    half = 3 * width // 2
    first = core_ref[0] == 0
    mine_buf[:, width:] = jnp.where(first, grad_qkv[:, :half], grad_qkv[:, half:])
    send_ref[:, width:] = jnp.where(first, grad_qkv[:, half:], grad_qkv[:, :half])
    mine_copy = pltpu.make_async_copy(mine_buf, mine_ref, sems.at[0])
    mine_copy.start()
    grad_normed = nt(grad_qkv, qkv_weight_ref[...])
    cubed = inverse * inverse * inverse
    grad = (
        cot.astype(F32) * loss_scale
        + inverse * grad_normed
        - wide * cubed * jnp.mean(grad_normed * wide, axis=-1, keepdims=True)
    )
    grad_ref[...] = to_blocks(grad, buckets)
    mine_copy.wait()


def outer_kernel(width, x_ref, mine_ref, theirs_ref, keep_ref, near_ref, far_ref):
    both = jnp.concatenate([mine_ref[...], theirs_ref[...]], axis=0)
    total = tn(both[:, :width], both[:, width:]).astype(BF16)
    first = x_ref[0] & 1 == 0
    start = 0
    for send_ref in (near_ref, far_ref):
        parts, depth, part = send_ref.shape
        low = total[:, 2 * start : 2 * start + part]
        high = total[:, 2 * start + part : 2 * start + 2 * part]
        keep_ref[:, :, start : start + part] = jnp.where(first, low, high).reshape(parts, depth, part)
        send_ref[...] = jnp.where(first, high, low).reshape(parts, depth, part)
        start += part


def score_kernel(
    users, slots, user_ref, day_ref, events_ref, centred_ref, weight_ref, grad_ref, keep_ref, near_ref, far_ref, out_ref
):
    width = events_ref.shape[1]
    heads = weight_ref.shape[0]
    parts, depth, half = keep_ref.shape
    lanes = out_ref.shape[2] - half
    start = 0
    for got_ref in (near_ref, far_ref):
        lane = slice(start, start + got_ref.shape[2])
        out_ref[:, :, lane] = (keep_ref[:, :, lane].astype(F32) + got_ref[...].astype(F32)).astype(BF16)
        start += got_ref.shape[2]
    rows = slot_rows(user_ref, day_ref, users, slots)
    grad = tn(rows, to_rows(grad_ref[...], width).astype(BF16))
    terms = (grad * centred_ref[...].astype(F32)).astype(BF16)
    reduce = one_hot(iota((heads, width), 1) // (width // heads) == iota((heads, width), 0))
    scores = (weight_ref[...] * nt(reduce, terms)).astype(BF16)
    scores = jnp.concatenate([scores.astype(F32), jnp.zeros((lanes - heads, scores.shape[1]), F32)], axis=0).astype(BF16)
    turned = jnp.transpose(nn(scores, events_ref[...]), (1, 0))
    out_ref[:, :, half:] = turned.reshape(parts, depth, lanes).astype(BF16)


def merge_kernel(cores, z_size, near, x_ref, out_ref):
    parts, depth, columns = x_ref.shape
    kept = columns - 128
    pairs = parts // (2 * z_size * cores)
    x = x_ref[...].astype(F32).reshape(pairs, 2, z_size, cores, depth, columns)
    total = jnp.sum(jnp.sum(x, axis=0), axis=1)
    pieces = []
    for core in range(cores):
        for lane in (slice(0, near), slice(near, kept)):
            pieces += [total[0, core, :, lane], total[1, core, :, lane]]
    pieces.append(jnp.sum(total[:, :, :, kept:], axis=(0, 1)))
    merged = jnp.concatenate(pieces, axis=1).astype(BF16)
    for i in range(out_ref.shape[0]):
        out_ref[i] = merged


def final_kernel(x_ref, weight_ref, score_ref):
    columns = weight_ref.shape[1]
    total = jnp.sum(x_ref[...].astype(F32), axis=0)
    weight_ref[...] = total[:, :columns]
    score_ref[...] = total[:, columns : columns + score_ref.shape[1]]


def call(kernel, outs, args, scalars=0, flops=0, moved=None, whole=(), held=(), out_whole=(), out_far=(), out_near=(), scratch=(), limit=24):
    vmem = pl.BlockSpec(memory_space=pltpu.VMEM)
    smem = pl.BlockSpec(memory_space=pltpu.SMEM)
    anywhere = pl.BlockSpec(memory_space=pltpu.HBM)
    specs = [smem if i < scalars else anywhere if i in whole else vmem for i in range(len(args))]
    if moved is None:
        moved = sum(a.size * a.dtype.itemsize for a in args) + sum(math.prod(s) * jnp.dtype(t).itemsize for s, t in outs)
    args = [pltpu.with_memory_space_constraint(a, pltpu.HBM) if i in whole + held else a for i, a in enumerate(args)]
    return pl.pallas_call(
        kernel,
        out_shape=[
            pltpu.HBM(s, t) if i in out_whole + out_far else pltpu.VMEM(s, t) if i in out_near else jax.ShapeDtypeStruct(s, t)
            for i, (s, t) in enumerate(outs)
        ],
        in_specs=specs,
        out_specs=[anywhere if i in out_whole else vmem for i in range(len(outs))],
        scratch_shapes=scratch,
        compiler_params=pltpu.CompilerParams(vmem_limit_bytes=limit * 2**20),
        cost_estimate=pl.CostEstimate(flops=flops, bytes_accessed=moved, transcendentals=0),
    )(*args)


def shards(sizes, events, event_user, event_day, score_weight, value_weight, qkv_weight, cotangent):
    groups, x_size, z_size, cores = sizes
    buckets = x_size * z_size * cores
    user_dev, days, width = cotangent.shape
    heads = score_weight.shape[1]
    day_dev = days // buckets
    users = user_dev * buckets
    slots = users * day_dev
    count = events.shape[0]
    rows = width // buckets
    half = 3 * width // 2
    loss_scale = 1.0 / math.sqrt(user_dev * buckets * groups * days)
    user_row = event_user.reshape(1, count)
    day_row = event_day.reshape(1, count)
    core = lax.axis_index("core").reshape(1)

    block = ((buckets, day_dev * width // 128, 128), BF16)
    summary, weight = call(
        functools.partial(pool_kernel, users, slots),
        [block, ((heads, count), F32)],
        (user_row, day_row, score_weight.T, events, value_weight),
        flops=2 * count * width * (width + slots),
        whole=(0, 1, 2, 3, 4),
        scratch=[
            pltpu.VMEM((1, count), jnp.int32),
            pltpu.VMEM((1, count), jnp.int32),
            pltpu.VMEM((heads, width), BF16),
            pltpu.VMEM((count, width), BF16),
            pltpu.VMEM((width, width), BF16),
            pltpu.SemaphoreType.DMA((5,)),
        ],
        limit=60,
    )
    by_user = lax.all_to_all(summary, DAY, split_axis=0, concat_axis=0, tiled=True)
    centred, qkv_held = call(
        functools.partial(centre_kernel, users, slots),
        [((count, width), BF16), (qkv_weight.shape, BF16)],
        (user_row, day_row, events, value_weight, summary, qkv_weight),
        flops=2 * count * width * (width + slots),
        whole=(5,),
        held=(2, 3),
        out_far=(0,),
        out_near=(1,),
        scratch=[pltpu.SemaphoreType.DMA],
    )
    grad_summary, mine, send = call(
        functools.partial(attention_kernel, heads, loss_scale),
        [block, ((days, width + half), BF16), ((days, width + half), BF16)],
        (core, by_user, cotangent.reshape(days, width), qkv_held),
        scalars=1,
        whole=(2,),
        flops=2 * days * width * (6 * width + 14 * days),
        out_whole=(1,),
        out_near=(2,),
        scratch=[pltpu.VMEM((days, width), BF16), pltpu.VMEM((days, width + half), BF16), pltpu.SemaphoreType.DMA((2,))],
    )
    grad_days = lax.all_to_all(grad_summary, DAY, split_axis=0, concat_axis=0, tiled=True)
    theirs = lax.ppermute(send, "core", [(i, cores - 1 - i) for i in range(cores)])
    x_row = lax.axis_index("x").reshape(1)
    near, far = width // 2, width // 4
    keep, send_near, send_far = call(
        functools.partial(outer_kernel, width),
        [((buckets, rows, columns), BF16) for columns in (near + far, near, far)],
        (x_row, mine, theirs),
        scalars=1,
        moved=0,
        held=(1,),
    )
    got_near = lax.ppermute(send_near, "x", [(i, i ^ 1) for i in range(x_size)])
    got_far = lax.ppermute(send_far, "x", [(i, (((i + 1) ^ 1) - 1) % x_size) for i in range(x_size)])
    (partial_sums,) = call(
        functools.partial(score_kernel, users, slots),
        [((buckets, rows, near + far + 128), BF16)],
        (user_row, day_row, events, centred, weight, grad_days, keep, got_near, got_far),
        flops=2 * count * width * (slots + 256),
    )
    gathered = lax.all_to_all(partial_sums, DAY, split_axis=0, concat_axis=0, tiled=True)
    (merged,) = call(
        functools.partial(merge_kernel, cores, z_size, near), [((groups, rows, 3 * width + 128), BF16)], (gathered,)
    )
    everyone = lax.all_to_all(merged, "rep", split_axis=0, concat_axis=0, tiled=True)
    return tuple(call(final_kernel, [((rows, 3 * width), F32), ((rows, heads), F32)], (everyone,)))


def solution(mesh):
    sizes = (8, 4, 8, 2)
    split = Mesh(mesh.devices.reshape(sizes), ("rep",) + DAY)
    whole = ("rep",) + DAY
    in_specs = (P(whole, None), P(whole), P(whole), P(), P(), P(), P(whole, None, None))
    out_specs = (P(DAY, None), P(DAY, None))
    return jax.shard_map(
        functools.partial(shards, sizes), mesh=split, in_specs=in_specs, out_specs=out_specs, check_vma=False
    )
```

```python
import functools
import math

import jax
import jax.numpy as jnp
from jax import lax
from jax.experimental import pallas as pl
from jax.experimental.pallas import tpu as pltpu
from jax.sharding import Mesh, PartitionSpec as P

DAY = ("x", "z", "core")
F32 = jnp.float32
BF16 = jnp.bfloat16
BF16_MAX = 3.3895313892515355e38


def iota(shape, dim):
    return lax.broadcasted_iota(jnp.int32, shape, dim)


def one_hot(condition):
    return jnp.where(condition, 1.0, 0.0).astype(BF16)


def dot(a, b, dims):
    return lax.dot_general(a, b, ((dims[0], dims[1]), ((), ())), preferred_element_type=F32)


def nn(a, b):
    return dot(a, b, ((1,), (0,)))


def nt(a, b):
    return dot(a, b, ((1,), (1,)))


def tn(a, b):
    return dot(a, b, ((0,), (0,)))


def split3(x):
    high = jnp.minimum(x, BF16_MAX).astype(BF16)
    rest = x - high.astype(F32)
    middle = rest.astype(BF16)
    low = (rest - middle.astype(F32)).astype(BF16)
    return jnp.concatenate([high.astype(F32), middle.astype(F32), low.astype(F32)], 0).astype(BF16)


def join3(x):
    n = x.shape[0] // 3
    return x[:n] + x[n : 2 * n] + x[2 * n :]


def slot_rows(user_ref, day_ref, users, slots):
    segment = user_ref[...] * (slots // users) + day_ref[...]
    return one_hot(iota((slots, segment.shape[1]), 0) == segment)


def to_rows(x, width):
    blocks, depth, lanes = x.shape
    parts = width // lanes
    x = x.astype(F32).reshape(blocks, parts, depth // parts, lanes)
    return jnp.concatenate([x[:, i].reshape(-1, lanes) for i in range(parts)], axis=1)


def to_blocks(x, blocks):
    parts = x.shape[1] // 128
    x = x.astype(F32)
    pieces = [x[:, i * 128 : (i + 1) * 128].reshape(blocks, -1, 128) for i in range(parts)]
    return jnp.concatenate(pieces, axis=1).astype(BF16)


def pool_kernel(users, slots, *refs):
    sources, (summary_ref, weight_ref), held, sems = refs[:5], refs[5:7], refs[7:12], refs[12]
    copies = [pltpu.make_async_copy(source, target, sems.at[i]) for i, (source, target) in enumerate(zip(sources, held))]
    for copy in copies:
        copy.start()
    user_ref, day_ref, score_ref, events_ref, value_ref = held
    heads, width = score_ref.shape
    expand = one_hot(iota((3 * heads, width), 1) // (width // heads) == iota((3 * heads, width), 0) % heads)
    copies[0].wait()
    copies[1].wait()
    rows = slot_rows(user_ref, day_ref, users, slots)
    copies[2].wait()
    copies[3].wait()
    exponent = jnp.exp(nt(score_ref[...], events_ref[...]))
    denominator = join3(nt(split3(exponent), rows))
    weight = exponent / join3(nn(split3(denominator), rows))
    weight_ref[...] = weight
    wide = tn(split3(weight), expand)
    copies[4].wait()
    weighted = (nn(events_ref[...], value_ref[...]) * wide).astype(BF16)
    summary_ref[...] = to_blocks(nn(rows, weighted), users)


def centre_kernel(users, slots, user_ref, day_ref, events_ref, value_ref, summary_ref, qkv_ref, out_ref, qkv_out, sem):
    copy = pltpu.make_async_copy(qkv_ref, qkv_out, sem)
    copy.start()
    rows = slot_rows(user_ref, day_ref, users, slots)
    pooled = to_rows(summary_ref[...], value_ref.shape[1]).astype(BF16)
    values = nn(events_ref[...], value_ref[...])
    out_ref[...] = (values - tn(rows, pooled)).astype(BF16)
    copy.wait()


def attention_kernel(heads, loss_scale, core_ref, x_ref, cot_ref, qkv_weight_ref, grad_ref, mine_ref, send_ref, cot_buf, sem):
    width = qkv_weight_ref.shape[0]
    days = cot_ref.shape[0]
    cot_copy = pltpu.make_async_copy(cot_ref, cot_buf, sem)
    cot_copy.start()
    buckets = x_ref.shape[0]
    size = width // heads
    causal = iota((days, days), 1) <= iota((days, days), 0)
    wide = to_rows(x_ref[...], width)
    inverse = lax.rsqrt(jnp.mean(wide * wide, axis=-1, keepdims=True) + 1e-06)
    normed = (wide * inverse).astype(BF16)
    mine_ref[:, :width] = normed
    send_ref[:, :width] = normed
    qkv = nn(normed, qkv_weight_ref[...]).astype(BF16)
    cot_copy.wait()
    cot = cot_buf[...]
    pair = 2 * size
    left = iota((days, pair), 1) < size
    zero = jnp.zeros((days, pair), BF16)
    root = 1.0 / math.sqrt(size)
    parts = ([], [], [])
    for start in range(0, width, pair):
        q, k, v = (qkv[:, i * width + start : i * width + start + pair] for i in range(3))
        c = cot[:, start : start + pair]
        held = ([], [], [], [], [])
        for half in range(2):
            mine = left if half == 0 else ~left
            q1, k1, v1, c1 = (jnp.where(mine, a, zero) for a in (q, k, v, c))
            exponent = jnp.where(causal, jnp.exp(nt(q, k1) * root), 0.0)
            total = jnp.sum(exponent, axis=-1, keepdims=True)
            guard = jnp.where(total > 1.0, 2.0**-64, 1.0)
            attention = (exponent * guard) * (1.0 / (total * guard))
            grad_probs = nt(c, v1) * loss_scale
            inner = jnp.sum(grad_probs * attention, axis=-1, keepdims=True)
            grad_logits = (attention * (grad_probs - inner) * root).astype(BF16)
            for group, item in zip(held, (grad_logits, attention.astype(BF16), q1, k1, c1)):
                group.append(item)
        logits_grad, probs, q2, k2, c2 = held
        parts[0].append(nn(jnp.concatenate(logits_grad, 1), jnp.concatenate(k2, 0)))
        parts[1].append(tn(jnp.concatenate(logits_grad, 0), jnp.concatenate(q2, 0)))
        parts[2].append(tn(jnp.concatenate(probs, 0), jnp.concatenate(c2, 0)) * loss_scale)
    grad_qkv = jnp.concatenate([a.astype(BF16) for part in parts for a in part], axis=1)
    half = 3 * width // 2
    first = core_ref[0] == 0
    mine_ref[:, width:] = jnp.where(first, grad_qkv[:, :half], grad_qkv[:, half:])
    send_ref[:, width:] = jnp.where(first, grad_qkv[:, half:], grad_qkv[:, :half])
    grad_normed = nt(grad_qkv, qkv_weight_ref[...])
    cubed = inverse * inverse * inverse
    grad = (
        cot.astype(F32) * loss_scale
        + inverse * grad_normed
        - wide * cubed * jnp.mean(grad_normed * wide, axis=-1, keepdims=True)
    )
    grad_ref[...] = to_blocks(grad, buckets)


def packed(total, quarter, lane):
    size = total.shape[0] // 2
    start = 4 * lane + quarter * (lane // 2)
    rest = total[:, start : start + lane // 2]
    return jnp.concatenate([total[:, quarter * lane : (quarter + 1) * lane], jnp.concatenate([rest[:size], rest[size:]], axis=1)], axis=0)


def outer_kernel(width, x_ref, mine_ref, theirs_ref, *out_refs):
    both = jnp.concatenate([mine_ref[...], theirs_ref[...]], axis=0)
    total = tn(both[:, :width], both[:, width:])
    quarters = [packed(total, i, out_refs[0].shape[1]).astype(BF16) for i in range(4)]
    for here in range(4):

        @pl.when(x_ref[0] == here)
        def _():
            for step, out_ref in enumerate(out_refs):
                out_ref[...] = quarters[(here + step) % 4]


def score_kernel(users, slots, user_ref, day_ref, events_ref, centred_ref, weight_ref, grad_ref, out_ref):
    width = events_ref.shape[1]
    heads = weight_ref.shape[0]
    lanes = out_ref.shape[1]
    rows = slot_rows(user_ref, day_ref, users, slots)
    grad = tn(rows, to_rows(grad_ref[...], width).astype(BF16))
    terms = (grad * centred_ref[...].astype(F32)).astype(BF16)
    reduce = one_hot(iota((lanes, width), 1) // (width // heads) == iota((lanes, width), 0) - lanes // 2)
    weight = weight_ref[...]
    blank = jnp.zeros((lanes // 2, weight.shape[1]), F32)
    weight = jnp.concatenate([blank, weight, blank[heads:]], axis=0)
    scores = (weight * nt(reduce, terms)).astype(BF16)
    out_ref[...] = jnp.transpose(nn(scores, events_ref[...]), (1, 0))


def join_kernel(score_ref, own_ref, a_ref, b_ref, c_ref, out_ref):
    width = score_ref.shape[0]
    parts, depth, _ = out_ref.shape
    total = own_ref[...].astype(F32) + a_ref[...].astype(F32) + b_ref[...].astype(F32) + c_ref[...].astype(F32)
    lanes = total.shape[1]
    size = lanes // 2
    out_ref[:, :, :lanes] = total[:width].reshape(parts, depth, lanes).astype(BF16)
    rest = total[width:]
    rest = jnp.concatenate([rest[:, :size], rest[:, size:]], axis=0)
    both = jnp.concatenate([rest, score_ref[:, size:]], axis=1)
    out_ref[:, :, lanes:] = both.reshape(parts, depth, lanes).astype(BF16)


def merge_kernel(cores, x_size, x_ref, out_ref):
    parts, depth, columns = x_ref.shape
    lanes = columns // 2
    x = x_ref[...].astype(F32).reshape(x_size, parts // (x_size * cores), cores, depth, columns)
    total = jnp.sum(x, axis=1)
    pieces = []
    for core in range(cores):
        pieces += [total[i, core, :, :lanes] for i in range(x_size)]
        pieces += [total[i, core, :, lanes : lanes + lanes // 2] for i in range(x_size)]
    score = jnp.sum(total[:, :, :, lanes + lanes // 2 :], axis=(0, 1))
    pieces += [score, jnp.zeros_like(score)]
    merged = jnp.concatenate(pieces, axis=1).astype(BF16)
    for i in range(out_ref.shape[0]):
        out_ref[i] = merged


def final_kernel(x_ref, weight_ref, score_ref):
    columns = weight_ref.shape[1]
    total = jnp.sum(x_ref[...].astype(F32), axis=0)
    weight_ref[...] = total[:, :columns]
    score_ref[...] = total[:, columns : columns + score_ref.shape[1]]


def call(kernel, outs, args, scalars=0, flops=0, moved=None, whole=(), held=(), out_whole=(), out_far=(), out_near=(), scratch=(), limit=24):
    vmem = pl.BlockSpec(memory_space=pltpu.VMEM)
    smem = pl.BlockSpec(memory_space=pltpu.SMEM)
    anywhere = pl.BlockSpec(memory_space=pltpu.HBM)
    specs = [smem if i < scalars else anywhere if i in whole else vmem for i in range(len(args))]
    if moved is None:
        moved = sum(a.size * a.dtype.itemsize for a in args) + sum(math.prod(s) * jnp.dtype(t).itemsize for s, t in outs)
    args = [pltpu.with_memory_space_constraint(a, pltpu.HBM) if i in whole + held else a for i, a in enumerate(args)]
    return pl.pallas_call(
        kernel,
        out_shape=[
            pltpu.HBM(s, t) if i in out_whole + out_far else pltpu.VMEM(s, t) if i in out_near else jax.ShapeDtypeStruct(s, t)
            for i, (s, t) in enumerate(outs)
        ],
        in_specs=specs,
        out_specs=[anywhere if i in out_whole else vmem for i in range(len(outs))],
        scratch_shapes=scratch,
        compiler_params=pltpu.CompilerParams(vmem_limit_bytes=limit * 2**20),
        cost_estimate=pl.CostEstimate(flops=flops, bytes_accessed=moved, transcendentals=0),
    )(*args)


def shards(sizes, events, event_user, event_day, score_weight, value_weight, qkv_weight, cotangent):
    groups, x_size, z_size, cores = sizes
    buckets = x_size * z_size * cores
    user_dev, days, width = cotangent.shape
    heads = score_weight.shape[1]
    day_dev = days // buckets
    users = user_dev * buckets
    slots = users * day_dev
    count = events.shape[0]
    rows = width // buckets
    half = 3 * width // 2
    loss_scale = 1.0 / math.sqrt(user_dev * buckets * groups * days)
    user_row = event_user.reshape(1, count)
    day_row = event_day.reshape(1, count)
    core = lax.axis_index("core").reshape(1)

    block = ((buckets, day_dev * width // 128, 128), BF16)
    summary, weight = call(
        functools.partial(pool_kernel, users, slots),
        [block, ((heads, count), F32)],
        (user_row, day_row, score_weight.T, events, value_weight),
        flops=2 * count * width * (width + slots),
        whole=(0, 1, 2, 3, 4),
        scratch=[
            pltpu.VMEM((1, count), jnp.int32),
            pltpu.VMEM((1, count), jnp.int32),
            pltpu.VMEM((heads, width), BF16),
            pltpu.VMEM((count, width), BF16),
            pltpu.VMEM((width, width), BF16),
            pltpu.SemaphoreType.DMA((5,)),
        ],
        limit=60,
    )
    by_user = lax.all_to_all(summary, DAY, split_axis=0, concat_axis=0, tiled=True)
    centred, qkv_held = call(
        functools.partial(centre_kernel, users, slots),
        [((count, width), BF16), (qkv_weight.shape, BF16)],
        (user_row, day_row, events, value_weight, summary, qkv_weight),
        flops=2 * count * width * (width + slots),
        whole=(5,),
        held=(2, 3),
        out_far=(0,),
        out_near=(1,),
        scratch=[pltpu.SemaphoreType.DMA],
    )
    grad_summary, mine, send = call(
        functools.partial(attention_kernel, heads, loss_scale),
        [block, ((days, width + half), BF16), ((days, width + half), BF16)],
        (core, by_user, cotangent.reshape(days, width), qkv_held),
        scalars=1,
        whole=(2,),
        flops=2 * days * width * (6 * width + 14 * days),
        out_near=(1, 2),
        scratch=[pltpu.VMEM((days, width), BF16), pltpu.SemaphoreType.DMA],
    )
    grad_days = lax.all_to_all(grad_summary, DAY, split_axis=0, concat_axis=0, tiled=True)
    theirs = lax.ppermute(send, "core", [(i, cores - 1 - i) for i in range(cores)])
    x_row = lax.axis_index("x").reshape(1)
    packs = call(
        functools.partial(outer_kernel, width),
        [((width + width // 2, 128), BF16)] * x_size,
        (x_row, mine, theirs),
        scalars=1,
        moved=0,
    )
    got = [lax.ppermute(packs[k], "x", [(i, (i + k) % x_size) for i in range(x_size)]) for k in (2, 1, 3)]
    (score,) = call(
        functools.partial(score_kernel, users, slots),
        [((width, 128), F32)],
        (user_row, day_row, events, centred, weight, grad_days),
        held=(2, 3),
        flops=2 * count * width * (slots + 256),
    )
    (partial_sums,) = call(join_kernel, [((buckets, rows, 256), BF16)], (score, packs[0], *got))
    gathered = lax.all_to_all(partial_sums, DAY, split_axis=0, concat_axis=0, tiled=True)
    (merged,) = call(functools.partial(merge_kernel, cores, x_size), [((groups, rows, 3 * width + 128), BF16)], (gathered,))
    everyone = lax.all_to_all(merged, "rep", split_axis=0, concat_axis=0, tiled=True)
    return tuple(call(final_kernel, [((rows, 3 * width), F32), ((rows, heads), F32)], (everyone,)))


def solution(mesh):
    sizes = (8, 4, 8, 2)
    split = Mesh(mesh.devices.reshape(sizes), ("rep",) + DAY)
    whole = ("rep",) + DAY
    in_specs = (P(whole, None), P(whole), P(whole), P(), P(), P(), P(whole, None, None))
    out_specs = (P(DAY, None), P(DAY, None))
    return jax.shard_map(
        functools.partial(shards, sizes), mesh=split, in_specs=in_specs, out_specs=out_specs, check_vma=False
    )
```

```python
import functools
import math

import jax
import jax.numpy as jnp
from jax import lax
from jax.experimental import pallas as pl
from jax.experimental.pallas import tpu as pltpu
from jax.sharding import Mesh, PartitionSpec as P

DAY = ("x", "z", "core")
F32 = jnp.float32
BF16 = jnp.bfloat16
BF16_MAX = 3.3895313892515355e38


def iota(shape, dim):
    return lax.broadcasted_iota(jnp.int32, shape, dim)


def one_hot(condition):
    return jnp.where(condition, 1.0, 0.0).astype(BF16)


def dot(a, b, dims):
    return lax.dot_general(a, b, ((dims[0], dims[1]), ((), ())), preferred_element_type=F32)


def nn(a, b):
    return dot(a, b, ((1,), (0,)))


def nt(a, b):
    return dot(a, b, ((1,), (1,)))


def tn(a, b):
    return dot(a, b, ((0,), (0,)))


def split3(x):
    high = jnp.minimum(x, BF16_MAX).astype(BF16)
    rest = x - high.astype(F32)
    middle = rest.astype(BF16)
    low = (rest - middle.astype(F32)).astype(BF16)
    return jnp.concatenate([high.astype(F32), middle.astype(F32), low.astype(F32)], 0).astype(BF16)


def join3(x):
    n = x.shape[0] // 3
    return x[:n] + x[n : 2 * n] + x[2 * n :]


def slot_rows(user_ref, day_ref, users, slots):
    segment = user_ref[...] * (slots // users) + day_ref[...]
    return one_hot(iota((slots, segment.shape[1]), 0) == segment)


def to_rows(x, width):
    blocks, depth, lanes = x.shape
    parts = width // lanes
    x = x.astype(F32).reshape(blocks, parts, depth // parts, lanes)
    return jnp.concatenate([x[:, i].reshape(-1, lanes) for i in range(parts)], axis=1)


def to_blocks(x, blocks):
    parts = x.shape[1] // 128
    x = x.astype(F32)
    pieces = [x[:, i * 128 : (i + 1) * 128].reshape(blocks, -1, 128) for i in range(parts)]
    return jnp.concatenate(pieces, axis=1).astype(BF16)


def pool_kernel(users, slots, *refs):
    sources, (summary_ref, weight_ref), held, sems = refs[:5], refs[5:7], refs[7:12], refs[12]
    copies = [pltpu.make_async_copy(source, target, sems.at[i]) for i, (source, target) in enumerate(zip(sources, held))]
    for copy in copies:
        copy.start()
    user_ref, day_ref, score_ref, events_ref, value_ref = held
    heads, width = score_ref.shape
    expand = one_hot(iota((3 * heads, width), 1) // (width // heads) == iota((3 * heads, width), 0) % heads)
    copies[0].wait()
    copies[1].wait()
    rows = slot_rows(user_ref, day_ref, users, slots)
    copies[2].wait()
    copies[3].wait()
    exponent = jnp.exp(nt(score_ref[...], events_ref[...]))
    denominator = join3(nt(split3(exponent), rows))
    weight = exponent / join3(nn(split3(denominator), rows))
    weight_ref[...] = weight
    wide = tn(split3(weight), expand)
    copies[4].wait()
    weighted = (nn(events_ref[...], value_ref[...]) * wide).astype(BF16)
    summary_ref[...] = to_blocks(nn(rows, weighted), users)


def centre_kernel(users, slots, user_ref, day_ref, events_ref, value_ref, summary_ref, qkv_ref, out_ref, qkv_out, sem):
    copy = pltpu.make_async_copy(qkv_ref, qkv_out, sem)
    copy.start()
    rows = slot_rows(user_ref, day_ref, users, slots)
    pooled = to_rows(summary_ref[...], value_ref.shape[1]).astype(BF16)
    values = nn(events_ref[...], value_ref[...])
    out_ref[...] = (values - tn(rows, pooled)).astype(BF16)
    copy.wait()


def attention_kernel(heads, loss_scale, core_ref, x_ref, cot_ref, qkv_weight_ref, grad_ref, mine_ref, send_ref, cot_buf, sem):
    width = qkv_weight_ref.shape[0]
    days = cot_ref.shape[0]
    cot_copy = pltpu.make_async_copy(cot_ref, cot_buf, sem)
    cot_copy.start()
    buckets = x_ref.shape[0]
    size = width // heads
    causal = iota((days, days), 1) <= iota((days, days), 0)
    wide = to_rows(x_ref[...], width)
    inverse = lax.rsqrt(jnp.mean(wide * wide, axis=-1, keepdims=True) + 1e-06)
    normed = (wide * inverse).astype(BF16)
    mine_ref[:, :width] = normed
    send_ref[:, :width] = normed
    qkv = nn(normed, qkv_weight_ref[...]).astype(BF16)
    cot_copy.wait()
    cot = cot_buf[...]
    pair = 2 * size
    left = iota((days, pair), 1) < size
    zero = jnp.zeros((days, pair), BF16)
    root = 1.0 / math.sqrt(size)
    parts = ([], [], [])
    for start in range(0, width, pair):
        q, k, v = (qkv[:, i * width + start : i * width + start + pair] for i in range(3))
        c = cot[:, start : start + pair]
        held = ([], [], [], [], [])
        for half in range(2):
            mine = left if half == 0 else ~left
            q1, k1, v1, c1 = (jnp.where(mine, a, zero) for a in (q, k, v, c))
            exponent = jnp.where(causal, jnp.exp(nt(q, k1) * root), 0.0)
            total = jnp.sum(exponent, axis=-1, keepdims=True)
            guard = jnp.where(total > 1.0, 2.0**-64, 1.0)
            attention = (exponent * guard) * (1.0 / (total * guard))
            grad_probs = nt(c, v1) * loss_scale
            inner = jnp.sum(grad_probs * attention, axis=-1, keepdims=True)
            grad_logits = (attention * (grad_probs - inner) * root).astype(BF16)
            for group, item in zip(held, (grad_logits, attention.astype(BF16), q1, k1, c1)):
                group.append(item)
        logits_grad, probs, q2, k2, c2 = held
        parts[0].append(nn(jnp.concatenate(logits_grad, 1), jnp.concatenate(k2, 0)))
        parts[1].append(tn(jnp.concatenate(logits_grad, 0), jnp.concatenate(q2, 0)))
        parts[2].append(tn(jnp.concatenate(probs, 0), jnp.concatenate(c2, 0)) * loss_scale)
    grad_qkv = jnp.concatenate([a.astype(BF16) for part in parts for a in part], axis=1)
    half = 3 * width // 2
    first = core_ref[0] == 0
    mine_ref[:, width:] = jnp.where(first, grad_qkv[:, :half], grad_qkv[:, half:])
    send_ref[:, width:] = jnp.where(first, grad_qkv[:, half:], grad_qkv[:, :half])
    grad_normed = nt(grad_qkv, qkv_weight_ref[...])
    cubed = inverse * inverse * inverse
    grad = (
        cot.astype(F32) * loss_scale
        + inverse * grad_normed
        - wide * cubed * jnp.mean(grad_normed * wide, axis=-1, keepdims=True)
    )
    grad_ref[...] = to_blocks(grad, buckets)


def outer_kernel(width, x_ref, mine_ref, theirs_ref, *out_refs):
    both = jnp.concatenate([mine_ref[...], theirs_ref[...]], axis=0)
    total = tn(both[:, :width], both[:, width:]).astype(BF16)
    count = len(out_refs)
    size = width // count
    for here in range(count):

        @pl.when(x_ref[0] == here)
        def _():
            for step, out_ref in enumerate(out_refs):
                start = (here + step) % count * size
                out_ref[...] = total[start : start + size]


def score_kernel(users, slots, user_ref, day_ref, events_ref, centred_ref, weight_ref, grad_ref, out_ref):
    width = events_ref.shape[1]
    planes, heads, lanes = out_ref.shape
    rows = slot_rows(user_ref, day_ref, users, slots)
    grad = tn(rows, to_rows(grad_ref[...], width).astype(BF16))
    terms = (grad * centred_ref[...].astype(F32)).astype(BF16)
    reduce = one_hot(iota((heads, width), 1) // (width // heads) == iota((heads, width), 0))
    scores = (weight_ref[...] * nt(reduce, terms)).astype(BF16)
    spread = nn(scores, events_ref[...])
    for i in range(planes):
        out_ref[i] = spread[:, i * lanes : (i + 1) * lanes].astype(BF16)


def join_kernel(score_ref, own_ref, a_ref, b_ref, c_ref, out_ref):
    parts, depth, columns = out_ref.shape
    lanes = score_ref.shape[2]
    total = own_ref[...].astype(F32) + a_ref[...].astype(F32) + b_ref[...].astype(F32) + c_ref[...].astype(F32)
    out_ref[:, :, : columns - lanes] = total.reshape(parts, depth, columns - lanes).astype(BF16)
    score = jnp.sum(score_ref[...].astype(F32), axis=0)
    blank = jnp.zeros((lanes - score.shape[0], lanes), F32)
    turned = jnp.transpose(jnp.concatenate([score, blank], axis=0), (1, 0))
    out_ref[:, :, columns - lanes :] = turned.reshape(parts, depth, lanes).astype(BF16)


def merge_kernel(cores, half, x_ref, out_ref):
    parts, depth, columns = x_ref.shape
    total = jnp.sum(x_ref[...].astype(F32).reshape(parts // cores, cores, depth, columns), axis=0)
    pieces = [total[core, :, :half] for core in range(cores)] + [jnp.sum(total[:, :, half:], axis=0)]
    merged = jnp.concatenate(pieces, axis=1).astype(BF16)
    for i in range(out_ref.shape[0]):
        out_ref[i] = merged


def final_kernel(x_ref, weight_ref, score_ref):
    columns = weight_ref.shape[1]
    total = jnp.sum(x_ref[...].astype(F32), axis=0)
    weight_ref[...] = total[:, :columns]
    score_ref[...] = total[:, columns : columns + score_ref.shape[1]]


def call(kernel, outs, args, scalars=0, flops=0, moved=None, whole=(), held=(), out_whole=(), out_far=(), out_near=(), scratch=(), limit=24):
    vmem = pl.BlockSpec(memory_space=pltpu.VMEM)
    smem = pl.BlockSpec(memory_space=pltpu.SMEM)
    anywhere = pl.BlockSpec(memory_space=pltpu.HBM)
    specs = [smem if i < scalars else anywhere if i in whole else vmem for i in range(len(args))]
    if moved is None:
        moved = sum(a.size * a.dtype.itemsize for a in args) + sum(math.prod(s) * jnp.dtype(t).itemsize for s, t in outs)
    args = [pltpu.with_memory_space_constraint(a, pltpu.HBM) if i in whole + held else a for i, a in enumerate(args)]
    return pl.pallas_call(
        kernel,
        out_shape=[
            pltpu.HBM(s, t) if i in out_whole + out_far else pltpu.VMEM(s, t) if i in out_near else jax.ShapeDtypeStruct(s, t)
            for i, (s, t) in enumerate(outs)
        ],
        in_specs=specs,
        out_specs=[anywhere if i in out_whole else vmem for i in range(len(outs))],
        scratch_shapes=scratch,
        compiler_params=pltpu.CompilerParams(vmem_limit_bytes=limit * 2**20),
        cost_estimate=pl.CostEstimate(flops=flops, bytes_accessed=moved, transcendentals=0),
    )(*args)


def shards(sizes, events, event_user, event_day, score_weight, value_weight, qkv_weight, cotangent):
    groups, x_size, z_size, cores = sizes
    buckets = x_size * z_size * cores
    user_dev, days, width = cotangent.shape
    heads = score_weight.shape[1]
    day_dev = days // buckets
    users = user_dev * buckets
    slots = users * day_dev
    count = events.shape[0]
    rows = width // buckets
    half = 3 * width // 2
    loss_scale = 1.0 / math.sqrt(user_dev * buckets * groups * days)
    user_row = event_user.reshape(1, count)
    day_row = event_day.reshape(1, count)
    core = lax.axis_index("core").reshape(1)

    block = ((buckets, day_dev * width // 128, 128), BF16)
    summary, weight = call(
        functools.partial(pool_kernel, users, slots),
        [block, ((heads, count), F32)],
        (user_row, day_row, score_weight.T, events, value_weight),
        flops=2 * count * width * (width + slots),
        whole=(0, 1, 2, 3, 4),
        scratch=[
            pltpu.VMEM((1, count), jnp.int32),
            pltpu.VMEM((1, count), jnp.int32),
            pltpu.VMEM((heads, width), BF16),
            pltpu.VMEM((count, width), BF16),
            pltpu.VMEM((width, width), BF16),
            pltpu.SemaphoreType.DMA((5,)),
        ],
        limit=60,
    )
    by_user = lax.all_to_all(summary, DAY, split_axis=0, concat_axis=0, tiled=True)
    centred, qkv_held = call(
        functools.partial(centre_kernel, users, slots),
        [((count, width), BF16), (qkv_weight.shape, BF16)],
        (user_row, day_row, events, value_weight, summary, qkv_weight),
        flops=2 * count * width * (width + slots),
        whole=(5,),
        held=(2, 3),
        out_far=(0,),
        out_near=(1,),
        scratch=[pltpu.SemaphoreType.DMA],
    )
    grad_summary, mine, send = call(
        functools.partial(attention_kernel, heads, loss_scale),
        [block, ((days, width + half), BF16), ((days, width + half), BF16)],
        (core, by_user, cotangent.reshape(days, width), qkv_held),
        scalars=1,
        whole=(2,),
        flops=2 * days * width * (6 * width + 14 * days),
        out_near=(1, 2),
        scratch=[pltpu.VMEM((days, width), BF16), pltpu.SemaphoreType.DMA],
    )
    grad_days = lax.all_to_all(grad_summary, DAY, split_axis=0, concat_axis=0, tiled=True)
    theirs = lax.ppermute(send, "core", [(i, cores - 1 - i) for i in range(cores)])
    x_row = lax.axis_index("x").reshape(1)
    plane = width // x_size
    packs = call(
        functools.partial(outer_kernel, width),
        [((plane, half), BF16)] * x_size,
        (x_row, mine, theirs),
        scalars=1,
        moved=0,
    )
    got = [lax.ppermute(packs[k], "x", [(i, (i + k) % x_size) for i in range(x_size)]) for k in (2, 1, 3)]
    (score,) = call(
        functools.partial(score_kernel, users, slots),
        [((x_size, heads, plane), BF16)],
        (user_row, day_row, events, centred, weight, grad_days),
        held=(2, 3),
        flops=2 * count * width * (slots + 256),
    )
    score_rows = lax.all_to_all(score, "x", split_axis=0, concat_axis=0, tiled=True)
    (partial_sums,) = call(
        join_kernel, [((z_size * cores, rows, half + plane), BF16)], (score_rows, packs[0], *got)
    )
    gathered = lax.all_to_all(partial_sums, ("z", "core"), split_axis=0, concat_axis=0, tiled=True)
    (merged,) = call(
        functools.partial(merge_kernel, cores, half), [((groups, rows, 3 * width + plane), BF16)], (gathered,)
    )
    everyone = lax.all_to_all(merged, "rep", split_axis=0, concat_axis=0, tiled=True)
    return tuple(call(final_kernel, [((rows, 3 * width), F32), ((rows, heads), F32)], (everyone,)))


def solution(mesh):
    sizes = (8, 4, 8, 2)
    split = Mesh(mesh.devices.reshape(sizes), ("rep",) + DAY)
    whole = ("rep",) + DAY
    in_specs = (P(whole, None), P(whole), P(whole), P(), P(), P(), P(whole, None, None))
    out_specs = (P(DAY, None), P(DAY, None))
    return jax.shard_map(
        functools.partial(shards, sizes), mesh=split, in_specs=in_specs, out_specs=out_specs, check_vma=False
    )
```

```python
import functools
import math

import jax
import jax.numpy as jnp
from jax import lax
from jax.experimental import pallas as pl
from jax.experimental.pallas import tpu as pltpu
from jax.sharding import Mesh, PartitionSpec as P

DAY = ("x", "z", "core")
F32 = jnp.float32
BF16 = jnp.bfloat16
BF16_MAX = 3.3895313892515355e38


def iota(shape, dim):
    return lax.broadcasted_iota(jnp.int32, shape, dim)


def one_hot(condition):
    return jnp.where(condition, 1.0, 0.0).astype(BF16)


def dot(a, b, dims):
    return lax.dot_general(a, b, ((dims[0], dims[1]), ((), ())), preferred_element_type=F32)


def nn(a, b):
    return dot(a, b, ((1,), (0,)))


def nt(a, b):
    return dot(a, b, ((1,), (1,)))


def tn(a, b):
    return dot(a, b, ((0,), (0,)))


def split3(x):
    high = jnp.minimum(x, BF16_MAX).astype(BF16)
    rest = x - high.astype(F32)
    middle = rest.astype(BF16)
    low = (rest - middle.astype(F32)).astype(BF16)
    return jnp.concatenate([high.astype(F32), middle.astype(F32), low.astype(F32)], 0).astype(BF16)


def join3(x):
    n = x.shape[0] // 3
    return x[:n] + x[n : 2 * n] + x[2 * n :]


def slot_rows(user_ref, day_ref, users, slots):
    segment = user_ref[...] * (slots // users) + day_ref[...]
    return one_hot(iota((slots, segment.shape[1]), 0) == segment)


def to_rows(x, width):
    blocks, depth, lanes = x.shape
    parts = width // lanes
    x = x.astype(F32).reshape(blocks, parts, depth // parts, lanes)
    return jnp.concatenate([x[:, i].reshape(-1, lanes) for i in range(parts)], axis=1)


def to_blocks(x, blocks):
    parts = x.shape[1] // 128
    x = x.astype(F32)
    pieces = [x[:, i * 128 : (i + 1) * 128].reshape(blocks, -1, 128) for i in range(parts)]
    return jnp.concatenate(pieces, axis=1).astype(BF16)


def pool_kernel(users, slots, *refs):
    sources, (summary_ref, weight_ref), held, sems = refs[:5], refs[5:7], refs[7:12], refs[12]
    copies = [pltpu.make_async_copy(source, target, sems.at[i]) for i, (source, target) in enumerate(zip(sources, held))]
    for copy in copies:
        copy.start()
    user_ref, day_ref, score_ref, events_ref, value_ref = held
    heads, width = score_ref.shape
    expand = one_hot(iota((3 * heads, width), 1) // (width // heads) == iota((3 * heads, width), 0) % heads)
    copies[0].wait()
    copies[1].wait()
    rows = slot_rows(user_ref, day_ref, users, slots)
    copies[2].wait()
    copies[3].wait()
    exponent = jnp.exp(nt(score_ref[...], events_ref[...]))
    denominator = join3(nt(split3(exponent), rows))
    weight = exponent / join3(nn(split3(denominator), rows))
    weight_ref[...] = weight
    wide = tn(split3(weight), expand)
    copies[4].wait()
    weighted = (nn(events_ref[...], value_ref[...]) * wide).astype(BF16)
    summary_ref[...] = to_blocks(nn(rows, weighted), users)


def centre_kernel(users, slots, user_ref, day_ref, events_ref, value_ref, summary_ref, qkv_ref, out_ref, qkv_out, sem):
    copy = pltpu.make_async_copy(qkv_ref, qkv_out, sem)
    copy.start()
    rows = slot_rows(user_ref, day_ref, users, slots)
    pooled = to_rows(summary_ref[...], value_ref.shape[1]).astype(BF16)
    values = nn(events_ref[...], value_ref[...])
    out_ref[...] = (values - tn(rows, pooled)).astype(BF16)
    copy.wait()


def attention_kernel(heads, loss_scale, core_ref, x_ref, cot_ref, qkv_weight_ref, grad_ref, mine_ref, send_ref, cot_buf, sem):
    width = qkv_weight_ref.shape[0]
    days = cot_ref.shape[0]
    cot_copy = pltpu.make_async_copy(cot_ref, cot_buf, sem)
    cot_copy.start()
    buckets = x_ref.shape[0]
    size = width // heads
    causal = iota((days, days), 1) <= iota((days, days), 0)
    wide = to_rows(x_ref[...], width)
    inverse = lax.rsqrt(jnp.mean(wide * wide, axis=-1, keepdims=True) + 1e-06)
    normed = (wide * inverse).astype(BF16)
    mine_ref[:, :width] = normed
    send_ref[:, :width] = normed
    qkv = nn(normed, qkv_weight_ref[...]).astype(BF16)
    cot_copy.wait()
    cot = cot_buf[...]
    pair = 2 * size
    left = iota((days, pair), 1) < size
    zero = jnp.zeros((days, pair), BF16)
    root = 1.0 / math.sqrt(size)
    parts = ([], [], [])
    for start in range(0, width, pair):
        q, k, v = (qkv[:, i * width + start : i * width + start + pair] for i in range(3))
        c = cot[:, start : start + pair]
        held = ([], [], [], [], [])
        for half in range(2):
            mine = left if half == 0 else ~left
            q1, k1, v1, c1 = (jnp.where(mine, a, zero) for a in (q, k, v, c))
            exponent = jnp.where(causal, jnp.exp(nt(q, k1) * root), 0.0)
            total = jnp.sum(exponent, axis=-1, keepdims=True)
            guard = jnp.where(total > 1.0, 2.0**-64, 1.0)
            attention = (exponent * guard) * (1.0 / (total * guard))
            grad_probs = nt(c, v1) * loss_scale
            inner = jnp.sum(grad_probs * attention, axis=-1, keepdims=True)
            grad_logits = (attention * (grad_probs - inner) * root).astype(BF16)
            for group, item in zip(held, (grad_logits, attention.astype(BF16), q1, k1, c1)):
                group.append(item)
        logits_grad, probs, q2, k2, c2 = held
        parts[0].append(nn(jnp.concatenate(logits_grad, 1), jnp.concatenate(k2, 0)))
        parts[1].append(tn(jnp.concatenate(logits_grad, 0), jnp.concatenate(q2, 0)))
        parts[2].append(tn(jnp.concatenate(probs, 0), jnp.concatenate(c2, 0)) * loss_scale)
    grad_qkv = jnp.concatenate([a.astype(BF16) for part in parts for a in part], axis=1)
    half = 3 * width // 2
    first = core_ref[0] == 0
    mine_ref[:, width:] = jnp.where(first, grad_qkv[:, :half], grad_qkv[:, half:])
    send_ref[:, width:] = jnp.where(first, grad_qkv[:, half:], grad_qkv[:, :half])
    grad_normed = nt(grad_qkv, qkv_weight_ref[...])
    cubed = inverse * inverse * inverse
    grad = (
        cot.astype(F32) * loss_scale
        + inverse * grad_normed
        - wide * cubed * jnp.mean(grad_normed * wide, axis=-1, keepdims=True)
    )
    grad_ref[...] = to_blocks(grad, buckets)


def packed(total, quarter, lane):
    size = total.shape[0] // 2
    start = 4 * lane + quarter * (lane // 2)
    rest = total[:, start : start + lane // 2]
    return jnp.concatenate([total[:, quarter * lane : (quarter + 1) * lane], jnp.concatenate([rest[:size], rest[size:]], axis=1)], axis=0)


def outer_kernel(width, place_ref, mine_ref, theirs_ref, *out_refs):
    both = jnp.concatenate([mine_ref[...], theirs_ref[...]], axis=0)
    total = tn(both[:, :width], both[:, width:])
    quarters = [packed(total, i, out_refs[0].shape[1]).astype(BF16) for i in range(4)]
    for here in range(4):

        @pl.when(place_ref[0] == here)
        def _():
            for step, out_ref in enumerate(out_refs):
                out_ref[...] = quarters[here ^ step]


def score_kernel(users, slots, user_ref, day_ref, events_ref, centred_ref, weight_ref, grad_ref, out_ref):
    width = events_ref.shape[1]
    heads = weight_ref.shape[0]
    lanes = out_ref.shape[1]
    rows = slot_rows(user_ref, day_ref, users, slots)
    grad = tn(rows, to_rows(grad_ref[...], width).astype(BF16))
    terms = (grad * centred_ref[...].astype(F32)).astype(BF16)
    reduce = one_hot(iota((lanes, width), 1) // (width // heads) == iota((lanes, width), 0) - lanes // 2)
    weight = weight_ref[...]
    blank = jnp.zeros((lanes // 2, weight.shape[1]), F32)
    weight = jnp.concatenate([blank, weight, blank[heads:]], axis=0)
    scores = (weight * nt(reduce, terms)).astype(BF16)
    out_ref[...] = jnp.transpose(nn(scores, events_ref[...]), (1, 0))


def join_kernel(score_ref, own_ref, a_ref, b_ref, c_ref, out_ref):
    width = score_ref.shape[0]
    parts, depth, _ = out_ref.shape
    total = own_ref[...].astype(F32) + a_ref[...].astype(F32) + b_ref[...].astype(F32) + c_ref[...].astype(F32)
    lanes = total.shape[1]
    size = lanes // 2
    out_ref[:, :, :lanes] = total[:width].reshape(parts, depth, lanes).astype(BF16)
    rest = total[width:]
    rest = jnp.concatenate([rest[:, :size], rest[:, size:]], axis=0)
    both = jnp.concatenate([rest, score_ref[:, size:]], axis=1)
    out_ref[:, :, lanes:] = both.reshape(parts, depth, lanes).astype(BF16)


def merge_kernel(cores, z_size, x_ref, out_ref):
    parts, depth, columns = x_ref.shape
    lanes = columns // 2
    x = x_ref[...].astype(F32).reshape(parts // (2 * z_size * cores), 2, z_size, cores, depth, columns)
    total = jnp.sum(jnp.sum(x, axis=0), axis=1)
    pieces = []
    for core in range(cores):
        pieces += [total[i, core, :, :lanes] for i in range(2)]
        pieces += [total[i, core, :, lanes : lanes + lanes // 2] for i in range(2)]
    score = jnp.sum(total[:, :, :, lanes + lanes // 2 :], axis=(0, 1))
    pieces += [score, jnp.zeros_like(score)]
    merged = jnp.concatenate(pieces, axis=1).astype(BF16)
    for i in range(out_ref.shape[0]):
        out_ref[i] = merged


def final_kernel(cores, x_ref, weight_ref, score_ref):
    groups, depth, columns = x_ref.shape
    total = jnp.sum(x_ref[...].astype(F32).reshape(groups // 2, 2, depth, columns), axis=0)
    half = weight_ref.shape[1] // cores
    held = half // 2
    near, far = 2 * half // 3, half // 3
    for core in range(cores):
        for side in range(2):
            start = core * half + side * (near // 2)
            weight_ref[:, start : start + near // 2] = total[side, :, core * held : core * held + near // 2]
            start = core * half + near + side * (far // 2)
            weight_ref[:, start : start + far // 2] = total[side, :, core * held + near // 2 : (core + 1) * held]
    score_ref[...] = jnp.sum(total, axis=0)[:, cores * held : cores * held + score_ref.shape[1]]


def call(kernel, outs, args, scalars=0, flops=0, moved=None, whole=(), held=(), out_whole=(), out_far=(), out_near=(), scratch=(), limit=24):
    vmem = pl.BlockSpec(memory_space=pltpu.VMEM)
    smem = pl.BlockSpec(memory_space=pltpu.SMEM)
    anywhere = pl.BlockSpec(memory_space=pltpu.HBM)
    specs = [smem if i < scalars else anywhere if i in whole else vmem for i in range(len(args))]
    if moved is None:
        moved = sum(a.size * a.dtype.itemsize for a in args) + sum(math.prod(s) * jnp.dtype(t).itemsize for s, t in outs)
    args = [pltpu.with_memory_space_constraint(a, pltpu.HBM) if i in whole + held else a for i, a in enumerate(args)]
    return pl.pallas_call(
        kernel,
        out_shape=[
            pltpu.HBM(s, t) if i in out_whole + out_far else pltpu.VMEM(s, t) if i in out_near else jax.ShapeDtypeStruct(s, t)
            for i, (s, t) in enumerate(outs)
        ],
        in_specs=specs,
        out_specs=[anywhere if i in out_whole else vmem for i in range(len(outs))],
        scratch_shapes=scratch,
        compiler_params=pltpu.CompilerParams(vmem_limit_bytes=limit * 2**20),
        cost_estimate=pl.CostEstimate(flops=flops, bytes_accessed=moved, transcendentals=0),
    )(*args)


def shards(sizes, events, event_user, event_day, score_weight, value_weight, qkv_weight, cotangent):
    groups, x_size, z_size, cores = sizes
    buckets = x_size * z_size * cores
    user_dev, days, width = cotangent.shape
    heads = score_weight.shape[1]
    day_dev = days // buckets
    users = user_dev * buckets
    slots = users * day_dev
    count = events.shape[0]
    rows = width // buckets
    half = 3 * width // 2
    loss_scale = 1.0 / math.sqrt(user_dev * buckets * groups * days)
    user_row = event_user.reshape(1, count)
    day_row = event_day.reshape(1, count)
    core = lax.axis_index("core").reshape(1)

    block = ((buckets, day_dev * width // 128, 128), BF16)
    summary, weight = call(
        functools.partial(pool_kernel, users, slots),
        [block, ((heads, count), F32)],
        (user_row, day_row, score_weight.T, events, value_weight),
        flops=2 * count * width * (width + slots),
        whole=(0, 1, 2, 3, 4),
        scratch=[
            pltpu.VMEM((1, count), jnp.int32),
            pltpu.VMEM((1, count), jnp.int32),
            pltpu.VMEM((heads, width), BF16),
            pltpu.VMEM((count, width), BF16),
            pltpu.VMEM((width, width), BF16),
            pltpu.SemaphoreType.DMA((5,)),
        ],
        limit=60,
    )
    by_user = lax.all_to_all(summary, DAY, split_axis=0, concat_axis=0, tiled=True)
    centred, qkv_held = call(
        functools.partial(centre_kernel, users, slots),
        [((count, width), BF16), (qkv_weight.shape, BF16)],
        (user_row, day_row, events, value_weight, summary, qkv_weight),
        flops=2 * count * width * (width + slots),
        whole=(5,),
        held=(2, 3),
        out_far=(0,),
        out_near=(1,),
        scratch=[pltpu.SemaphoreType.DMA],
    )
    grad_summary, mine, send = call(
        functools.partial(attention_kernel, heads, loss_scale),
        [block, ((days, width + half), BF16), ((days, width + half), BF16)],
        (core, by_user, cotangent.reshape(days, width), qkv_held),
        scalars=1,
        whole=(2,),
        flops=2 * days * width * (6 * width + 14 * days),
        out_near=(1, 2),
        scratch=[pltpu.VMEM((days, width), BF16), pltpu.SemaphoreType.DMA],
    )
    grad_days = lax.all_to_all(grad_summary, DAY, split_axis=0, concat_axis=0, tiled=True)
    theirs = lax.ppermute(send, "core", [(i, cores - 1 - i) for i in range(cores)])
    place = ((lax.axis_index("rep") & 1) * 2 + (lax.axis_index("x") & 1)).reshape(1)
    packs = call(
        functools.partial(outer_kernel, width),
        [((width + width // 2, 128), BF16)] * 4,
        (place, mine, theirs),
        scalars=1,
        moved=0,
    )
    square = [(i, (i // x_size ^ 1) * x_size + (i % x_size ^ 1)) for i in range(groups * x_size)]
    got = [
        lax.ppermute(packs[3], ("rep", "x"), square),
        lax.ppermute(packs[2], "rep", [(i, i ^ 1) for i in range(groups)]),
        lax.ppermute(packs[1], "x", [(i, i ^ 1) for i in range(x_size)]),
    ]
    (score,) = call(
        functools.partial(score_kernel, users, slots),
        [((width, 128), F32)],
        (user_row, day_row, events, centred, weight, grad_days),
        held=(2, 3),
        flops=2 * count * width * (slots + 256),
    )
    (partial_sums,) = call(join_kernel, [((buckets, rows, 256), BF16)], (score, packs[0], *got))
    gathered = lax.all_to_all(partial_sums, DAY, split_axis=0, concat_axis=0, tiled=True)
    (merged,) = call(
        functools.partial(merge_kernel, cores, z_size), [((groups, rows, half + 128), BF16)], (gathered,)
    )
    everyone = lax.all_to_all(merged, "rep", split_axis=0, concat_axis=0, tiled=True)
    return tuple(
        call(functools.partial(final_kernel, cores), [((rows, 3 * width), F32), ((rows, heads), F32)], (everyone,))
    )


def solution(mesh):
    sizes = (8, 4, 8, 2)
    split = Mesh(mesh.devices.reshape(sizes), ("rep",) + DAY)
    whole = ("rep",) + DAY
    in_specs = (P(whole, None), P(whole), P(whole), P(), P(), P(), P(whole, None, None))
    out_specs = (P(DAY, None), P(DAY, None))
    return jax.shard_map(
        functools.partial(shards, sizes), mesh=split, in_specs=in_specs, out_specs=out_specs, check_vma=False
    )
```

```python
import functools
import math

import jax
import jax.numpy as jnp
from jax import lax
from jax.experimental import pallas as pl
from jax.experimental.pallas import tpu as pltpu
from jax.sharding import Mesh, PartitionSpec as P

DAY = ("x", "z", "core")
F32 = jnp.float32
BF16 = jnp.bfloat16
BF16_MAX = 3.3895313892515355e38


def iota(shape, dim):
    return lax.broadcasted_iota(jnp.int32, shape, dim)


def one_hot(condition):
    return jnp.where(condition, 1.0, 0.0).astype(BF16)


def dot(a, b, dims):
    return lax.dot_general(a, b, ((dims[0], dims[1]), ((), ())), preferred_element_type=F32)


def nn(a, b):
    return dot(a, b, ((1,), (0,)))


def nt(a, b):
    return dot(a, b, ((1,), (1,)))


def tn(a, b):
    return dot(a, b, ((0,), (0,)))


def split3(x):
    high = jnp.minimum(x, BF16_MAX).astype(BF16)
    rest = x - high.astype(F32)
    middle = rest.astype(BF16)
    low = (rest - middle.astype(F32)).astype(BF16)
    return jnp.concatenate([high.astype(F32), middle.astype(F32), low.astype(F32)], 0).astype(BF16)


def join3(x):
    n = x.shape[0] // 3
    return x[:n] + x[n : 2 * n] + x[2 * n :]


def slot_rows(user_ref, day_ref, users, slots):
    segment = user_ref[...] * (slots // users) + day_ref[...]
    return one_hot(iota((slots, segment.shape[1]), 0) == segment)


def to_rows(x, width):
    blocks, depth, lanes = x.shape
    parts = width // lanes
    x = x.astype(F32).reshape(blocks, parts, depth // parts, lanes)
    return jnp.concatenate([x[:, i].reshape(-1, lanes) for i in range(parts)], axis=1)


def to_blocks(x, blocks):
    parts = x.shape[1] // 128
    x = x.astype(F32)
    pieces = [x[:, i * 128 : (i + 1) * 128].reshape(blocks, -1, 128) for i in range(parts)]
    return jnp.concatenate(pieces, axis=1).astype(BF16)


def pool_kernel(users, slots, *refs):
    sources, (summary_ref, weight_ref), held, sems = refs[:5], refs[5:7], refs[7:12], refs[12]
    copies = [pltpu.make_async_copy(source, target, sems.at[i]) for i, (source, target) in enumerate(zip(sources, held))]
    for copy in copies:
        copy.start()
    user_ref, day_ref, score_ref, events_ref, value_ref = held
    heads, width = score_ref.shape
    expand = one_hot(iota((3 * heads, width), 1) // (width // heads) == iota((3 * heads, width), 0) % heads)
    copies[0].wait()
    copies[1].wait()
    rows = slot_rows(user_ref, day_ref, users, slots)
    copies[2].wait()
    copies[3].wait()
    exponent = jnp.exp(nt(score_ref[...], events_ref[...]))
    denominator = join3(nt(split3(exponent), rows))
    weight = exponent / join3(nn(split3(denominator), rows))
    weight_ref[...] = weight
    wide = tn(split3(weight), expand)
    copies[4].wait()
    weighted = (nn(events_ref[...], value_ref[...]) * wide).astype(BF16)
    summary_ref[...] = to_blocks(nn(rows, weighted), users)


def centre_kernel(users, slots, user_ref, day_ref, events_ref, value_ref, summary_ref, qkv_ref, out_ref, qkv_out, sem):
    copy = pltpu.make_async_copy(qkv_ref, qkv_out, sem)
    copy.start()
    rows = slot_rows(user_ref, day_ref, users, slots)
    pooled = to_rows(summary_ref[...], value_ref.shape[1]).astype(BF16)
    values = nn(events_ref[...], value_ref[...])
    out_ref[...] = (values - tn(rows, pooled)).astype(BF16)
    copy.wait()


def attention_kernel(heads, loss_scale, core_ref, x_ref, cot_ref, qkv_weight_ref, grad_ref, mine_ref, send_ref, cot_buf, sem):
    width = qkv_weight_ref.shape[0]
    days = cot_ref.shape[0]
    cot_copy = pltpu.make_async_copy(cot_ref, cot_buf, sem)
    cot_copy.start()
    buckets = x_ref.shape[0]
    size = width // heads
    causal = iota((days, days), 1) <= iota((days, days), 0)
    wide = to_rows(x_ref[...], width)
    inverse = lax.rsqrt(jnp.mean(wide * wide, axis=-1, keepdims=True) + 1e-06)
    normed = (wide * inverse).astype(BF16)
    mine_ref[:, :width] = normed
    send_ref[:, :width] = normed
    qkv = nn(normed, qkv_weight_ref[...]).astype(BF16)
    cot_copy.wait()
    cot = cot_buf[...]
    pair = 2 * size
    left = iota((days, pair), 1) < size
    zero = jnp.zeros((days, pair), BF16)
    root = 1.0 / math.sqrt(size)
    parts = ([], [], [])
    for start in range(0, width, pair):
        q, k, v = (qkv[:, i * width + start : i * width + start + pair] for i in range(3))
        c = cot[:, start : start + pair]
        held = ([], [], [], [], [])
        for half in range(2):
            mine = left if half == 0 else ~left
            q1, k1, v1, c1 = (jnp.where(mine, a, zero) for a in (q, k, v, c))
            exponent = jnp.where(causal, jnp.exp(nt(q, k1) * root), 0.0)
            total = jnp.sum(exponent, axis=-1, keepdims=True)
            guard = jnp.where(total > 1.0, 2.0**-64, 1.0)
            attention = (exponent * guard) * (1.0 / (total * guard))
            grad_probs = nt(c, v1) * loss_scale
            inner = jnp.sum(grad_probs * attention, axis=-1, keepdims=True)
            grad_logits = (attention * (grad_probs - inner) * root).astype(BF16)
            for group, item in zip(held, (grad_logits, attention.astype(BF16), q1, k1, c1)):
                group.append(item)
        logits_grad, probs, q2, k2, c2 = held
        parts[0].append(nn(jnp.concatenate(logits_grad, 1), jnp.concatenate(k2, 0)))
        parts[1].append(tn(jnp.concatenate(logits_grad, 0), jnp.concatenate(q2, 0)))
        parts[2].append(tn(jnp.concatenate(probs, 0), jnp.concatenate(c2, 0)) * loss_scale)
    grad_qkv = jnp.concatenate([a.astype(BF16) for part in parts for a in part], axis=1)
    half = 3 * width // 2
    first = core_ref[0] == 0
    mine_ref[:, width:] = jnp.where(first, grad_qkv[:, :half], grad_qkv[:, half:])
    send_ref[:, width:] = jnp.where(first, grad_qkv[:, half:], grad_qkv[:, :half])
    grad_normed = nt(grad_qkv, qkv_weight_ref[...])
    cubed = inverse * inverse * inverse
    grad = (
        cot.astype(F32) * loss_scale
        + inverse * grad_normed
        - wide * cubed * jnp.mean(grad_normed * wide, axis=-1, keepdims=True)
    )
    grad_ref[...] = to_blocks(grad, buckets)


def packed(total, quarter, lane):
    size = total.shape[0] // 2
    start = 4 * lane + quarter * (lane // 2)
    rest = total[:, start : start + lane // 2]
    return jnp.concatenate([total[:, quarter * lane : (quarter + 1) * lane], jnp.concatenate([rest[:size], rest[size:]], axis=1)], axis=0)


def outer_kernel(width, place_ref, mine_ref, theirs_ref, *out_refs):
    both = jnp.concatenate([mine_ref[...], theirs_ref[...]], axis=0)
    total = tn(both[:, :width], both[:, width:])
    quarters = [packed(total, i, out_refs[0].shape[1]).astype(BF16) for i in range(4)]
    for here in range(4):

        @pl.when(place_ref[0] == here)
        def _():
            for step, out_ref in enumerate(out_refs):
                out_ref[...] = quarters[here ^ step]


def score_kernel(users, slots, user_ref, day_ref, events_ref, centred_ref, weight_ref, grad_ref, out_ref):
    width = events_ref.shape[1]
    heads = weight_ref.shape[0]
    lanes = out_ref.shape[1]
    rows = slot_rows(user_ref, day_ref, users, slots)
    grad = tn(rows, to_rows(grad_ref[...], width).astype(BF16))
    terms = (grad * centred_ref[...].astype(F32)).astype(BF16)
    reduce = one_hot(iota((lanes, width), 1) // (width // heads) == iota((lanes, width), 0) - lanes // 2)
    weight = weight_ref[...]
    blank = jnp.zeros((lanes // 2, weight.shape[1]), F32)
    weight = jnp.concatenate([blank, weight, blank[heads:]], axis=0)
    scores = (weight * nt(reduce, terms)).astype(BF16)
    out_ref[...] = jnp.transpose(nn(scores, events_ref[...]), (1, 0))


def join_kernel(score_ref, own_ref, a_ref, b_ref, c_ref, out_ref):
    width = score_ref.shape[0]
    parts, depth, _ = out_ref.shape
    total = own_ref[...].astype(F32) + a_ref[...].astype(F32) + b_ref[...].astype(F32) + c_ref[...].astype(F32)
    lanes = total.shape[1]
    size = lanes // 2
    out_ref[:, :, :lanes] = total[:width].reshape(parts, depth, lanes).astype(BF16)
    rest = total[width:]
    rest = jnp.concatenate([rest[:, :size], rest[:, size:]], axis=0)
    both = jnp.concatenate([rest, score_ref[:, size:]], axis=1)
    out_ref[:, :, lanes:] = both.reshape(parts, depth, lanes).astype(BF16)


def merge_kernel(cores, z_size, x_ref, out_ref):
    parts, depth, columns = x_ref.shape
    lanes = columns // 2
    x = x_ref[...].astype(F32).reshape(parts // (2 * z_size * cores), 2, z_size, cores, depth, columns)
    total = jnp.sum(jnp.sum(x, axis=0), axis=1)
    pieces = []
    for core in range(cores):
        pieces += [total[i, core, :, :lanes] for i in range(2)]
        pieces += [total[i, core, :, lanes : lanes + lanes // 2] for i in range(2)]
    score = jnp.sum(total[:, :, :, lanes + lanes // 2 :], axis=(0, 1))
    pieces += [score, jnp.zeros_like(score)]
    merged = jnp.concatenate(pieces, axis=1).astype(BF16)
    for i in range(out_ref.shape[0]):
        out_ref[i] = merged


def final_kernel(cores, x_ref, weight_ref, score_ref):
    groups, depth, columns = x_ref.shape
    total = jnp.sum(x_ref[...].astype(F32).reshape(groups // 2, 2, depth, columns), axis=0)
    half = weight_ref.shape[1] // cores
    held = half // 2
    near, far = 2 * half // 3, half // 3
    for core in range(cores):
        for side in range(2):
            start = core * half + side * (near // 2)
            weight_ref[:, start : start + near // 2] = total[side, :, core * held : core * held + near // 2]
            start = core * half + near + side * (far // 2)
            weight_ref[:, start : start + far // 2] = total[side, :, core * held + near // 2 : (core + 1) * held]
    score_ref[...] = jnp.sum(total, axis=0)[:, cores * held : cores * held + score_ref.shape[1]]


def call(kernel, outs, args, scalars=0, flops=0, moved=None, whole=(), held=(), out_whole=(), out_far=(), out_near=(), scratch=(), limit=24):
    vmem = pl.BlockSpec(memory_space=pltpu.VMEM)
    smem = pl.BlockSpec(memory_space=pltpu.SMEM)
    anywhere = pl.BlockSpec(memory_space=pltpu.HBM)
    specs = [smem if i < scalars else anywhere if i in whole else vmem for i in range(len(args))]
    if moved is None:
        moved = sum(a.size * a.dtype.itemsize for a in args) + sum(math.prod(s) * jnp.dtype(t).itemsize for s, t in outs)
    args = [pltpu.with_memory_space_constraint(a, pltpu.HBM) if i in whole + held else a for i, a in enumerate(args)]
    return pl.pallas_call(
        kernel,
        out_shape=[
            pltpu.HBM(s, t) if i in out_whole + out_far else pltpu.VMEM(s, t) if i in out_near else jax.ShapeDtypeStruct(s, t)
            for i, (s, t) in enumerate(outs)
        ],
        in_specs=specs,
        out_specs=[anywhere if i in out_whole else vmem for i in range(len(outs))],
        scratch_shapes=scratch,
        compiler_params=pltpu.CompilerParams(vmem_limit_bytes=limit * 2**20),
        cost_estimate=pl.CostEstimate(flops=flops, bytes_accessed=moved, transcendentals=0),
    )(*args)


def shards(sizes, events, event_user, event_day, score_weight, value_weight, qkv_weight, cotangent):
    groups, x_size, z_size, cores = sizes
    buckets = x_size * z_size * cores
    user_dev, days, width = cotangent.shape
    heads = score_weight.shape[1]
    day_dev = days // buckets
    users = user_dev * buckets
    slots = users * day_dev
    count = events.shape[0]
    rows = width // buckets
    half = 3 * width // 2
    loss_scale = 1.0 / math.sqrt(user_dev * buckets * groups * days)
    user_row = event_user.reshape(1, count)
    day_row = event_day.reshape(1, count)
    core = lax.axis_index("core").reshape(1)

    block = ((buckets, day_dev * width // 128, 128), BF16)
    summary, weight = call(
        functools.partial(pool_kernel, users, slots),
        [block, ((heads, count), F32)],
        (user_row, day_row, score_weight.T, events, value_weight),
        flops=2 * count * width * (width + slots),
        whole=(0, 1, 2, 3, 4),
        scratch=[
            pltpu.VMEM((1, count), jnp.int32),
            pltpu.VMEM((1, count), jnp.int32),
            pltpu.VMEM((heads, width), BF16),
            pltpu.VMEM((count, width), BF16),
            pltpu.VMEM((width, width), BF16),
            pltpu.SemaphoreType.DMA((5,)),
        ],
        limit=60,
    )
    by_user = lax.all_to_all(summary, DAY, split_axis=0, concat_axis=0, tiled=True)
    centred, qkv_held = call(
        functools.partial(centre_kernel, users, slots),
        [((count, width), BF16), (qkv_weight.shape, BF16)],
        (user_row, day_row, events, value_weight, summary, qkv_weight),
        flops=2 * count * width * (width + slots),
        whole=(5,),
        held=(2, 3),
        out_far=(0,),
        out_near=(1,),
        scratch=[pltpu.SemaphoreType.DMA],
    )
    grad_summary, mine, send = call(
        functools.partial(attention_kernel, heads, loss_scale),
        [block, ((days, width + half), BF16), ((days, width + half), BF16)],
        (core, by_user, cotangent.reshape(days, width), qkv_held),
        scalars=1,
        whole=(2,),
        flops=2 * days * width * (6 * width + 14 * days),
        out_near=(1, 2),
        scratch=[pltpu.VMEM((days, width), BF16), pltpu.SemaphoreType.DMA],
    )
    grad_days = lax.all_to_all(grad_summary, DAY, split_axis=0, concat_axis=0, tiled=True)
    theirs = lax.ppermute(send, "core", [(i, cores - 1 - i) for i in range(cores)])
    place = ((lax.axis_index("rep") & 1) * 2 + (lax.axis_index("x") & 1)).reshape(1)
    packs = call(
        functools.partial(outer_kernel, width),
        [((width + width // 2, 128), BF16)] * 4,
        (place, mine, theirs),
        scalars=1,
        moved=0,
    )
    square = [(i, (i // x_size ^ 1) * x_size + (i % x_size ^ 1)) for i in range(groups * x_size)]
    got = [
        lax.ppermute(packs[3], ("rep", "x"), square),
        lax.ppermute(packs[2], "rep", [(i, (((i + 1) ^ 1) - 1) % groups) for i in range(groups)]),
        lax.ppermute(packs[1], "x", [(i, (((i + 1) ^ 1) - 1) % x_size) for i in range(x_size)]),
    ]
    (score,) = call(
        functools.partial(score_kernel, users, slots),
        [((width, 128), F32)],
        (user_row, day_row, events, centred, weight, grad_days),
        held=(2, 3),
        flops=2 * count * width * (slots + 256),
    )
    (partial_sums,) = call(join_kernel, [((buckets, rows, 256), BF16)], (score, packs[0], *got))
    gathered = lax.all_to_all(partial_sums, DAY, split_axis=0, concat_axis=0, tiled=True)
    (merged,) = call(
        functools.partial(merge_kernel, cores, z_size), [((groups, rows, half + 128), BF16)], (gathered,)
    )
    everyone = lax.all_to_all(merged, "rep", split_axis=0, concat_axis=0, tiled=True)
    return tuple(
        call(functools.partial(final_kernel, cores), [((rows, 3 * width), F32), ((rows, heads), F32)], (everyone,))
    )


def solution(mesh):
    sizes = (8, 4, 8, 2)
    split = Mesh(mesh.devices.reshape(sizes), ("rep",) + DAY)
    whole = ("rep",) + DAY
    in_specs = (P(whole, None), P(whole), P(whole), P(), P(), P(), P(whole, None, None))
    out_specs = (P(DAY, None), P(DAY, None))
    return jax.shard_map(
        functools.partial(shards, sizes), mesh=split, in_specs=in_specs, out_specs=out_specs, check_vma=False
    )
```

```python
import functools
import math

import jax
import jax.numpy as jnp
from jax import lax
from jax.experimental import pallas as pl
from jax.experimental.pallas import tpu as pltpu
from jax.sharding import Mesh, PartitionSpec as P

DAY = ("x", "z", "core")
F32 = jnp.float32
BF16 = jnp.bfloat16
BF16_MAX = 3.3895313892515355e38


def iota(shape, dim):
    return lax.broadcasted_iota(jnp.int32, shape, dim)


def one_hot(condition):
    return jnp.where(condition, 1.0, 0.0).astype(BF16)


def dot(a, b, dims):
    return lax.dot_general(a, b, ((dims[0], dims[1]), ((), ())), preferred_element_type=F32)


def nn(a, b):
    return dot(a, b, ((1,), (0,)))


def nt(a, b):
    return dot(a, b, ((1,), (1,)))


def tn(a, b):
    return dot(a, b, ((0,), (0,)))


def split3(x):
    high = jnp.minimum(x, BF16_MAX).astype(BF16)
    rest = x - high.astype(F32)
    middle = rest.astype(BF16)
    low = (rest - middle.astype(F32)).astype(BF16)
    return jnp.concatenate([high.astype(F32), middle.astype(F32), low.astype(F32)], 0).astype(BF16)


def join3(x):
    n = x.shape[0] // 3
    return x[:n] + x[n : 2 * n] + x[2 * n :]


def slot_rows(user_ref, day_ref, users, slots):
    segment = user_ref[...] * (slots // users) + day_ref[...]
    return one_hot(iota((slots, segment.shape[1]), 0) == segment)


def to_rows(x, width):
    blocks, depth, lanes = x.shape
    parts = width // lanes
    x = x.astype(F32).reshape(blocks, parts, depth // parts, lanes)
    return jnp.concatenate([x[:, i].reshape(-1, lanes) for i in range(parts)], axis=1)


def to_blocks(x, blocks):
    parts = x.shape[1] // 128
    x = x.astype(F32)
    pieces = [x[:, i * 128 : (i + 1) * 128].reshape(blocks, -1, 128) for i in range(parts)]
    return jnp.concatenate(pieces, axis=1).astype(BF16)


def pool_kernel(users, slots, *refs):
    sources, (summary_ref, weight_ref), held, sems = refs[:5], refs[5:7], refs[7:12], refs[12]
    copies = [pltpu.make_async_copy(source, target, sems.at[i]) for i, (source, target) in enumerate(zip(sources, held))]
    for copy in copies:
        copy.start()
    user_ref, day_ref, score_ref, events_ref, value_ref = held
    heads, width = score_ref.shape
    expand = one_hot(iota((3 * heads, width), 1) // (width // heads) == iota((3 * heads, width), 0) % heads)
    copies[0].wait()
    copies[1].wait()
    rows = slot_rows(user_ref, day_ref, users, slots)
    copies[2].wait()
    copies[3].wait()
    exponent = jnp.exp(nt(score_ref[...], events_ref[...]))
    denominator = join3(nt(split3(exponent), rows))
    weight = exponent / join3(nn(split3(denominator), rows))
    weight_ref[...] = weight
    wide = tn(split3(weight), expand)
    copies[4].wait()
    weighted = (nn(events_ref[...], value_ref[...]) * wide).astype(BF16)
    summary_ref[...] = to_blocks(nn(rows, weighted), users)


def centre_kernel(users, slots, user_ref, day_ref, events_ref, value_ref, summary_ref, qkv_ref, out_ref, qkv_out, sem):
    copy = pltpu.make_async_copy(qkv_ref, qkv_out, sem)
    copy.start()
    rows = slot_rows(user_ref, day_ref, users, slots)
    pooled = to_rows(summary_ref[...], value_ref.shape[1]).astype(BF16)
    values = nn(events_ref[...], value_ref[...])
    out_ref[...] = (values - tn(rows, pooled)).astype(BF16)
    copy.wait()


def attention_kernel(heads, loss_scale, core_ref, x_ref, cot_ref, qkv_weight_ref, grad_ref, mine_ref, send_ref, cot_buf, sem):
    width = qkv_weight_ref.shape[0]
    days = cot_ref.shape[0]
    cot_copy = pltpu.make_async_copy(cot_ref, cot_buf, sem)
    cot_copy.start()
    buckets = x_ref.shape[0]
    size = width // heads
    causal = iota((days, days), 0) <= iota((days, days), 1)
    wide = to_rows(x_ref[...], width)
    inverse = lax.rsqrt(jnp.mean(wide * wide, axis=-1, keepdims=True) + 1e-06)
    normed = (wide * inverse).astype(BF16)
    mine_ref[:, :width] = normed
    send_ref[:, :width] = normed
    qkv = nn(normed, qkv_weight_ref[...]).astype(BF16)
    pair = 2 * size
    left = iota((days, pair), 1) < size
    zero = jnp.zeros((days, pair), BF16)
    root = 1.0 / math.sqrt(size)
    parts = ([], [], [])
    starts = range(0, width, pair)
    rows = [[qkv[:, i * width + start : i * width + start + pair] for start in starts] for i in range(3)]
    halves = [(i, mine) for i in range(len(starts)) for mine in (left, ~left)]
    queries, keys, values = ([jnp.where(mine, a[i], zero) for i, mine in halves] for a in rows)
    logits = [nt(keys[n] * root, rows[0][i]) for n, (i, _) in enumerate(halves)]
    cot_copy.wait()
    cot = cot_buf[...]
    cots = [cot[:, start : start + pair] for start in starts]
    grad_probs = [nt(values[n], cots[i]) for n, (i, _) in enumerate(halves)]
    probs, logits_grad = [], []
    for n in range(len(halves)):
        exponent = jnp.where(causal, jnp.exp(logits[n]), 0.0)
        total = jnp.sum(exponent, axis=0, keepdims=True)
        guard = jnp.where(total > 1.0, 2.0**-64, 1.0)
        attention = (exponent * guard) * (1.0 / (total * guard))
        inner = jnp.sum(grad_probs[n] * attention, axis=0, keepdims=True)
        probs.append(attention.astype(BF16))
        logits_grad.append((attention * (grad_probs[n] - inner) * (loss_scale * root)).astype(BF16))
    for i, c in enumerate(cots):
        pick = slice(2 * i, 2 * i + 2)
        masked = [jnp.where(mine, c, zero) for mine in (left, ~left)]
        wide_grad = jnp.concatenate(logits_grad[pick], 1)
        parts[0].append(tn(jnp.concatenate(logits_grad[pick], 0), jnp.concatenate(keys[pick], 0)))
        parts[1].append(nn(wide_grad, jnp.concatenate(queries[pick], 0)))
        parts[2].append(nn(jnp.concatenate(probs[pick], 1), jnp.concatenate(masked, 0)) * loss_scale)
    grad_qkv = jnp.concatenate([a.astype(BF16) for part in parts for a in part], axis=1)
    half = 3 * width // 2
    first = core_ref[0] == 0
    mine_ref[:, width:] = jnp.where(first, grad_qkv[:, :half], grad_qkv[:, half:])
    send_ref[:, width:] = jnp.where(first, grad_qkv[:, half:], grad_qkv[:, :half])
    grad_normed = nt(grad_qkv, qkv_weight_ref[...])
    cubed = inverse * inverse * inverse
    grad = (
        cot.astype(F32) * loss_scale
        + inverse * grad_normed
        - wide * cubed * jnp.mean(grad_normed * wide, axis=-1, keepdims=True)
    )
    grad_ref[...] = to_blocks(grad, buckets)


def packed(total, quarter, lane):
    size = total.shape[0] // 2
    start = 4 * lane + quarter * (lane // 2)
    rest = total[:, start : start + lane // 2]
    return jnp.concatenate([total[:, quarter * lane : (quarter + 1) * lane], jnp.concatenate([rest[:size], rest[size:]], axis=1)], axis=0)


def outer_kernel(width, place_ref, mine_ref, theirs_ref, *out_refs):
    both = jnp.concatenate([mine_ref[...], theirs_ref[...]], axis=0)
    total = tn(both[:, :width], both[:, width:])
    quarters = [packed(total, i, out_refs[0].shape[1]).astype(BF16) for i in range(4)]
    for here in range(4):

        @pl.when(place_ref[0] == here)
        def _():
            for step, out_ref in enumerate(out_refs):
                out_ref[...] = quarters[here ^ step]


def score_kernel(users, slots, user_ref, day_ref, events_ref, centred_ref, weight_ref, grad_ref, out_ref):
    width = events_ref.shape[1]
    heads = weight_ref.shape[0]
    lanes = out_ref.shape[1]
    rows = slot_rows(user_ref, day_ref, users, slots)
    grad = tn(rows, to_rows(grad_ref[...], width).astype(BF16))
    terms = (grad * centred_ref[...].astype(F32)).astype(BF16)
    reduce = one_hot(iota((lanes, width), 1) // (width // heads) == iota((lanes, width), 0) - lanes // 2)
    weight = weight_ref[...]
    blank = jnp.zeros((lanes // 2, weight.shape[1]), F32)
    weight = jnp.concatenate([blank, weight, blank[heads:]], axis=0)
    scores = (weight * nt(reduce, terms)).astype(BF16)
    out_ref[...] = jnp.transpose(nn(scores, events_ref[...]), (1, 0))


def join_kernel(score_ref, own_ref, a_ref, b_ref, c_ref, out_ref):
    width = score_ref.shape[0]
    parts, depth, _ = out_ref.shape
    total = own_ref[...].astype(F32) + a_ref[...].astype(F32) + b_ref[...].astype(F32) + c_ref[...].astype(F32)
    lanes = total.shape[1]
    size = lanes // 2
    out_ref[:, :, :lanes] = total[:width].reshape(parts, depth, lanes).astype(BF16)
    rest = total[width:]
    rest = jnp.concatenate([rest[:, :size], rest[:, size:]], axis=0)
    both = jnp.concatenate([rest, score_ref[:, size:]], axis=1)
    out_ref[:, :, lanes:] = both.reshape(parts, depth, lanes).astype(BF16)


def merge_kernel(cores, z_size, x_ref, out_ref):
    parts, depth, columns = x_ref.shape
    lanes = columns // 2
    x = x_ref[...].astype(F32).reshape(parts // (2 * z_size * cores), 2, z_size, cores, depth, columns)
    total = jnp.sum(jnp.sum(x, axis=0), axis=1)
    pieces = []
    for core in range(cores):
        pieces += [total[i, core, :, :lanes] for i in range(2)]
        pieces += [total[i, core, :, lanes : lanes + lanes // 2] for i in range(2)]
    score = jnp.sum(total[:, :, :, lanes + lanes // 2 :], axis=(0, 1))
    pieces += [score, jnp.zeros_like(score)]
    merged = jnp.concatenate(pieces, axis=1).astype(BF16)
    for i in range(out_ref.shape[0]):
        out_ref[i] = merged


def final_kernel(cores, x_ref, weight_ref, score_ref):
    groups, depth, columns = x_ref.shape
    total = jnp.sum(x_ref[...].astype(F32).reshape(groups // 2, 2, depth, columns), axis=0)
    half = weight_ref.shape[1] // cores
    held = half // 2
    near, far = 2 * half // 3, half // 3
    for core in range(cores):
        for side in range(2):
            start = core * half + side * (near // 2)
            weight_ref[:, start : start + near // 2] = total[side, :, core * held : core * held + near // 2]
            start = core * half + near + side * (far // 2)
            weight_ref[:, start : start + far // 2] = total[side, :, core * held + near // 2 : (core + 1) * held]
    score_ref[...] = jnp.sum(total, axis=0)[:, cores * held : cores * held + score_ref.shape[1]]


def call(kernel, outs, args, scalars=0, flops=0, moved=None, whole=(), held=(), out_whole=(), out_far=(), out_near=(), scratch=(), limit=24):
    vmem = pl.BlockSpec(memory_space=pltpu.VMEM)
    smem = pl.BlockSpec(memory_space=pltpu.SMEM)
    anywhere = pl.BlockSpec(memory_space=pltpu.HBM)
    specs = [smem if i < scalars else anywhere if i in whole else vmem for i in range(len(args))]
    if moved is None:
        moved = sum(a.size * a.dtype.itemsize for a in args) + sum(math.prod(s) * jnp.dtype(t).itemsize for s, t in outs)
    args = [pltpu.with_memory_space_constraint(a, pltpu.HBM) if i in whole + held else a for i, a in enumerate(args)]
    return pl.pallas_call(
        kernel,
        out_shape=[
            pltpu.HBM(s, t) if i in out_whole + out_far else pltpu.VMEM(s, t) if i in out_near else jax.ShapeDtypeStruct(s, t)
            for i, (s, t) in enumerate(outs)
        ],
        in_specs=specs,
        out_specs=[anywhere if i in out_whole else vmem for i in range(len(outs))],
        scratch_shapes=scratch,
        compiler_params=pltpu.CompilerParams(vmem_limit_bytes=limit * 2**20),
        cost_estimate=pl.CostEstimate(flops=flops, bytes_accessed=moved, transcendentals=0),
    )(*args)


def shards(sizes, events, event_user, event_day, score_weight, value_weight, qkv_weight, cotangent):
    groups, x_size, z_size, cores = sizes
    buckets = x_size * z_size * cores
    user_dev, days, width = cotangent.shape
    heads = score_weight.shape[1]
    day_dev = days // buckets
    users = user_dev * buckets
    slots = users * day_dev
    count = events.shape[0]
    rows = width // buckets
    half = 3 * width // 2
    loss_scale = 1.0 / math.sqrt(user_dev * buckets * groups * days)
    user_row = event_user.reshape(1, count)
    day_row = event_day.reshape(1, count)
    core = lax.axis_index("core").reshape(1)

    block = ((buckets, day_dev * width // 128, 128), BF16)
    summary, weight = call(
        functools.partial(pool_kernel, users, slots),
        [block, ((heads, count), F32)],
        (user_row, day_row, score_weight.T, events, value_weight),
        flops=2 * count * width * (width + slots),
        whole=(0, 1, 2, 3, 4),
        scratch=[
            pltpu.VMEM((1, count), jnp.int32),
            pltpu.VMEM((1, count), jnp.int32),
            pltpu.VMEM((heads, width), BF16),
            pltpu.VMEM((count, width), BF16),
            pltpu.VMEM((width, width), BF16),
            pltpu.SemaphoreType.DMA((5,)),
        ],
        limit=60,
    )
    by_user = lax.all_to_all(summary, DAY, split_axis=0, concat_axis=0, tiled=True)
    centred, qkv_held = call(
        functools.partial(centre_kernel, users, slots),
        [((count, width), BF16), (qkv_weight.shape, BF16)],
        (user_row, day_row, events, value_weight, summary, qkv_weight),
        flops=2 * count * width * (width + slots),
        whole=(5,),
        held=(2, 3),
        out_far=(0,),
        out_near=(1,),
        scratch=[pltpu.SemaphoreType.DMA],
    )
    grad_summary, mine, send = call(
        functools.partial(attention_kernel, heads, loss_scale),
        [block, ((days, width + half), BF16), ((days, width + half), BF16)],
        (core, by_user, cotangent.reshape(days, width), qkv_held),
        scalars=1,
        whole=(2,),
        flops=2 * days * width * (6 * width + 14 * days),
        out_near=(1, 2),
        scratch=[pltpu.VMEM((days, width), BF16), pltpu.SemaphoreType.DMA],
    )
    grad_days = lax.all_to_all(grad_summary, DAY, split_axis=0, concat_axis=0, tiled=True)
    theirs = lax.ppermute(send, "core", [(i, cores - 1 - i) for i in range(cores)])
    place = ((lax.axis_index("rep") & 1) * 2 + (lax.axis_index("x") & 1)).reshape(1)
    packs = call(
        functools.partial(outer_kernel, width),
        [((width + width // 2, 128), BF16)] * 4,
        (place, mine, theirs),
        scalars=1,
        moved=0,
    )
    square = [(i, (i // x_size ^ 1) * x_size + (i % x_size ^ 1)) for i in range(groups * x_size)]
    got = [
        lax.ppermute(packs[3], ("rep", "x"), square),
        lax.ppermute(packs[2], "rep", [(i, (((i + 1) ^ 1) - 1) % groups) for i in range(groups)]),
        lax.ppermute(packs[1], "x", [(i, (((i + 1) ^ 1) - 1) % x_size) for i in range(x_size)]),
    ]
    (score,) = call(
        functools.partial(score_kernel, users, slots),
        [((width, 128), F32)],
        (user_row, day_row, events, centred, weight, grad_days),
        held=(2, 3),
        flops=2 * count * width * (slots + 256),
    )
    (partial_sums,) = call(join_kernel, [((buckets, rows, 256), BF16)], (score, packs[0], *got))
    gathered = lax.all_to_all(partial_sums, DAY, split_axis=0, concat_axis=0, tiled=True)
    (merged,) = call(
        functools.partial(merge_kernel, cores, z_size), [((groups, rows, half + 128), BF16)], (gathered,)
    )
    everyone = lax.all_to_all(merged, "rep", split_axis=0, concat_axis=0, tiled=True)
    return tuple(
        call(functools.partial(final_kernel, cores), [((rows, 3 * width), F32), ((rows, heads), F32)], (everyone,))
    )


def solution(mesh):
    sizes = (8, 4, 8, 2)
    split = Mesh(mesh.devices.reshape(sizes), ("rep",) + DAY)
    whole = ("rep",) + DAY
    in_specs = (P(whole, None), P(whole), P(whole), P(), P(), P(), P(whole, None, None))
    out_specs = (P(DAY, None), P(DAY, None))
    return jax.shard_map(
        functools.partial(shards, sizes), mesh=split, in_specs=in_specs, out_specs=out_specs, check_vma=False
    )
```

```python
import functools
import itertools
import math

import jax
import jax.numpy as jnp
from jax import lax
from jax.experimental import pallas as pl
from jax.experimental.pallas import tpu as pltpu
from jax.sharding import Mesh, PartitionSpec as P

DAY = ("x", "z", "core")
F32 = jnp.float32
BF16 = jnp.bfloat16
BF16_MAX = 3.3895313892515355e38


def iota(shape, dim):
    return lax.broadcasted_iota(jnp.int32, shape, dim)


def one_hot(condition):
    return jnp.where(condition, 1.0, 0.0).astype(BF16)


def dot(a, b, dims):
    return lax.dot_general(a, b, ((dims[0], dims[1]), ((), ())), preferred_element_type=F32)


def nn(a, b):
    return dot(a, b, ((1,), (0,)))


def nt(a, b):
    return dot(a, b, ((1,), (1,)))


def tn(a, b):
    return dot(a, b, ((0,), (0,)))


def split3(x):
    high = jnp.minimum(x, BF16_MAX).astype(BF16)
    rest = x - high.astype(F32)
    middle = rest.astype(BF16)
    low = (rest - middle.astype(F32)).astype(BF16)
    return jnp.concatenate([high.astype(F32), middle.astype(F32), low.astype(F32)], 0).astype(BF16)


def join3(x):
    n = x.shape[0] // 3
    return x[:n] + x[n : 2 * n] + x[2 * n :]


def slot_rows(user_ref, day_ref, users, slots):
    segment = user_ref[...] * (slots // users) + day_ref[...]
    return one_hot(iota((slots, segment.shape[1]), 0) == segment)


def to_rows(x, width):
    blocks, depth, lanes = x.shape
    parts = width // lanes
    x = x.astype(F32).reshape(blocks, parts, depth // parts, lanes)
    return jnp.concatenate([x[:, i].reshape(-1, lanes) for i in range(parts)], axis=1)


def to_blocks(x, blocks):
    parts = x.shape[1] // 128
    x = x.astype(F32)
    pieces = [x[:, i * 128 : (i + 1) * 128].reshape(blocks, -1, 128) for i in range(parts)]
    return jnp.concatenate(pieces, axis=1).astype(BF16)


def pool_kernel(users, slots, *refs):
    sources, (summary_ref, weight_ref), held, sems = refs[:5], refs[5:7], refs[7:12], refs[12]
    copies = [pltpu.make_async_copy(source, target, sems.at[i]) for i, (source, target) in enumerate(zip(sources, held))]
    for copy in copies:
        copy.start()
    user_ref, day_ref, score_ref, events_ref, value_ref = held
    heads, width = score_ref.shape
    expand = one_hot(iota((3 * heads, width), 1) // (width // heads) == iota((3 * heads, width), 0) % heads)
    copies[0].wait()
    copies[1].wait()
    rows = slot_rows(user_ref, day_ref, users, slots)
    copies[2].wait()
    copies[3].wait()
    exponent = jnp.exp(nt(score_ref[...], events_ref[...]))
    denominator = join3(nt(split3(exponent), rows))
    weight = exponent / join3(nn(split3(denominator), rows))
    weight_ref[...] = weight
    wide = tn(split3(weight), expand)
    copies[4].wait()
    weighted = (nn(events_ref[...], value_ref[...]) * wide).astype(BF16)
    summary_ref[...] = to_blocks(nn(rows, weighted), users)


def centre_kernel(users, slots, user_ref, day_ref, events_ref, value_ref, summary_ref, qkv_ref, out_ref, qkv_out, sem):
    copy = pltpu.make_async_copy(qkv_ref, qkv_out, sem)
    copy.start()
    rows = slot_rows(user_ref, day_ref, users, slots)
    pooled = to_rows(summary_ref[...], value_ref.shape[1]).astype(BF16)
    values = nn(events_ref[...], value_ref[...])
    out_ref[...] = (values - tn(rows, pooled)).astype(BF16)
    copy.wait()


def attention_kernel(heads, loss_scale, core_ref, x_ref, cot_ref, qkv_weight_ref, grad_ref, mine_ref, send_ref, cot_buf, sem):
    width = qkv_weight_ref.shape[0]
    days = cot_ref.shape[0]
    cot_copy = pltpu.make_async_copy(cot_ref, cot_buf, sem)
    cot_copy.start()
    buckets = x_ref.shape[0]
    size = width // heads
    causal = iota((days, days), 0) <= iota((days, days), 1)
    wide = to_rows(x_ref[...], width)
    inverse = lax.rsqrt(jnp.mean(wide * wide, axis=-1, keepdims=True) + 1e-06)
    normed = (wide * inverse).astype(BF16)
    mine_ref[:, :width] = normed
    send_ref[:, :width] = normed
    qkv = nn(normed, qkv_weight_ref[...]).astype(BF16)
    pair = 2 * size
    left = iota((days, pair), 1) < size
    zero = jnp.zeros((days, pair), BF16)
    root = 1.0 / math.sqrt(size)
    parts = ([], [], [])
    starts = range(0, width, pair)
    rows = [[qkv[:, i * width + start : i * width + start + pair] for start in starts] for i in range(3)]
    halves = [(i, mine) for i in range(len(starts)) for mine in (left, ~left)]
    queries, keys, values = ([jnp.where(mine, a[i], zero) for i, mine in halves] for a in rows)
    logits = [nt(keys[n] * root, rows[0][i]) for n, (i, _) in enumerate(halves)]
    cot_copy.wait()
    cot = cot_buf[...]
    cots = [cot[:, start : start + pair] for start in starts]
    grad_probs = [nt(values[n], cots[i]) for n, (i, _) in enumerate(halves)]
    probs, logits_grad = [], []
    for n in range(len(halves)):
        exponent = jnp.where(causal, jnp.exp(logits[n]), 0.0)
        total = jnp.sum(exponent, axis=0, keepdims=True)
        guard = jnp.where(total > 1.0, 2.0**-64, 1.0)
        attention = (exponent * guard) * (1.0 / (total * guard))
        inner = jnp.sum(grad_probs[n] * attention, axis=0, keepdims=True)
        probs.append(attention.astype(BF16))
        logits_grad.append((attention * (grad_probs[n] - inner) * (loss_scale * root)).astype(BF16))
    for i, c in enumerate(cots):
        pick = slice(2 * i, 2 * i + 2)
        masked = [jnp.where(mine, c, zero) for mine in (left, ~left)]
        wide_grad = jnp.concatenate(logits_grad[pick], 1)
        parts[0].append(tn(jnp.concatenate(logits_grad[pick], 0), jnp.concatenate(keys[pick], 0)))
        parts[1].append(nn(wide_grad, jnp.concatenate(queries[pick], 0)))
        parts[2].append(nn(jnp.concatenate(probs[pick], 1), jnp.concatenate(masked, 0)) * loss_scale)
    grad_qkv = jnp.concatenate([a.astype(BF16) for part in parts for a in part], axis=1)
    half = 3 * width // 2
    first = core_ref[0] == 0
    mine_ref[:, width:] = jnp.where(first, grad_qkv[:, :half], grad_qkv[:, half:])
    send_ref[:, width:] = jnp.where(first, grad_qkv[:, half:], grad_qkv[:, :half])
    grad_normed = nt(grad_qkv, qkv_weight_ref[...])
    cubed = inverse * inverse * inverse
    grad = (
        cot.astype(F32) * loss_scale
        + inverse * grad_normed
        - wide * cubed * jnp.mean(grad_normed * wide, axis=-1, keepdims=True)
    )
    grad_ref[...] = to_blocks(grad, buckets)


def packed(total, quarter, lane):
    size = total.shape[0] // 2
    start = 4 * lane + quarter * (lane // 2)
    rest = total[:, start : start + lane // 2]
    return jnp.concatenate([total[:, quarter * lane : (quarter + 1) * lane], jnp.concatenate([rest[:size], rest[size:]], axis=1)], axis=0)


def outer_kernel(width, place_ref, mine_ref, theirs_ref, *out_refs):
    both = jnp.concatenate([mine_ref[...], theirs_ref[...]], axis=0)
    total = tn(both[:, :width], both[:, width:])
    quarters = [packed(total, i, out_refs[0].shape[1]).astype(BF16) for i in range(4)]
    for here in range(4):

        @pl.when(place_ref[0] == here)
        def _():
            for step, out_ref in enumerate(out_refs):
                out_ref[...] = quarters[here ^ step]


def score_kernel(users, slots, user_ref, day_ref, events_ref, centred_ref, weight_ref, grad_ref, out_ref):
    width = events_ref.shape[1]
    heads = weight_ref.shape[0]
    lanes = out_ref.shape[1]
    rows = slot_rows(user_ref, day_ref, users, slots)
    grad = tn(rows, to_rows(grad_ref[...], width).astype(BF16))
    terms = (grad * centred_ref[...].astype(F32)).astype(BF16)
    reduce = one_hot(iota((lanes, width), 1) // (width // heads) == iota((lanes, width), 0) - lanes // 2)
    weight = weight_ref[...]
    blank = jnp.zeros((lanes // 2, weight.shape[1]), F32)
    weight = jnp.concatenate([blank, weight, blank[heads:]], axis=0)
    scores = (weight * nt(reduce, terms)).astype(BF16)
    out_ref[...] = jnp.transpose(nn(scores, events_ref[...]), (1, 0))


def join_kernel(score_ref, own_ref, a_ref, b_ref, c_ref, out_ref):
    width = score_ref.shape[0]
    parts, depth, _ = out_ref.shape
    total = own_ref[...].astype(F32) + a_ref[...].astype(F32) + b_ref[...].astype(F32) + c_ref[...].astype(F32)
    lanes = total.shape[1]
    size = lanes // 2
    out_ref[:, :, :lanes] = total[:width].reshape(parts, depth, lanes).astype(BF16)
    rest = total[width:]
    rest = jnp.concatenate([rest[:, :size], rest[:, size:]], axis=0)
    both = jnp.concatenate([rest, score_ref[:, size:]], axis=1)
    out_ref[:, :, lanes:] = both.reshape(parts, depth, lanes).astype(BF16)


def merge_kernel(cores, z_size, x_ref, out_ref):
    parts, depth, columns = x_ref.shape
    lanes = columns // 2
    x = x_ref[...].astype(F32).reshape(parts // (2 * z_size * cores), 2, z_size, cores, depth, columns)
    total = jnp.sum(jnp.sum(x, axis=0), axis=1)
    pieces = []
    for core in range(cores):
        pieces += [total[i, core, :, :lanes] for i in range(2)]
        pieces += [total[i, core, :, lanes : lanes + lanes // 2] for i in range(2)]
    score = jnp.sum(total[:, :, :, lanes + lanes // 2 :], axis=(0, 1))
    pieces += [score, jnp.zeros_like(score)]
    merged = jnp.concatenate(pieces, axis=1).astype(BF16)
    for i in range(out_ref.shape[0]):
        out_ref[i] = merged


def final_kernel(cores, x_ref, weight_ref, score_ref):
    groups, depth, columns = x_ref.shape
    total = jnp.sum(x_ref[...].astype(F32).reshape(groups // 2, 2, depth, columns), axis=0)
    half = weight_ref.shape[1] // cores
    held = half // 2
    near, far = 2 * half // 3, half // 3
    for core in range(cores):
        for side in range(2):
            start = core * half + side * (near // 2)
            weight_ref[:, start : start + near // 2] = total[side, :, core * held : core * held + near // 2]
            start = core * half + near + side * (far // 2)
            weight_ref[:, start : start + far // 2] = total[side, :, core * held + near // 2 : (core + 1) * held]
    score_ref[...] = jnp.sum(total, axis=0)[:, cores * held : cores * held + score_ref.shape[1]]


def call(kernel, outs, args, scalars=0, flops=0, moved=None, whole=(), held=(), out_whole=(), out_far=(), out_near=(), scratch=(), limit=24):
    vmem = pl.BlockSpec(memory_space=pltpu.VMEM)
    smem = pl.BlockSpec(memory_space=pltpu.SMEM)
    anywhere = pl.BlockSpec(memory_space=pltpu.HBM)
    specs = [smem if i < scalars else anywhere if i in whole else vmem for i in range(len(args))]
    if moved is None:
        moved = sum(a.size * a.dtype.itemsize for a in args) + sum(math.prod(s) * jnp.dtype(t).itemsize for s, t in outs)
    args = [pltpu.with_memory_space_constraint(a, pltpu.HBM) if i in whole + held else a for i, a in enumerate(args)]
    return pl.pallas_call(
        kernel,
        out_shape=[
            pltpu.HBM(s, t) if i in out_whole + out_far else pltpu.VMEM(s, t) if i in out_near else jax.ShapeDtypeStruct(s, t)
            for i, (s, t) in enumerate(outs)
        ],
        in_specs=specs,
        out_specs=[anywhere if i in out_whole else vmem for i in range(len(outs))],
        scratch_shapes=scratch,
        compiler_params=pltpu.CompilerParams(vmem_limit_bytes=limit * 2**20),
        cost_estimate=pl.CostEstimate(flops=flops, bytes_accessed=moved, transcendentals=0),
    )(*args)


def neighbours(sizes, far):
    pairs = []
    for place in itertools.product(*map(range, sizes)):
        skip = int(place[-1] == far)
        there = [((i + skip ^ 1) - skip) % n for i, n in zip(place[:-1], sizes)] + [place[-1]]
        flat = [0, 0]
        for i, j, n in zip(place, there, sizes):
            flat = [flat[0] * n + i, flat[1] * n + j]
        pairs.append(tuple(flat))
    return pairs


def shards(sizes, events, event_user, event_day, score_weight, value_weight, qkv_weight, cotangent):
    groups, x_size, z_size, cores = sizes
    buckets = x_size * z_size * cores
    user_dev, days, width = cotangent.shape
    heads = score_weight.shape[1]
    day_dev = days // buckets
    users = user_dev * buckets
    slots = users * day_dev
    count = events.shape[0]
    rows = width // buckets
    half = 3 * width // 2
    loss_scale = 1.0 / math.sqrt(user_dev * buckets * groups * days)
    user_row = event_user.reshape(1, count)
    day_row = event_day.reshape(1, count)
    core = lax.axis_index("core").reshape(1)

    block = ((buckets, day_dev * width // 128, 128), BF16)
    summary, weight = call(
        functools.partial(pool_kernel, users, slots),
        [block, ((heads, count), F32)],
        (user_row, day_row, score_weight.T, events, value_weight),
        flops=2 * count * width * (width + slots),
        whole=(0, 1, 2, 3, 4),
        scratch=[
            pltpu.VMEM((1, count), jnp.int32),
            pltpu.VMEM((1, count), jnp.int32),
            pltpu.VMEM((heads, width), BF16),
            pltpu.VMEM((count, width), BF16),
            pltpu.VMEM((width, width), BF16),
            pltpu.SemaphoreType.DMA((5,)),
        ],
        limit=60,
    )
    by_user = lax.all_to_all(summary, DAY, split_axis=0, concat_axis=0, tiled=True)
    centred, qkv_held = call(
        functools.partial(centre_kernel, users, slots),
        [((count, width), BF16), (qkv_weight.shape, BF16)],
        (user_row, day_row, events, value_weight, summary, qkv_weight),
        flops=2 * count * width * (width + slots),
        whole=(5,),
        held=(2, 3),
        out_far=(0,),
        out_near=(1,),
        scratch=[pltpu.SemaphoreType.DMA],
    )
    grad_summary, mine, send = call(
        functools.partial(attention_kernel, heads, loss_scale),
        [block, ((days, width + half), BF16), ((days, width + half), BF16)],
        (core, by_user, cotangent.reshape(days, width), qkv_held),
        scalars=1,
        whole=(2,),
        flops=2 * days * width * (6 * width + 14 * days),
        out_near=(1, 2),
        scratch=[pltpu.VMEM((days, width), BF16), pltpu.SemaphoreType.DMA],
    )
    grad_days = lax.all_to_all(grad_summary, DAY, split_axis=0, concat_axis=0, tiled=True)
    theirs = lax.ppermute(send, "core", [(i, cores - 1 - i) for i in range(cores)])
    place = ((lax.axis_index("rep") & 1) * 2 + (lax.axis_index("x") & 1)).reshape(1)
    packs = call(
        functools.partial(outer_kernel, width),
        [((width + width // 2, 128), BF16)] * 4,
        (place, mine, theirs),
        scalars=1,
        moved=0,
    )
    got = [
        lax.ppermute(packs[step], axes, neighbours(sizes_of, far))
        for step, axes, sizes_of, far in (
            (3, ("rep", "x", "core"), (groups, x_size, cores), 0),
            (1, ("x", "core"), (x_size, cores), 1),
            (2, ("rep", "core"), (groups, cores), 1),
        )
    ]
    (score,) = call(
        functools.partial(score_kernel, users, slots),
        [((width, 128), F32)],
        (user_row, day_row, events, centred, weight, grad_days),
        held=(2, 3),
        flops=2 * count * width * (slots + 256),
    )
    (partial_sums,) = call(join_kernel, [((buckets, rows, 256), BF16)], (score, packs[0], *got))
    gathered = lax.all_to_all(partial_sums, DAY, split_axis=0, concat_axis=0, tiled=True)
    (merged,) = call(
        functools.partial(merge_kernel, cores, z_size), [((groups, rows, half + 128), BF16)], (gathered,)
    )
    everyone = lax.all_to_all(merged, "rep", split_axis=0, concat_axis=0, tiled=True)
    return tuple(
        call(functools.partial(final_kernel, cores), [((rows, 3 * width), F32), ((rows, heads), F32)], (everyone,))
    )


def solution(mesh):
    sizes = (8, 4, 8, 2)
    split = Mesh(mesh.devices.reshape(sizes), ("rep",) + DAY)
    whole = ("rep",) + DAY
    in_specs = (P(whole, None), P(whole), P(whole), P(), P(), P(), P(whole, None, None))
    out_specs = (P(DAY, None), P(DAY, None))
    return jax.shard_map(
        functools.partial(shards, sizes), mesh=split, in_specs=in_specs, out_specs=out_specs, check_vma=False
    )
```

```python
import functools
import itertools
import math

import jax
import jax.numpy as jnp
from jax import lax
from jax.experimental import pallas as pl
from jax.experimental.pallas import tpu as pltpu
from jax.sharding import Mesh, PartitionSpec as P

DAY = ("x", "z", "core")
F32 = jnp.float32
BF16 = jnp.bfloat16
BF16_MAX = 3.3895313892515355e38


def iota(shape, dim):
    return lax.broadcasted_iota(jnp.int32, shape, dim)


def one_hot(condition):
    return jnp.where(condition, 1.0, 0.0).astype(BF16)


def dot(a, b, dims):
    return lax.dot_general(a, b, ((dims[0], dims[1]), ((), ())), preferred_element_type=F32)


def nn(a, b):
    return dot(a, b, ((1,), (0,)))


def nt(a, b):
    return dot(a, b, ((1,), (1,)))


def tn(a, b):
    return dot(a, b, ((0,), (0,)))


def split3(x):
    high = jnp.minimum(x, BF16_MAX).astype(BF16)
    rest = x - high.astype(F32)
    middle = rest.astype(BF16)
    low = (rest - middle.astype(F32)).astype(BF16)
    return jnp.concatenate([high.astype(F32), middle.astype(F32), low.astype(F32)], 0).astype(BF16)


def join3(x):
    n = x.shape[0] // 3
    return x[:n] + x[n : 2 * n] + x[2 * n :]


def slot_rows(user_ref, day_ref, users, slots):
    segment = user_ref[...] * (slots // users) + day_ref[...]
    return one_hot(iota((slots, segment.shape[1]), 0) == segment)


def to_rows(x, width):
    blocks, depth, lanes = x.shape
    parts = width // lanes
    x = x.astype(F32).reshape(blocks, parts, depth // parts, lanes)
    return jnp.concatenate([x[:, i].reshape(-1, lanes) for i in range(parts)], axis=1)


def to_blocks(x, blocks):
    parts = x.shape[1] // 128
    x = x.astype(F32)
    pieces = [x[:, i * 128 : (i + 1) * 128].reshape(blocks, -1, 128) for i in range(parts)]
    return jnp.concatenate(pieces, axis=1).astype(BF16)


def pool_kernel(users, slots, user_ref, day_ref, score_ref, events_ref, value_ref, summary_ref, weight_ref):
    heads, width = score_ref.shape
    expand = one_hot(iota((3 * heads, width), 1) // (width // heads) == iota((3 * heads, width), 0) % heads)
    rows = slot_rows(user_ref, day_ref, users, slots)
    exponent = jnp.exp(nt(score_ref[...], events_ref[...]))
    denominator = join3(nt(split3(exponent), rows))
    weight = exponent / join3(nn(split3(denominator), rows))
    weight_ref[...] = weight
    wide = tn(split3(weight), expand)
    weighted = (nn(events_ref[...], value_ref[...]) * wide).astype(BF16)
    summary_ref[...] = to_blocks(nn(rows, weighted), users)


def centre_kernel(users, slots, user_ref, day_ref, events_ref, value_ref, summary_ref, qkv_ref, out_ref, qkv_out, sem):
    copy = pltpu.make_async_copy(qkv_ref, qkv_out, sem)
    copy.start()
    rows = slot_rows(user_ref, day_ref, users, slots)
    pooled = to_rows(summary_ref[...], value_ref.shape[1]).astype(BF16)
    values = nn(events_ref[...], value_ref[...])
    out_ref[...] = (values - tn(rows, pooled)).astype(BF16)
    copy.wait()


def attention_kernel(heads, loss_scale, core_ref, x_ref, cot_ref, qkv_weight_ref, grad_ref, mine_ref, send_ref, cot_buf, sem):
    width = qkv_weight_ref.shape[0]
    days = cot_ref.shape[0]
    cot_copy = pltpu.make_async_copy(cot_ref, cot_buf, sem)
    cot_copy.start()
    buckets = x_ref.shape[0]
    size = width // heads
    causal = iota((days, days), 0) <= iota((days, days), 1)
    wide = to_rows(x_ref[...], width)
    inverse = lax.rsqrt(jnp.mean(wide * wide, axis=-1, keepdims=True) + 1e-06)
    normed = (wide * inverse).astype(BF16)
    mine_ref[:, :width] = normed
    send_ref[:, :width] = normed
    qkv = nn(normed, qkv_weight_ref[...]).astype(BF16)
    pair = 2 * size
    left = iota((days, pair), 1) < size
    zero = jnp.zeros((days, pair), BF16)
    root = 1.0 / math.sqrt(size)
    parts = ([], [], [])
    starts = range(0, width, pair)
    rows = [[qkv[:, i * width + start : i * width + start + pair] for start in starts] for i in range(3)]
    halves = [(i, mine) for i in range(len(starts)) for mine in (left, ~left)]
    queries, keys, values = ([jnp.where(mine, a[i], zero) for i, mine in halves] for a in rows)
    logits = [nt(keys[n] * root, rows[0][i]) for n, (i, _) in enumerate(halves)]
    cot_copy.wait()
    cot = cot_buf[...]
    cots = [cot[:, start : start + pair] for start in starts]
    grad_probs = [nt(values[n], cots[i]) for n, (i, _) in enumerate(halves)]
    probs, logits_grad = [], []
    for n in range(len(halves)):
        exponent = jnp.where(causal, jnp.exp(logits[n]), 0.0)
        total = jnp.sum(exponent, axis=0, keepdims=True)
        guard = jnp.where(total > 1.0, 2.0**-64, 1.0)
        attention = (exponent * guard) * (1.0 / (total * guard))
        inner = jnp.sum(grad_probs[n] * attention, axis=0, keepdims=True)
        probs.append(attention.astype(BF16))
        logits_grad.append((attention * (grad_probs[n] - inner) * (loss_scale * root)).astype(BF16))
    for i, c in enumerate(cots):
        pick = slice(2 * i, 2 * i + 2)
        masked = [jnp.where(mine, c, zero) for mine in (left, ~left)]
        wide_grad = jnp.concatenate(logits_grad[pick], 1)
        parts[0].append(tn(jnp.concatenate(logits_grad[pick], 0), jnp.concatenate(keys[pick], 0)))
        parts[1].append(nn(wide_grad, jnp.concatenate(queries[pick], 0)))
        parts[2].append(nn(jnp.concatenate(probs[pick], 1), jnp.concatenate(masked, 0)) * loss_scale)
    grad_qkv = jnp.concatenate([a.astype(BF16) for part in parts for a in part], axis=1)
    half = 3 * width // 2
    first = core_ref[0] == 0
    mine_ref[:, width:] = jnp.where(first, grad_qkv[:, :half], grad_qkv[:, half:])
    send_ref[:, width:] = jnp.where(first, grad_qkv[:, half:], grad_qkv[:, :half])
    grad_normed = nt(grad_qkv, qkv_weight_ref[...])
    cubed = inverse * inverse * inverse
    grad = (
        cot.astype(F32) * loss_scale
        + inverse * grad_normed
        - wide * cubed * jnp.mean(grad_normed * wide, axis=-1, keepdims=True)
    )
    grad_ref[...] = to_blocks(grad, buckets)


def packed(total, quarter, lane):
    size = total.shape[0] // 2
    start = 4 * lane + quarter * (lane // 2)
    rest = total[:, start : start + lane // 2]
    return jnp.concatenate([total[:, quarter * lane : (quarter + 1) * lane], jnp.concatenate([rest[:size], rest[size:]], axis=1)], axis=0)


def outer_kernel(width, place_ref, mine_ref, theirs_ref, *out_refs):
    both = jnp.concatenate([mine_ref[...], theirs_ref[...]], axis=0)
    total = tn(both[:, :width], both[:, width:])
    quarters = [packed(total, i, out_refs[0].shape[1]).astype(BF16) for i in range(4)]
    for here in range(4):

        @pl.when(place_ref[0] == here)
        def _():
            for step, out_ref in enumerate(out_refs):
                out_ref[...] = quarters[here ^ step]


def score_kernel(users, slots, user_ref, day_ref, events_ref, centred_ref, weight_ref, grad_ref, out_ref):
    width = events_ref.shape[1]
    heads = weight_ref.shape[0]
    lanes = out_ref.shape[1]
    rows = slot_rows(user_ref, day_ref, users, slots)
    grad = tn(rows, to_rows(grad_ref[...], width).astype(BF16))
    terms = (grad * centred_ref[...].astype(F32)).astype(BF16)
    reduce = one_hot(iota((lanes, width), 1) // (width // heads) == iota((lanes, width), 0) - lanes // 2)
    weight = weight_ref[...]
    blank = jnp.zeros((lanes // 2, weight.shape[1]), F32)
    weight = jnp.concatenate([blank, weight, blank[heads:]], axis=0)
    scores = (weight * nt(reduce, terms)).astype(BF16)
    out_ref[...] = jnp.transpose(nn(scores, events_ref[...]), (1, 0))


def join_kernel(score_ref, own_ref, a_ref, b_ref, c_ref, out_ref):
    width = score_ref.shape[0]
    parts, depth, _ = out_ref.shape
    total = own_ref[...].astype(F32) + a_ref[...].astype(F32) + b_ref[...].astype(F32) + c_ref[...].astype(F32)
    lanes = total.shape[1]
    size = lanes // 2
    out_ref[:, :, :lanes] = total[:width].reshape(parts, depth, lanes).astype(BF16)
    rest = total[width:]
    rest = jnp.concatenate([rest[:, :size], rest[:, size:]], axis=0)
    both = jnp.concatenate([rest, score_ref[:, size:]], axis=1)
    out_ref[:, :, lanes:] = both.reshape(parts, depth, lanes).astype(BF16)


def merge_kernel(cores, z_size, x_ref, out_ref):
    parts, depth, columns = x_ref.shape
    lanes = columns // 2
    x = x_ref[...].astype(F32).reshape(parts // (2 * z_size * cores), 2, z_size, cores, depth, columns)
    total = jnp.sum(jnp.sum(x, axis=0), axis=1)
    pieces = []
    for core in range(cores):
        pieces += [total[i, core, :, :lanes] for i in range(2)]
        pieces += [total[i, core, :, lanes : lanes + lanes // 2] for i in range(2)]
    score = jnp.sum(total[:, :, :, lanes + lanes // 2 :], axis=(0, 1))
    pieces += [score, jnp.zeros_like(score)]
    merged = jnp.concatenate(pieces, axis=1).astype(BF16)
    for i in range(out_ref.shape[0]):
        out_ref[i] = merged


def final_kernel(cores, x_ref, weight_ref, score_ref):
    groups, depth, columns = x_ref.shape
    total = jnp.sum(x_ref[...].astype(F32).reshape(groups // 2, 2, depth, columns), axis=0)
    half = weight_ref.shape[1] // cores
    held = half // 2
    near, far = 2 * half // 3, half // 3
    for core in range(cores):
        for side in range(2):
            start = core * half + side * (near // 2)
            weight_ref[:, start : start + near // 2] = total[side, :, core * held : core * held + near // 2]
            start = core * half + near + side * (far // 2)
            weight_ref[:, start : start + far // 2] = total[side, :, core * held + near // 2 : (core + 1) * held]
    score_ref[...] = jnp.sum(total, axis=0)[:, cores * held : cores * held + score_ref.shape[1]]


def call(kernel, outs, args, scalars=0, flops=0, moved=None, whole=(), held=(), out_whole=(), out_far=(), out_near=(), scratch=(), limit=24):
    vmem = pl.BlockSpec(memory_space=pltpu.VMEM)
    smem = pl.BlockSpec(memory_space=pltpu.SMEM)
    anywhere = pl.BlockSpec(memory_space=pltpu.HBM)
    specs = [smem if i < scalars else anywhere if i in whole else vmem for i in range(len(args))]
    if moved is None:
        moved = sum(a.size * a.dtype.itemsize for a in args) + sum(math.prod(s) * jnp.dtype(t).itemsize for s, t in outs)
    args = [pltpu.with_memory_space_constraint(a, pltpu.HBM) if i in whole + held else a for i, a in enumerate(args)]
    return pl.pallas_call(
        kernel,
        out_shape=[
            pltpu.HBM(s, t) if i in out_whole + out_far else pltpu.VMEM(s, t) if i in out_near else jax.ShapeDtypeStruct(s, t)
            for i, (s, t) in enumerate(outs)
        ],
        in_specs=specs,
        out_specs=[anywhere if i in out_whole else vmem for i in range(len(outs))],
        scratch_shapes=scratch,
        compiler_params=pltpu.CompilerParams(vmem_limit_bytes=limit * 2**20),
        cost_estimate=pl.CostEstimate(flops=flops, bytes_accessed=moved, transcendentals=0),
    )(*args)


def neighbours(sizes, far):
    pairs = []
    for place in itertools.product(*map(range, sizes)):
        skip = int(place[-1] == far)
        there = [((i + skip ^ 1) - skip) % n for i, n in zip(place[:-1], sizes)] + [place[-1]]
        flat = [0, 0]
        for i, j, n in zip(place, there, sizes):
            flat = [flat[0] * n + i, flat[1] * n + j]
        pairs.append(tuple(flat))
    return pairs


def shards(sizes, events, event_user, event_day, score_weight, value_weight, qkv_weight, cotangent):
    groups, x_size, z_size, cores = sizes
    buckets = x_size * z_size * cores
    user_dev, days, width = cotangent.shape
    heads = score_weight.shape[1]
    day_dev = days // buckets
    users = user_dev * buckets
    slots = users * day_dev
    count = events.shape[0]
    rows = width // buckets
    half = 3 * width // 2
    loss_scale = 1.0 / math.sqrt(user_dev * buckets * groups * days)
    user_row = event_user.reshape(1, count)
    day_row = event_day.reshape(1, count)
    core = lax.axis_index("core").reshape(1)

    block = ((buckets, day_dev * width // 128, 128), BF16)
    summary, weight = call(
        functools.partial(pool_kernel, users, slots),
        [block, ((heads, count), F32)],
        (user_row, day_row, score_weight.T, events, value_weight),
        flops=2 * count * width * (width + slots),
        held=(0, 1, 2, 3, 4),
    )
    by_user = lax.all_to_all(summary, DAY, split_axis=0, concat_axis=0, tiled=True)
    centred, qkv_held = call(
        functools.partial(centre_kernel, users, slots),
        [((count, width), BF16), (qkv_weight.shape, BF16)],
        (user_row, day_row, events, value_weight, summary, qkv_weight),
        flops=2 * count * width * (width + slots),
        whole=(5,),
        held=(2, 3),
        out_far=(0,),
        out_near=(1,),
        scratch=[pltpu.SemaphoreType.DMA],
    )
    grad_summary, mine, send = call(
        functools.partial(attention_kernel, heads, loss_scale),
        [block, ((days, width + half), BF16), ((days, width + half), BF16)],
        (core, by_user, cotangent.reshape(days, width), qkv_held),
        scalars=1,
        whole=(2,),
        flops=2 * days * width * (6 * width + 14 * days),
        out_near=(1, 2),
        scratch=[pltpu.VMEM((days, width), BF16), pltpu.SemaphoreType.DMA],
    )
    grad_days = lax.all_to_all(grad_summary, DAY, split_axis=0, concat_axis=0, tiled=True)
    theirs = lax.ppermute(send, "core", [(i, cores - 1 - i) for i in range(cores)])
    place = ((lax.axis_index("rep") & 1) * 2 + (lax.axis_index("x") & 1)).reshape(1)
    packs = call(
        functools.partial(outer_kernel, width),
        [((width + width // 2, 128), BF16)] * 4,
        (place, mine, theirs),
        scalars=1,
        moved=0,
    )
    got = [
        lax.ppermute(packs[step], axes, neighbours(sizes_of, far))
        for step, axes, sizes_of, far in (
            (3, ("rep", "x", "core"), (groups, x_size, cores), 0),
            (1, ("x", "core"), (x_size, cores), 1),
            (2, ("rep", "core"), (groups, cores), 1),
        )
    ]
    (score,) = call(
        functools.partial(score_kernel, users, slots),
        [((width, 128), F32)],
        (user_row, day_row, events, centred, weight, grad_days),
        held=(2, 3),
        flops=2 * count * width * (slots + 256),
    )
    (partial_sums,) = call(join_kernel, [((buckets, rows, 256), BF16)], (score, packs[0], *got))
    gathered = lax.all_to_all(partial_sums, DAY, split_axis=0, concat_axis=0, tiled=True)
    (merged,) = call(
        functools.partial(merge_kernel, cores, z_size), [((groups, rows, half + 128), BF16)], (gathered,)
    )
    everyone = lax.all_to_all(merged, "rep", split_axis=0, concat_axis=0, tiled=True)
    return tuple(
        call(functools.partial(final_kernel, cores), [((rows, 3 * width), F32), ((rows, heads), F32)], (everyone,))
    )


def solution(mesh):
    sizes = (8, 4, 8, 2)
    split = Mesh(mesh.devices.reshape(sizes), ("rep",) + DAY)
    whole = ("rep",) + DAY
    in_specs = (P(whole, None), P(whole), P(whole), P(), P(), P(), P(whole, None, None))
    out_specs = (P(DAY, None), P(DAY, None))
    return jax.shard_map(
        functools.partial(shards, sizes), mesh=split, in_specs=in_specs, out_specs=out_specs, check_vma=False
    )
```

```python
import functools
import itertools
import math

import jax
import jax.numpy as jnp
from jax import lax
from jax.experimental import pallas as pl
from jax.experimental.pallas import tpu as pltpu
from jax.sharding import Mesh, PartitionSpec as P

DAY = ("x", "z", "core")
F32 = jnp.float32
BF16 = jnp.bfloat16
BF16_MAX = 3.3895313892515355e38


def iota(shape, dim):
    return lax.broadcasted_iota(jnp.int32, shape, dim)


def one_hot(condition):
    return jnp.where(condition, 1.0, 0.0).astype(BF16)


def dot(a, b, dims):
    return lax.dot_general(a, b, ((dims[0], dims[1]), ((), ())), preferred_element_type=F32)


def nn(a, b):
    return dot(a, b, ((1,), (0,)))


def nt(a, b):
    return dot(a, b, ((1,), (1,)))


def tn(a, b):
    return dot(a, b, ((0,), (0,)))


def split3(x):
    high = jnp.minimum(x, BF16_MAX).astype(BF16)
    rest = x - high.astype(F32)
    middle = rest.astype(BF16)
    low = (rest - middle.astype(F32)).astype(BF16)
    return jnp.concatenate([high.astype(F32), middle.astype(F32), low.astype(F32)], 0).astype(BF16)


def join3(x):
    n = x.shape[0] // 3
    return x[:n] + x[n : 2 * n] + x[2 * n :]


def slot_rows(user_ref, day_ref, users, slots):
    segment = user_ref[...] * (slots // users) + day_ref[...]
    return one_hot(iota((slots, segment.shape[1]), 0) == segment)


def to_rows(x, width):
    blocks, depth, lanes = x.shape
    parts = width // lanes
    x = x.astype(F32).reshape(blocks, parts, depth // parts, lanes)
    return jnp.concatenate([x[:, i].reshape(-1, lanes) for i in range(parts)], axis=1)


def to_blocks(x, blocks):
    parts = x.shape[1] // 128
    x = x.astype(F32)
    pieces = [x[:, i * 128 : (i + 1) * 128].reshape(blocks, -1, 128) for i in range(parts)]
    return jnp.concatenate(pieces, axis=1).astype(BF16)


def pool_kernel(users, slots, user_ref, day_ref, score_ref, events_ref, value_ref, summary_ref, weight_ref):
    heads, width = score_ref.shape
    expand = one_hot(iota((3 * heads, width), 1) // (width // heads) == iota((3 * heads, width), 0) % heads)
    rows = slot_rows(user_ref, day_ref, users, slots)
    exponent = jnp.exp(nt(score_ref[...], events_ref[...]))
    denominator = join3(nt(split3(exponent), rows))
    weight = exponent / join3(nn(split3(denominator), rows))
    weight_ref[...] = weight
    wide = tn(split3(weight), expand)
    weighted = (nn(events_ref[...], value_ref[...]) * wide).astype(BF16)
    summary_ref[...] = to_blocks(nn(rows, weighted), users)


def centre_kernel(users, slots, user_ref, day_ref, events_ref, value_ref, summary_ref, qkv_ref, out_ref, qkv_out, sem):
    copy = pltpu.make_async_copy(qkv_ref, qkv_out, sem)
    copy.start()
    rows = slot_rows(user_ref, day_ref, users, slots)
    pooled = to_rows(summary_ref[...], value_ref.shape[1]).astype(BF16)
    values = nn(events_ref[...], value_ref[...])
    out_ref[...] = (values - tn(rows, pooled)).astype(BF16)
    copy.wait()


def attention_kernel(heads, loss_scale, core_ref, x_ref, cot_ref, qkv_weight_ref, grad_ref, mine_ref, send_ref, cot_buf, sem):
    width = qkv_weight_ref.shape[0]
    days = cot_ref.shape[0]
    cot_copy = pltpu.make_async_copy(cot_ref, cot_buf, sem)
    cot_copy.start()
    buckets = x_ref.shape[0]
    size = width // heads
    causal = iota((days, days), 0) <= iota((days, days), 1)
    wide = to_rows(x_ref[...], width)
    inverse = lax.rsqrt(jnp.mean(wide * wide, axis=-1, keepdims=True) + 1e-06)
    normed = (wide * inverse).astype(BF16)
    mine_ref[:, :width] = normed
    send_ref[:, :width] = normed
    qkv = nn(normed, qkv_weight_ref[...]).astype(BF16)
    pair = 2 * size
    left = iota((days, pair), 1) < size
    zero = jnp.zeros((days, pair), BF16)
    root = 1.0 / math.sqrt(size)
    parts = ([], [], [])
    starts = range(0, width, pair)
    rows = [[qkv[:, i * width + start : i * width + start + pair] for start in starts] for i in range(3)]
    halves = [(i, mine) for i in range(len(starts)) for mine in (left, ~left)]
    queries, keys, values = ([jnp.where(mine, a[i], zero) for i, mine in halves] for a in rows)
    logits = [nt(keys[n] * root, rows[0][i]) for n, (i, _) in enumerate(halves)]
    cot_copy.wait()
    cot = cot_buf[...]
    cots = [cot[:, start : start + pair] for start in starts]
    grad_probs = [nt(values[n], cots[i]) for n, (i, _) in enumerate(halves)]
    probs, logits_grad = [], []
    for n in range(len(halves)):
        exponent = jnp.where(causal, jnp.exp(logits[n]), 0.0)
        total = jnp.sum(exponent, axis=0, keepdims=True)
        guard = jnp.where(total > 1.0, 2.0**-64, 1.0)
        attention = (exponent * guard) * (1.0 / (total * guard))
        inner = jnp.sum(grad_probs[n] * attention, axis=0, keepdims=True)
        probs.append(attention.astype(BF16))
        logits_grad.append((attention * (grad_probs[n] - inner) * (loss_scale * root)).astype(BF16))
    for i, c in enumerate(cots):
        pick = slice(2 * i, 2 * i + 2)
        masked = [jnp.where(mine, c, zero) for mine in (left, ~left)]
        wide_grad = jnp.concatenate(logits_grad[pick], 1)
        parts[0].append(tn(jnp.concatenate(logits_grad[pick], 0), jnp.concatenate(keys[pick], 0)))
        parts[1].append(nn(wide_grad, jnp.concatenate(queries[pick], 0)))
        parts[2].append(nn(jnp.concatenate(probs[pick], 1), jnp.concatenate(masked, 0)) * loss_scale)
    grad_qkv = jnp.concatenate([a.astype(BF16) for part in parts for a in part], axis=1)
    half = 3 * width // 2
    first = core_ref[0] == 0
    mine_ref[:, width:] = jnp.where(first, grad_qkv[:, :half], grad_qkv[:, half:])
    send_ref[:, width:] = jnp.where(first, grad_qkv[:, half:], grad_qkv[:, :half])
    grad_normed = nt(grad_qkv, qkv_weight_ref[...])
    cubed = inverse * inverse * inverse
    grad = (
        cot.astype(F32) * loss_scale
        + inverse * grad_normed
        - wide * cubed * jnp.mean(grad_normed * wide, axis=-1, keepdims=True)
    )
    grad_ref[...] = to_blocks(grad, buckets)


def packed(total, quarter, lane):
    size = total.shape[0] // 2
    start = 4 * lane + quarter * (lane // 2)
    rest = total[:, start : start + lane // 2]
    return jnp.concatenate([total[:, quarter * lane : (quarter + 1) * lane], jnp.concatenate([rest[:size], rest[size:]], axis=1)], axis=0)


def outer_kernel(width, place_ref, mine_ref, theirs_ref, *out_refs):
    both = jnp.concatenate([mine_ref[...], theirs_ref[...]], axis=0)
    total = tn(both[:, :width], both[:, width:])
    quarters = [packed(total, i, out_refs[0].shape[1]).astype(BF16) for i in range(4)]
    for here in range(4):

        @pl.when(place_ref[0] == here)
        def _():
            for step, out_ref in enumerate(out_refs):
                out_ref[...] = quarters[here ^ step]


def score_kernel(users, slots, user_ref, day_ref, events_ref, centred_ref, weight_ref, grad_ref, out_ref):
    width = events_ref.shape[1]
    heads = weight_ref.shape[0]
    lanes = out_ref.shape[1]
    rows = slot_rows(user_ref, day_ref, users, slots)
    grad = tn(rows, to_rows(grad_ref[...], width).astype(BF16))
    terms = (grad * centred_ref[...].astype(F32)).astype(BF16)
    reduce = one_hot(iota((lanes, width), 1) // (width // heads) == iota((lanes, width), 0) - lanes // 2)
    weight = weight_ref[...]
    blank = jnp.zeros((lanes // 2, weight.shape[1]), F32)
    weight = jnp.concatenate([blank, weight, blank[heads:]], axis=0)
    scores = (weight * nt(reduce, terms)).astype(BF16)
    out_ref[...] = jnp.transpose(nn(scores, events_ref[...]), (1, 0))


def join_kernel(score_ref, own_ref, a_ref, b_ref, c_ref, out_ref):
    width = score_ref.shape[0]
    parts, depth, _ = out_ref.shape
    total = own_ref[...].astype(F32) + a_ref[...].astype(F32) + b_ref[...].astype(F32) + c_ref[...].astype(F32)
    lanes = total.shape[1]
    size = lanes // 2
    out_ref[:, :, :lanes] = total[:width].reshape(parts, depth, lanes).astype(BF16)
    rest = total[width:]
    rest = jnp.concatenate([rest[:, :size], rest[:, size:]], axis=0)
    both = jnp.concatenate([rest, score_ref[:, size:]], axis=1)
    out_ref[:, :, lanes:] = both.reshape(parts, depth, lanes).astype(BF16)


def merge_kernel(cores, z_size, x_ref, out_ref):
    parts, depth, columns = x_ref.shape
    lanes = columns // 2
    x = x_ref[...].astype(F32).reshape(parts // (2 * z_size * cores), 2, z_size, cores, depth, columns)
    total = jnp.sum(jnp.sum(x, axis=0), axis=1)
    pieces = []
    for core in range(cores):
        pieces += [total[i, core, :, :lanes] for i in range(2)]
        pieces += [total[i, core, :, lanes : lanes + lanes // 2] for i in range(2)]
    score = jnp.sum(total[:, :, :, lanes + lanes // 2 :], axis=(0, 1))
    pieces += [score, jnp.zeros_like(score)]
    merged = jnp.concatenate(pieces, axis=1).astype(BF16)
    for i in range(out_ref.shape[0]):
        out_ref[i] = merged


def final_kernel(cores, x_ref, weight_ref, score_ref):
    groups, depth, columns = x_ref.shape
    total = jnp.sum(x_ref[...].astype(F32).reshape(groups // 2, 2, depth, columns), axis=0)
    half = weight_ref.shape[1] // cores
    held = half // 2
    near, far = 2 * half // 3, half // 3
    for core in range(cores):
        for side in range(2):
            start = core * half + side * (near // 2)
            weight_ref[:, start : start + near // 2] = total[side, :, core * held : core * held + near // 2]
            start = core * half + near + side * (far // 2)
            weight_ref[:, start : start + far // 2] = total[side, :, core * held + near // 2 : (core + 1) * held]
    score_ref[...] = jnp.sum(total, axis=0)[:, cores * held : cores * held + score_ref.shape[1]]


def call(kernel, outs, args, scalars=0, flops=0, moved=None, whole=(), held=(), out_whole=(), out_far=(), out_near=(), scratch=(), limit=24):
    vmem = pl.BlockSpec(memory_space=pltpu.VMEM)
    smem = pl.BlockSpec(memory_space=pltpu.SMEM)
    anywhere = pl.BlockSpec(memory_space=pltpu.HBM)
    specs = [smem if i < scalars else anywhere if i in whole else vmem for i in range(len(args))]
    if moved is None:
        moved = sum(a.size * a.dtype.itemsize for a in args) + sum(math.prod(s) * jnp.dtype(t).itemsize for s, t in outs)
    args = [pltpu.with_memory_space_constraint(a, pltpu.HBM) if i in whole + held else a for i, a in enumerate(args)]
    return pl.pallas_call(
        kernel,
        out_shape=[
            pltpu.HBM(s, t) if i in out_whole + out_far else pltpu.VMEM(s, t) if i in out_near else jax.ShapeDtypeStruct(s, t)
            for i, (s, t) in enumerate(outs)
        ],
        in_specs=specs,
        out_specs=[anywhere if i in out_whole else vmem for i in range(len(outs))],
        scratch_shapes=scratch,
        compiler_params=pltpu.CompilerParams(vmem_limit_bytes=limit * 2**20),
        cost_estimate=pl.CostEstimate(flops=flops, bytes_accessed=moved, transcendentals=0),
    )(*args)


def neighbours(sizes, far):
    pairs = []
    for place in itertools.product(*map(range, sizes)):
        skip = int(place[-1] == far)
        there = [((i + skip ^ 1) - skip) % n for i, n in zip(place[:-1], sizes)] + [place[-1]]
        flat = [0, 0]
        for i, j, n in zip(place, there, sizes):
            flat = [flat[0] * n + i, flat[1] * n + j]
        pairs.append(tuple(flat))
    return pairs


def shards(sizes, events, event_user, event_day, score_weight, value_weight, qkv_weight, cotangent):
    groups, x_size, z_size, cores = sizes
    buckets = x_size * z_size * cores
    user_dev, days, width = cotangent.shape
    heads = score_weight.shape[1]
    day_dev = days // buckets
    users = user_dev * buckets
    slots = users * day_dev
    count = events.shape[0]
    rows = width // buckets
    half = 3 * width // 2
    loss_scale = 1.0 / math.sqrt(user_dev * buckets * groups * days)
    user_row = event_user.reshape(1, count)
    day_row = event_day.reshape(1, count)
    core = lax.axis_index("core").reshape(1)

    block = ((buckets, day_dev * width // 128, 128), BF16)
    summary, weight = call(
        functools.partial(pool_kernel, users, slots),
        [block, ((heads, count), F32)],
        (user_row, day_row, score_weight.T, events, value_weight),
        flops=2 * count * width * (width + slots),
        held=(0, 1, 2, 3, 4),
    )
    by_user = lax.all_to_all(summary, DAY, split_axis=0, concat_axis=0, tiled=True)
    centred, qkv_held = call(
        functools.partial(centre_kernel, users, slots),
        [((count, width), BF16), (qkv_weight.shape, BF16)],
        (user_row, day_row, events, value_weight, summary, qkv_weight),
        flops=2 * count * width * (width + slots),
        whole=(5,),
        held=(2, 3),
        out_far=(0,),
        out_near=(1,),
        scratch=[pltpu.SemaphoreType.DMA],
    )
    grad_summary, mine, send = call(
        functools.partial(attention_kernel, heads, loss_scale),
        [block, ((days, width + half), BF16), ((days, width + half), BF16)],
        (core, by_user, cotangent.reshape(days, width), qkv_held),
        scalars=1,
        whole=(2,),
        flops=2 * days * width * (6 * width + 14 * days),
        out_near=(1, 2),
        scratch=[pltpu.VMEM((days, width), BF16), pltpu.SemaphoreType.DMA],
    )
    grad_days = lax.all_to_all(grad_summary, DAY, split_axis=0, concat_axis=0, tiled=True)
    theirs = lax.ppermute(send, "core", [(i, cores - 1 - i) for i in range(cores)])
    place = ((lax.axis_index("rep") & 1) * 2 + (lax.axis_index("x") & 1)).reshape(1)
    packs = call(
        functools.partial(outer_kernel, width),
        [((width + width // 2, 128), BF16)] * 4,
        (place, mine, theirs),
        scalars=1,
        moved=0,
    )
    got = [
        lax.ppermute(packs[step], axes, neighbours(sizes_of, far))
        for step, axes, sizes_of, far in (
            (3, ("rep", "x", "core"), (groups, x_size, cores), 0),
            (2, ("rep", "core"), (groups, cores), 1),
            (1, ("x", "core"), (x_size, cores), 1),
        )
    ]
    (score,) = call(
        functools.partial(score_kernel, users, slots),
        [((width, 128), F32)],
        (user_row, day_row, events, centred, weight, grad_days),
        held=(2, 3),
        flops=2 * count * width * (slots + 256),
    )
    (partial_sums,) = call(join_kernel, [((buckets, rows, 256), BF16)], (score, packs[0], *got))
    gathered = lax.all_to_all(partial_sums, DAY, split_axis=0, concat_axis=0, tiled=True)
    (merged,) = call(
        functools.partial(merge_kernel, cores, z_size), [((groups, rows, half + 128), BF16)], (gathered,)
    )
    everyone = lax.all_to_all(merged, "rep", split_axis=0, concat_axis=0, tiled=True)
    return tuple(
        call(functools.partial(final_kernel, cores), [((rows, 3 * width), F32), ((rows, heads), F32)], (everyone,))
    )


def solution(mesh):
    sizes = (8, 4, 8, 2)
    split = Mesh(mesh.devices.reshape(sizes), ("rep",) + DAY)
    whole = ("rep",) + DAY
    in_specs = (P(whole, None), P(whole), P(whole), P(), P(), P(), P(whole, None, None))
    out_specs = (P(DAY, None), P(DAY, None))
    return jax.shard_map(
        functools.partial(shards, sizes), mesh=split, in_specs=in_specs, out_specs=out_specs, check_vma=False
    )
```

```python
import functools
import itertools
import math

import jax
import jax.numpy as jnp
from jax import lax
from jax.experimental import pallas as pl
from jax.experimental.pallas import tpu as pltpu
from jax.sharding import Mesh, PartitionSpec as P

DAY = ("x", "z", "core")
F32 = jnp.float32
BF16 = jnp.bfloat16
BF16_MAX = 3.3895313892515355e38


def iota(shape, dim):
    return lax.broadcasted_iota(jnp.int32, shape, dim)


def one_hot(condition):
    return jnp.where(condition, 1.0, 0.0).astype(BF16)


def dot(a, b, dims):
    return lax.dot_general(a, b, ((dims[0], dims[1]), ((), ())), preferred_element_type=F32)


def nn(a, b):
    return dot(a, b, ((1,), (0,)))


def nt(a, b):
    return dot(a, b, ((1,), (1,)))


def tn(a, b):
    return dot(a, b, ((0,), (0,)))


def split3(x):
    high = jnp.minimum(x, BF16_MAX).astype(BF16)
    rest = x - high.astype(F32)
    middle = rest.astype(BF16)
    low = (rest - middle.astype(F32)).astype(BF16)
    return jnp.concatenate([high.astype(F32), middle.astype(F32), low.astype(F32)], 0).astype(BF16)


def join3(x):
    n = x.shape[0] // 3
    return x[:n] + x[n : 2 * n] + x[2 * n :]


def slot_rows(user_ref, day_ref, users, slots):
    segment = user_ref[...] * (slots // users) + day_ref[...]
    return one_hot(iota((slots, segment.shape[1]), 0) == segment)


def to_rows(x, width):
    blocks, depth, lanes = x.shape
    parts = width // lanes
    x = x.astype(F32).reshape(blocks, parts, depth // parts, lanes)
    return jnp.concatenate([x[:, i].reshape(-1, lanes) for i in range(parts)], axis=1)


def to_blocks(x, blocks):
    parts = x.shape[1] // 128
    x = x.astype(F32)
    pieces = [x[:, i * 128 : (i + 1) * 128].reshape(blocks, -1, 128) for i in range(parts)]
    return jnp.concatenate(pieces, axis=1).astype(BF16)


def pool_kernel(users, slots, user_ref, day_ref, score_ref, events_ref, value_ref, summary_ref, weight_ref):
    heads, width = score_ref.shape
    expand = one_hot(iota((3 * heads, width), 1) // (width // heads) == iota((3 * heads, width), 0) % heads)
    rows = slot_rows(user_ref, day_ref, users, slots)
    values = nn(events_ref[...], value_ref[...])
    exponent = jnp.exp(nt(score_ref[...], events_ref[...]))
    denominator = join3(nt(split3(exponent), rows))
    weight = exponent / join3(nn(split3(denominator), rows))
    weight_ref[...] = weight
    weighted = (values * tn(split3(weight), expand)).astype(BF16)
    summary_ref[...] = to_blocks(nn(rows, weighted), users)


def centre_kernel(users, slots, user_ref, day_ref, events_ref, value_ref, summary_ref, qkv_ref, out_ref, qkv_out, sem):
    copy = pltpu.make_async_copy(qkv_ref, qkv_out, sem)
    copy.start()
    rows = slot_rows(user_ref, day_ref, users, slots)
    pooled = to_rows(summary_ref[...], value_ref.shape[1]).astype(BF16)
    values = nn(events_ref[...], value_ref[...])
    out_ref[...] = (values - tn(rows, pooled)).astype(BF16)
    copy.wait()


def attention_kernel(heads, loss_scale, core_ref, x_ref, cot_ref, qkv_weight_ref, grad_ref, mine_ref, send_ref, cot_buf, sem):
    width = qkv_weight_ref.shape[0]
    days = cot_ref.shape[0]
    cot_copy = pltpu.make_async_copy(cot_ref, cot_buf, sem)
    cot_copy.start()
    buckets = x_ref.shape[0]
    size = width // heads
    causal = iota((days, days), 0) <= iota((days, days), 1)
    wide = to_rows(x_ref[...], width)
    inverse = lax.rsqrt(jnp.mean(wide * wide, axis=-1, keepdims=True) + 1e-06)
    normed = (wide * inverse).astype(BF16)
    mine_ref[:, :width] = normed
    send_ref[:, :width] = normed
    qkv = nn(normed, qkv_weight_ref[...]).astype(BF16)
    pair = 2 * size
    left = iota((days, pair), 1) < size
    zero = jnp.zeros((days, pair), BF16)
    root = 1.0 / math.sqrt(size)
    parts = ([], [], [])
    starts = range(0, width, pair)
    rows = [[qkv[:, i * width + start : i * width + start + pair] for start in starts] for i in range(3)]
    halves = [(i, mine) for i in range(len(starts)) for mine in (left, ~left)]
    queries, keys, values = ([jnp.where(mine, a[i], zero) for i, mine in halves] for a in rows)
    logits = [nt(keys[n] * root, rows[0][i]) for n, (i, _) in enumerate(halves)]
    cot_copy.wait()
    cot = cot_buf[...]
    cots = [cot[:, start : start + pair] for start in starts]
    grad_probs = [nt(values[n], cots[i]) for n, (i, _) in enumerate(halves)]
    probs, logits_grad = [], []
    for n in range(len(halves)):
        exponent = jnp.where(causal, jnp.exp(logits[n]), 0.0)
        total = jnp.sum(exponent, axis=0, keepdims=True)
        guard = jnp.where(total > 1.0, 2.0**-64, 1.0)
        attention = (exponent * guard) * (1.0 / (total * guard))
        inner = jnp.sum(grad_probs[n] * attention, axis=0, keepdims=True)
        probs.append(attention.astype(BF16))
        logits_grad.append((attention * (grad_probs[n] - inner) * (loss_scale * root)).astype(BF16))
    for i, c in enumerate(cots):
        pick = slice(2 * i, 2 * i + 2)
        masked = [jnp.where(mine, c, zero) for mine in (left, ~left)]
        wide_grad = jnp.concatenate(logits_grad[pick], 1)
        parts[0].append(tn(jnp.concatenate(logits_grad[pick], 0), jnp.concatenate(keys[pick], 0)))
        parts[1].append(nn(wide_grad, jnp.concatenate(queries[pick], 0)))
        parts[2].append(nn(jnp.concatenate(probs[pick], 1), jnp.concatenate(masked, 0)) * loss_scale)
    grad_qkv = jnp.concatenate([a.astype(BF16) for part in parts for a in part], axis=1)
    half = 3 * width // 2
    first = core_ref[0] == 0
    mine_ref[:, width:] = jnp.where(first, grad_qkv[:, :half], grad_qkv[:, half:])
    send_ref[:, width:] = jnp.where(first, grad_qkv[:, half:], grad_qkv[:, :half])
    grad_normed = nt(grad_qkv, qkv_weight_ref[...])
    cubed = inverse * inverse * inverse
    grad = (
        cot.astype(F32) * loss_scale
        + inverse * grad_normed
        - wide * cubed * jnp.mean(grad_normed * wide, axis=-1, keepdims=True)
    )
    grad_ref[...] = to_blocks(grad, buckets)


def packed(total, quarter, lane):
    size = total.shape[0] // 2
    start = 4 * lane + quarter * (lane // 2)
    rest = total[:, start : start + lane // 2]
    return jnp.concatenate([total[:, quarter * lane : (quarter + 1) * lane], jnp.concatenate([rest[:size], rest[size:]], axis=1)], axis=0)


def outer_kernel(width, place_ref, mine_ref, theirs_ref, *out_refs):
    both = jnp.concatenate([mine_ref[...], theirs_ref[...]], axis=0)
    total = tn(both[:, :width], both[:, width:])
    quarters = [packed(total, i, out_refs[0].shape[1]).astype(BF16) for i in range(4)]
    for here in range(4):

        @pl.when(place_ref[0] == here)
        def _():
            for step, out_ref in enumerate(out_refs):
                out_ref[...] = quarters[here ^ step]


def score_kernel(users, slots, user_ref, day_ref, events_ref, centred_ref, weight_ref, grad_ref, out_ref):
    width = events_ref.shape[1]
    heads = weight_ref.shape[0]
    lanes = out_ref.shape[1]
    rows = slot_rows(user_ref, day_ref, users, slots)
    grad = tn(rows, to_rows(grad_ref[...], width).astype(BF16))
    terms = (grad * centred_ref[...].astype(F32)).astype(BF16)
    reduce = one_hot(iota((lanes, width), 1) // (width // heads) == iota((lanes, width), 0) - lanes // 2)
    weight = weight_ref[...]
    blank = jnp.zeros((lanes // 2, weight.shape[1]), F32)
    weight = jnp.concatenate([blank, weight, blank[heads:]], axis=0)
    scores = (weight * nt(reduce, terms)).astype(BF16)
    out_ref[...] = jnp.transpose(nn(scores, events_ref[...]), (1, 0))


def join_kernel(score_ref, own_ref, a_ref, b_ref, c_ref, out_ref):
    width = score_ref.shape[0]
    parts, depth, _ = out_ref.shape
    total = own_ref[...].astype(F32) + a_ref[...].astype(F32) + b_ref[...].astype(F32) + c_ref[...].astype(F32)
    lanes = total.shape[1]
    size = lanes // 2
    out_ref[:, :, :lanes] = total[:width].reshape(parts, depth, lanes).astype(BF16)
    rest = total[width:]
    rest = jnp.concatenate([rest[:, :size], rest[:, size:]], axis=0)
    both = jnp.concatenate([rest, score_ref[:, size:]], axis=1)
    out_ref[:, :, lanes:] = both.reshape(parts, depth, lanes).astype(BF16)


def merge_kernel(cores, z_size, x_ref, out_ref):
    parts, depth, columns = x_ref.shape
    lanes = columns // 2
    x = x_ref[...].astype(F32).reshape(parts // (2 * z_size * cores), 2, z_size, cores, depth, columns)
    total = jnp.sum(jnp.sum(x, axis=0), axis=1)
    pieces = []
    for core in range(cores):
        pieces += [total[i, core, :, :lanes] for i in range(2)]
        pieces += [total[i, core, :, lanes : lanes + lanes // 2] for i in range(2)]
    score = jnp.sum(total[:, :, :, lanes + lanes // 2 :], axis=(0, 1))
    pieces += [score, jnp.zeros_like(score)]
    merged = jnp.concatenate(pieces, axis=1).astype(BF16)
    for i in range(out_ref.shape[0]):
        out_ref[i] = merged


def final_kernel(cores, x_ref, weight_ref, score_ref):
    groups, depth, columns = x_ref.shape
    total = jnp.sum(x_ref[...].astype(F32).reshape(groups // 2, 2, depth, columns), axis=0)
    half = weight_ref.shape[1] // cores
    held = half // 2
    near, far = 2 * half // 3, half // 3
    for core in range(cores):
        for side in range(2):
            start = core * half + side * (near // 2)
            weight_ref[:, start : start + near // 2] = total[side, :, core * held : core * held + near // 2]
            start = core * half + near + side * (far // 2)
            weight_ref[:, start : start + far // 2] = total[side, :, core * held + near // 2 : (core + 1) * held]
    score_ref[...] = jnp.sum(total, axis=0)[:, cores * held : cores * held + score_ref.shape[1]]


def call(kernel, outs, args, scalars=0, flops=0, moved=None, whole=(), held=(), out_whole=(), out_far=(), out_near=(), scratch=(), limit=24):
    vmem = pl.BlockSpec(memory_space=pltpu.VMEM)
    smem = pl.BlockSpec(memory_space=pltpu.SMEM)
    anywhere = pl.BlockSpec(memory_space=pltpu.HBM)
    specs = [smem if i < scalars else anywhere if i in whole else vmem for i in range(len(args))]
    if moved is None:
        moved = sum(a.size * a.dtype.itemsize for a in args) + sum(math.prod(s) * jnp.dtype(t).itemsize for s, t in outs)
    args = [pltpu.with_memory_space_constraint(a, pltpu.HBM) if i in whole + held else a for i, a in enumerate(args)]
    return pl.pallas_call(
        kernel,
        out_shape=[
            pltpu.HBM(s, t) if i in out_whole + out_far else pltpu.VMEM(s, t) if i in out_near else jax.ShapeDtypeStruct(s, t)
            for i, (s, t) in enumerate(outs)
        ],
        in_specs=specs,
        out_specs=[anywhere if i in out_whole else vmem for i in range(len(outs))],
        scratch_shapes=scratch,
        compiler_params=pltpu.CompilerParams(vmem_limit_bytes=limit * 2**20),
        cost_estimate=pl.CostEstimate(flops=flops, bytes_accessed=moved, transcendentals=0),
    )(*args)


def neighbours(sizes, far):
    pairs = []
    for place in itertools.product(*map(range, sizes)):
        skip = int(place[-1] == far)
        there = [((i + skip ^ 1) - skip) % n for i, n in zip(place[:-1], sizes)] + [place[-1]]
        flat = [0, 0]
        for i, j, n in zip(place, there, sizes):
            flat = [flat[0] * n + i, flat[1] * n + j]
        pairs.append(tuple(flat))
    return pairs


def shards(sizes, events, event_user, event_day, score_weight, value_weight, qkv_weight, cotangent):
    groups, x_size, z_size, cores = sizes
    buckets = x_size * z_size * cores
    user_dev, days, width = cotangent.shape
    heads = score_weight.shape[1]
    day_dev = days // buckets
    users = user_dev * buckets
    slots = users * day_dev
    count = events.shape[0]
    rows = width // buckets
    half = 3 * width // 2
    loss_scale = 1.0 / math.sqrt(user_dev * buckets * groups * days)
    user_row = event_user.reshape(1, count)
    day_row = event_day.reshape(1, count)
    core = lax.axis_index("core").reshape(1)

    block = ((buckets, day_dev * width // 128, 128), BF16)
    summary, weight = call(
        functools.partial(pool_kernel, users, slots),
        [block, ((heads, count), F32)],
        (user_row, day_row, score_weight.T, events, value_weight),
        flops=2 * count * width * (width + slots),
        held=(0, 1, 2, 3, 4),
    )
    by_user = lax.all_to_all(summary, DAY, split_axis=0, concat_axis=0, tiled=True)
    centred, qkv_held = call(
        functools.partial(centre_kernel, users, slots),
        [((count, width), BF16), (qkv_weight.shape, BF16)],
        (user_row, day_row, events, value_weight, summary, qkv_weight),
        flops=2 * count * width * (width + slots),
        whole=(5,),
        held=(2, 3),
        out_far=(0,),
        out_near=(1,),
        scratch=[pltpu.SemaphoreType.DMA],
    )
    grad_summary, mine, send = call(
        functools.partial(attention_kernel, heads, loss_scale),
        [block, ((days, width + half), BF16), ((days, width + half), BF16)],
        (core, by_user, cotangent.reshape(days, width), qkv_held),
        scalars=1,
        whole=(2,),
        flops=2 * days * width * (6 * width + 14 * days),
        out_near=(1, 2),
        scratch=[pltpu.VMEM((days, width), BF16), pltpu.SemaphoreType.DMA],
    )
    grad_days = lax.all_to_all(grad_summary, DAY, split_axis=0, concat_axis=0, tiled=True)
    theirs = lax.ppermute(send, "core", [(i, cores - 1 - i) for i in range(cores)])
    place = ((lax.axis_index("rep") & 1) * 2 + (lax.axis_index("x") & 1)).reshape(1)
    packs = call(
        functools.partial(outer_kernel, width),
        [((width + width // 2, 128), BF16)] * 4,
        (place, mine, theirs),
        scalars=1,
        moved=0,
    )
    got = [
        lax.ppermute(packs[step], axes, neighbours(sizes_of, far))
        for step, axes, sizes_of, far in (
            (3, ("rep", "x", "core"), (groups, x_size, cores), 0),
            (2, ("rep", "core"), (groups, cores), 1),
            (1, ("x", "core"), (x_size, cores), 1),
        )
    ]
    (score,) = call(
        functools.partial(score_kernel, users, slots),
        [((width, 128), F32)],
        (user_row, day_row, events, centred, weight, grad_days),
        held=(2, 3),
        flops=2 * count * width * (slots + 256),
    )
    (partial_sums,) = call(join_kernel, [((buckets, rows, 256), BF16)], (score, packs[0], *got))
    gathered = lax.all_to_all(partial_sums, DAY, split_axis=0, concat_axis=0, tiled=True)
    (merged,) = call(
        functools.partial(merge_kernel, cores, z_size), [((groups, rows, half + 128), BF16)], (gathered,)
    )
    everyone = lax.all_to_all(merged, "rep", split_axis=0, concat_axis=0, tiled=True)
    return tuple(
        call(functools.partial(final_kernel, cores), [((rows, 3 * width), F32), ((rows, heads), F32)], (everyone,))
    )


def solution(mesh):
    sizes = (8, 4, 8, 2)
    split = Mesh(mesh.devices.reshape(sizes), ("rep",) + DAY)
    whole = ("rep",) + DAY
    in_specs = (P(whole, None), P(whole), P(whole), P(), P(), P(), P(whole, None, None))
    out_specs = (P(DAY, None), P(DAY, None))
    return jax.shard_map(
        functools.partial(shards, sizes), mesh=split, in_specs=in_specs, out_specs=out_specs, check_vma=False
    )
```
